32 devices in a mesh: dp: 2 (over x), tile: 16 (over z, y, core).
Axes of the slice: x: 2, y: 2, z: 4, core: 2. Of those that a mesh axis runs over, the one named last changes fastest.
Arguments:
- features: bfloat16 [8, 2, 2048, 1024], P('dp', None, 'tile'), may hold values from -6 to 6
- proj_weight: bfloat16 [2, 1024, 256], replicated, may hold values from -0.1875 to 0.1875
- conv_weight: bfloat16 [2, 3, 3, 256, 256], replicated, may hold values from -0.125 to 0.125
- saved: bfloat16 [8, 2, 128, 16, 256], P('dp', None, 'tile'), may hold values from -6 to 6
- cotangent: bfloat16 [8, 256, 32, 256], P('dp', 'tile'), may hold values from -6 to 6
Outputs:
- feature_grad: bfloat16 [8, 2, 2048, 1024], P('dp', None, 'tile')
- head_grad: float32 [6656, 256], P(('dp', 'tile'))
The draws below stay inside these ranges and needn't reach their ends.
All inputs are finite; a program needn't handle non-finite values.
Results may differ from the reference program's by a relative error of at most 0.0057.
Values may be sent and summed in bfloat16 or wider, within the bound.
No kernel may reach another device: no remote copies, remote signals or barrier semaphores. Data moves between devices by JAX's collectives and lax.ppermute only.
A program may use at most 128 MiB of HBM per device.

```python
import math
import jax
import jax.numpy as jnp
from jax import lax

D = 1024
C = 256
DEPTHS = 2
TILE_H = 8
TILE_W = 16
TILE_COLS = 8
IMAGES = 8
GRID_H = 16
GRID_W = 128
TOKENS = 2048
N_TILE = 16


def levels(own_key, shape, split, least, high):
    level, own = 1.0, jax.random.fold_in(own_key, 6)
    for axis_at, shards_of in split:
        draws = jnp.exp(jax.random.uniform(jax.random.fold_in(own, axis_at), (shards_of,), jnp.float32, least / len(split), high / len(split)))
        level = level * jnp.repeat(draws, shape[axis_at] // shards_of).reshape([-1 if axis == axis_at else 1 for axis in range(len(shape))])
    return level


def normal_values(key, extent, scale, bound, cuts=(), dtype=jnp.bfloat16):
    loudness = levels(key, extent, cuts, -0.22, 0.18) if cuts else 1.0
    array = jax.random.normal(key, extent, jnp.float32) * scale * loudness
    return jnp.minimum(jnp.maximum(array, -bound), bound).astype(dtype)


def setup_inputs(seed: int = 0) -> dict:
    arg_keys = jax.random.split(jax.random.key(seed), 6)
    features = normal_values(arg_keys[0], (IMAGES, DEPTHS, TOKENS, D), 1.0, 6.0, ((0, 2), (2, 16)))
    proj_weight = normal_values(arg_keys[1], (DEPTHS, D, C), D ** -0.5, 0.1875)
    conv_weight = normal_values(arg_keys[2], (DEPTHS, 3, 3, C, C), (9 * C) ** -0.5, 0.125)
    saved = normal_values(arg_keys[3], (IMAGES, DEPTHS, N_TILE * TILE_H, TILE_W, C), 1.0, 6.0, ((0, 2), (2, 16)))
    cotangent = normal_values(arg_keys[4], (IMAGES, N_TILE * 2 * TILE_H, 2 * TILE_W, C), 1.0, 6.0, ((0, 2), (1, 16)))
    return dict(features=features, proj_weight=proj_weight, conv_weight=conv_weight, saved=saved, cotangent=cotangent)


def untile(field_in, cell_rows, cell_cols):
    leading = field_in.shape[0]
    channels = field_in.shape[-1]
    blocks = field_in.reshape(leading, N_TILE // TILE_COLS, TILE_COLS, cell_rows, cell_cols, channels)
    order = [column ^ column >> 1 for column in range(TILE_COLS)]
    blocks = blocks[:, :, order]
    blocks = blocks.transpose(0, 1, 3, 2, 4, 5)
    return blocks.reshape(leading, N_TILE // TILE_COLS * cell_rows, TILE_COLS * cell_cols, channels)

def pool(values_in, along_dim, lo_edge, hi_edge):
    cell_count = (values_in.shape[along_dim] - 2) // 2
    even_part = lax.slice_in_dim(values_in, 1, 2 * cell_count + 1, 2, along_dim)
    odd_part = lax.slice_in_dim(values_in, 2, 2 * cell_count + 2, 2, along_dim)
    before = lax.slice_in_dim(values_in, 0, 2 * cell_count, 2, along_dim)
    after = lax.slice_in_dim(values_in, 3, 2 * cell_count + 2, 2, along_dim)
    target_shape = [1] * values_in.ndim
    target_shape[along_dim] = cell_count
    iota_pos = lax.broadcasted_iota(jnp.int32, tuple(target_shape), along_dim)
    at_first = jnp.logical_and(iota_pos == 0, lo_edge)
    at_last = jnp.logical_and(iota_pos == cell_count - 1, hi_edge)
    result = 0.75 * (even_part + odd_part) + 0.25 * (before + after)
    result = result + 0.25 * jnp.where(at_first, even_part, jnp.zeros_like(even_part))
    result = result + 0.25 * jnp.where(at_last, odd_part, jnp.zeros_like(odd_part))
    return result

def reference(features, proj_weight, conv_weight, saved, cotangent):
    grid_grad = untile(cotangent.astype(jnp.float32), 2 * TILE_H, 2 * TILE_W)
    padded = jnp.pad(grid_grad, ((0, 0), (1, 1), (1, 1), (0, 0)))
    row_pooled = pool(padded, 1, True, True)
    pooled = pool(row_pooled, 2, True, True).astype(jnp.bfloat16)
    dpad = jnp.pad(pooled, ((0, 0), (1, 1), (1, 1), (0, 0)))
    activ = untile(saved.reshape(IMAGES * DEPTHS, N_TILE * TILE_H, TILE_W, C), TILE_H, TILE_W)
    activ = activ.reshape(IMAGES, DEPTHS, GRID_H, GRID_W, C)
    grads_out = []
    proj_rows = []
    conv_rows = []
    for depth_index in range(DEPTHS):
        summed = jnp.zeros((IMAGES * GRID_H * GRID_W, C), jnp.float32)
        flat_act = activ[:, depth_index].reshape(-1, C)
        for kernel_row in range(3):
            for kernel_col in range(3):
                shifted = dpad[:, 2 - kernel_row:2 - kernel_row + GRID_H, 2 - kernel_col:2 - kernel_col + GRID_W]
                shifted = shifted.reshape(-1, C)
                summed = summed + jnp.dot(shifted, conv_weight[depth_index, kernel_row, kernel_col].T, preferred_element_type=jnp.float32)
                conv_rows.append(jnp.dot(flat_act.T, shifted, preferred_element_type=jnp.float32))
        token_grad = summed.astype(jnp.bfloat16)
        feat_grad = jnp.dot(token_grad, proj_weight[depth_index].T, preferred_element_type=jnp.float32)
        grads_out.append(feat_grad.astype(jnp.bfloat16).reshape(IMAGES, TOKENS, D))
        proj_rows.append(jnp.dot(features[:, depth_index].reshape(-1, D).T, token_grad, preferred_element_type=jnp.float32))
    feature_grad = jnp.stack(grads_out, axis=1)
    head_grad = jnp.concatenate(proj_rows + conv_rows, axis=0) * (1.0 / math.sqrt(IMAGES * TOKENS))
    return (feature_grad, head_grad)
```

```python
import functools
import math

import jax
import jax.numpy as jnp
from jax import lax
from jax.experimental import pallas as pl
from jax.experimental.pallas import tpu as pltpu
from jax.sharding import PartitionSpec as P

TILE_COLS = 8
HALO = 4
LEFT = 8
BF16 = jnp.bfloat16
F32 = jnp.float32


def gray_of(column):
    return column ^ column >> 1


def paired(count, first):
    pairs = []
    for low in range(first, count - 1, 2):
        pairs += [(low, low + 1), (low + 1, low)]
    return pairs


def tile_route(row_pairs, col_pairs, rows):
    row_moves = row_pairs if row_pairs is not None else [(r, r) for r in range(rows)]
    col_moves = col_pairs if col_pairs is not None else [(c, c) for c in range(TILE_COLS)]
    return [
        (r0 * TILE_COLS + gray_of(c0), r1 * TILE_COLS + gray_of(c1))
        for r0, r1 in row_moves
        for c0, c1 in col_moves
    ]


def pool_conv_kernel(
    has_second, flags, cot, row_a, row_b, col_a, col_b, aa, ab, ba, bb, weight, saved, ig, early, late,
    rows_ref, cells_ref, patch_ref, acc_ref,
):
    images, height2, width2, channels = cot.shape
    height, width = height2 // 2, width2 // 2
    depths = weight.shape[0]
    row_odd, col_odd = flags[0] == 1, flags[1] == 1
    top, bottom, left, right = flags[2] == 1, flags[3] == 1, flags[4] == 1, flags[5] == 1
    zero = jnp.zeros((), F32)

    def mix(odd, when_odd, when_even):
        if when_even is None:
            return jnp.where(odd, when_odd, zero)
        if when_odd is None:
            return jnp.where(odd, zero, when_even)
        return jnp.where(odd, when_odd, when_even)

    def load(ref, *at):
        return ref[at].astype(F32)

    def pool_rows(line, up, down):
        first, last = line(0), line(height2 - 1)
        above = jnp.where(top, first, up[1])
        below = jnp.where(bottom, last, down[0])
        out = [jnp.where(top, zero, up[0] + 0.25 * first)]
        for j in range(height):
            before = above if j == 0 else line(2 * j - 1)
            after = below if j == height - 1 else line(2 * j + 2)
            out.append(0.75 * (line(2 * j) + line(2 * j + 1)) + 0.25 * (before + after))
        out.append(jnp.where(bottom, zero, down[1] + 0.25 * last))
        return out

    def per_image(i, carry):
        def ends(first_ref, second_ref):
            up = [mix(row_odd, load(first_ref, i, n), load(second_ref, i, n) if has_second else None) for n in range(2)]
            down = [mix(row_odd, load(second_ref, i, n) if has_second else None, load(first_ref, i, n)) for n in range(2)]
            return up, down

        def corner(first_ref, second_ref, n, is_left):
            one, two = load(first_ref, i, n), load(second_ref, i, n)
            return jnp.where(col_odd, one, two) if is_left else jnp.where(col_odd, two, one)

        def put(d, at, value):
            for h in range(channels // 128):
                rows_ref[h, d, at : at + value.shape[0], :] = value[:, h * 128 : (h + 1) * 128]

        up, down = ends(row_a, row_b)
        centre = pool_rows(lambda r: load(cot, i, r), up, down)
        for d, value in enumerate(centre):
            put(d, LEFT, value)
        for is_left in (True, False):
            def line(r):
                one, two = load(col_a, i, r), load(col_b, i, r)
                return jnp.where(col_odd, one, two) if is_left else jnp.where(col_odd, two, one)

            firsts = [corner(aa, ab, n, is_left) for n in range(2)]
            seconds = [corner(ba, bb, n, is_left) for n in range(2)] if has_second else [None, None]
            side_up = [mix(row_odd, firsts[n], seconds[n]) for n in range(2)]
            side_down = [mix(row_odd, seconds[n], firsts[n]) for n in range(2)]
            for d, value in enumerate(pool_rows(line, side_up, side_down)):
                if is_left:
                    value = jnp.where(left, jnp.broadcast_to(centre[d][0:1], value.shape), value)
                    put(d, LEFT - HALO, value)
                else:
                    value = jnp.where(right, jnp.broadcast_to(centre[d][width2 - 1 : width2], value.shape), value)
                    put(d, LEFT + width2, value)
        cells = width + 8
        column = lax.broadcasted_iota(jnp.int32, (cells, channels), 0)
        outside = jnp.logical_or(
            jnp.logical_and(column == 0, left), jnp.logical_and(column == width + 1, right)
        )
        for d in range(height + 2):
            taps = [
                jnp.concatenate(
                    [rows_ref[h, d, pl.ds(LEFT - 3 + n, cells, stride=2), :] for h in range(channels // 128)],
                    axis=1,
                )
                for n in range(4)
            ]
            pooled = 0.75 * (taps[1] + taps[2]) + 0.25 * (taps[0] + taps[3])
            cells_ref[d] = jnp.where(outside, 0.0, pooled)
        for d in range(height + 2):
            for v in range(3):
                block = cells_ref[d, pl.ds(2 - v, width), :].astype(BF16)
                for u in range(3):
                    h = d - 2 + u
                    if 0 <= h < height:
                        at = pl.multiple_of((i * height + h) * width, width)
                        patch_ref[pl.ds(at, width), pl.ds((u * 3 + v) * channels, channels)] = block
        return carry

    rows_ref[...] = jnp.zeros_like(rows_ref)
    lax.fori_loop(0, images, per_image, 0)
    for k in range(depths):
        for n in range(9):
            part = lax.dot_general(
                patch_ref[:, pl.ds(n * channels, channels)],
                weight[k, n // 3, n % 3],
                (((1,), (1,)), ((), ())),
                preferred_element_type=F32,
            )
            if n == 0:
                acc_ref[...] = part
            else:
                acc_ref[...] += part
        for i in range(images):
            for h in range(height):
                at = (i * height + h) * width
                ig[h, i, k] = acc_ref[at : at + width, :].astype(BF16)
    split = late.shape[0]
    for k in range(depths):
        flat = saved[:, k].reshape(images * height * width, channels)
        flat_t = flat.T
        for n in range(9):
            part = jnp.dot(
                flat_t, patch_ref[:, pl.ds(n * channels, channels)], preferred_element_type=F32
            ).astype(BF16)
            at = (k * 9 + n) * channels
            if at < split:
                late[at : at + channels, :] = part
            else:
                early[at - split : at - split + channels, :] = part


def proj_term_kernel(came, feats, conv_late, out, tokens):
    groups, images, depths, width, channels = came.shape
    for k in range(depths):
        for i in range(images):
            for c in range(groups):
                at = (i * groups + c) * width
                tokens[k, at : at + width, :] = came[gray_of(c), i, k]
    dim = feats.shape[3]
    for k in range(depths):
        flat = feats[:, k].reshape(images * feats.shape[2], dim)
        part = lax.dot_general(
            flat, tokens[k], (((0,), (0,)), ((), ())), preferred_element_type=F32
        )
        out[k * dim : (k + 1) * dim, :] = part.astype(BF16)
    out[depths * dim :, :] = conv_late[...]


def feat_grad_kernel(tokens, weight, out):
    images, depths, count, dim = out.shape
    for k in range(depths):
        part = lax.dot_general(
            tokens[k], weight[k], (((1,), (1,)), ((), ())), preferred_element_type=F32
        )
        out[:, k] = part.astype(BF16).reshape(images, count, dim)


def vmem_call(kernel, out_shape, operands, scratch=(), scalars=0, flops=0, limit=48):
    whole = pl.BlockSpec(memory_space=pltpu.VMEM)
    moved = sum(a.size * a.dtype.itemsize for a in operands)
    moved += sum(math.prod(s.shape) * s.dtype.itemsize for s in jax.tree.leaves(out_shape))
    return pl.pallas_call(
        kernel,
        out_shape=out_shape,
        in_specs=[pl.BlockSpec(memory_space=pltpu.SMEM)] * scalars + [whole] * (len(operands) - scalars),
        out_specs=jax.tree.map(lambda _: whole, out_shape),
        scratch_shapes=list(scratch),
        compiler_params=pltpu.CompilerParams(vmem_limit_bytes=limit << 20),
        cost_estimate=pl.CostEstimate(flops=flops, bytes_accessed=moved, transcendentals=0),
    )(*operands)


def halved(block, index, bit):
    count = lax.axis_size("tile")
    rows, channels = block.shape[1:]
    pairs = block.reshape(block.shape[0] // 2, 2, rows, channels)
    mine = index >> bit & 1
    sent = lax.dynamic_index_in_dim(pairs, 1 - mine, 1, keepdims=False)
    kept = lax.dynamic_index_in_dim(pairs, mine, 1, keepdims=False)
    came = lax.ppermute(sent, "tile", [(t, t ^ 1 << bit) for t in range(count)])
    return kept.astype(F32) + came.astype(F32)


def scatter_sum(terms, index):
    count = lax.axis_size("tile")
    block = terms.reshape(count, terms.shape[0] // count, terms.shape[1])
    bits = count.bit_length() - 1
    for bit in range(bits):
        total = halved(block, index, bit)
        block = total.astype(BF16)
    return total[0]


def per_device(features, proj_weight, conv_weight, saved, cotangent):
    position = lax.axis_index("tile")
    tile_count = lax.axis_size("tile")
    rows = tile_count // TILE_COLS
    gray = position % TILE_COLS
    col = gray ^ gray >> 1 ^ gray >> 2
    row = position // TILE_COLS
    images, height2, width2, channels = cotangent.shape
    depths, dim = proj_weight.shape[:2]
    height, width = height2 // 2, width2 // 2
    patches = images * height * width
    row_odd, col_odd = row % 2 == 1, col % 2 == 1

    cot = cotangent
    wide = cot.astype(F32)
    to_below = jnp.stack(
        [0.25 * wide[:, -3] + 0.75 * (wide[:, -2] + wide[:, -1]), wide[:, -1]], axis=1
    ).astype(BF16)
    to_above = jnp.stack(
        [wide[:, 0], 0.75 * (wide[:, 0] + wide[:, 1]) + 0.25 * wide[:, 2]], axis=1
    ).astype(BF16)
    has_second = rows > 2

    def swap(block, row_pairs, col_pairs):
        return lax.ppermute(block, "tile", tile_route(row_pairs, col_pairs, rows))

    row_first, row_second = paired(rows, 0), paired(rows, 1)
    col_first, col_second = paired(TILE_COLS, 0), paired(TILE_COLS, 1)
    row_out = jnp.where(row_odd, to_above, to_below)
    row_a = swap(row_out, row_first, None)

    def edge(block, odd):
        return jnp.where(odd, block[:, :, :HALO], block[:, :, width2 - HALO :])

    col_b = swap(edge(cot, jnp.logical_not(col_odd)), None, col_second)
    col_a = swap(edge(cot, col_odd), None, col_first)
    ab = swap(edge(row_out, jnp.logical_not(col_odd)), row_first, col_second)
    aa = swap(edge(row_out, col_odd), row_first, col_first)
    if has_second:
        row_out = jnp.where(row_odd, to_below, to_above)
        row_b = swap(row_out, row_second, None)
        bb = swap(edge(row_out, jnp.logical_not(col_odd)), row_second, col_second)
        ba = swap(edge(row_out, col_odd), row_second, col_first)
    else:
        row_b, ba, bb = row_a, aa, ab
    flags = jnp.stack(
        [row % 2, col % 2, row == 0, row == rows - 1, col == 0, col == TILE_COLS - 1]
    ).astype(jnp.int32)
    head_rows = depths * (dim + 9 * channels)
    conv_late = head_rows // 2 - depths * dim
    conv_early = head_rows // 2
    sds = jax.ShapeDtypeStruct
    conv_flops = 2 * patches * depths * 9 * channels * channels
    ig, early, late = vmem_call(
        functools.partial(pool_conv_kernel, has_second),
        (
            sds((height, images, depths, width, channels), BF16),
            sds((conv_early, channels), BF16),
            sds((conv_late, channels), BF16),
        ),
        (flags, cot, row_a, row_b, col_a, col_b, aa, ab, ba, bb, conv_weight, saved),
        scratch=(
            pltpu.VMEM((channels // 128, height + 2, LEFT + width2 + 16, 128), F32),
            pltpu.VMEM((height + 2, width + 8, channels), F32),
            pltpu.VMEM((patches, 9 * channels), BF16),
            pltpu.VMEM((patches, channels), F32),
        ),
        scalars=1,
        flops=2 * conv_flops,
    )
    groups = [[g * TILE_COLS + t for t in range(TILE_COLS)] for g in range(rows)]
    came = lax.all_to_all(ig, "tile", 0, 0, axis_index_groups=groups, tiled=True)
    early_sum = scatter_sum(early, position)
    tokens = features.shape[2]
    proj_flops = 2 * images * tokens * depths * dim * channels
    terms, token_grad = vmem_call(
        proj_term_kernel,
        (sds((head_rows // 2, channels), BF16), sds((depths, images * tokens, channels), BF16)),
        (came, features, late),
        flops=proj_flops,
    )
    feature_grad = vmem_call(
        feat_grad_kernel,
        sds((images, depths, tokens, dim), BF16),
        (token_grad, proj_weight),
        flops=proj_flops,
    )
    late_sum = scatter_sum(terms, position)
    first = lax.axis_index("dp") == 0
    sent = jnp.where(first, early_sum, late_sum).astype(BF16)
    kept = jnp.where(first, late_sum, early_sum)
    other = lax.ppermute(sent, "dp", [(0, 1), (1, 0)])
    scale = 1.0 / math.sqrt(images * lax.axis_size("dp") * tokens * tile_count)
    head_grad = (kept + other.astype(F32)) * scale
    return feature_grad, head_grad


def solution(mesh):
    in_specs = (
        P("dp", None, "tile", None),
        P(),
        P(),
        P("dp", None, "tile", None, None),
        P("dp", "tile", None, None),
    )
    out_specs = (P("dp", None, "tile", None), P(("dp", "tile"), None))
    return jax.shard_map(
        per_device, mesh=mesh, in_specs=in_specs, out_specs=out_specs, check_vma=False
    )
```

```python
import functools
import math

import jax
import jax.numpy as jnp
from jax import lax
from jax.experimental import pallas as pl
from jax.experimental.pallas import tpu as pltpu
from jax.sharding import PartitionSpec as P

TILE_COLS = 8
HALO = 4
LEFT = 8
BF16 = jnp.bfloat16
F32 = jnp.float32


def gray_of(column):
    return column ^ column >> 1


def paired(count, first):
    pairs = []
    for low in range(first, count - 1, 2):
        pairs += [(low, low + 1), (low + 1, low)]
    return pairs


def tile_route(row_pairs, col_pairs, rows):
    row_moves = row_pairs if row_pairs is not None else [(r, r) for r in range(rows)]
    col_moves = col_pairs if col_pairs is not None else [(c, c) for c in range(TILE_COLS)]
    return [
        (r0 * TILE_COLS + gray_of(c0), r1 * TILE_COLS + gray_of(c1))
        for r0, r1 in row_moves
        for c0, c1 in col_moves
    ]


def pool_conv_kernel(
    has_second, flags, cot, row_a, row_b, col_a, col_b, aa, ab, ba, bb, weight, saved,
    *outs_and_scratch,
):
    igs, (split_refs, late) = outs_and_scratch[:TILE_COLS], (outs_and_scratch[TILE_COLS:-6], outs_and_scratch[-6])
    rows_ref, cells_ref, patch_ref, acc_ref, full_ref = outs_and_scratch[-5:]
    images, height2, width2, channels = cot.shape
    height, width = height2 // 2, width2 // 2
    depths = weight.shape[0]
    row_odd, col_odd = flags[0] == 1, flags[1] == 1
    top, bottom, left, right = flags[2] == 1, flags[3] == 1, flags[4] == 1, flags[5] == 1
    zero = jnp.zeros((), F32)

    def mix(odd, when_odd, when_even):
        if when_even is None:
            return jnp.where(odd, when_odd, zero)
        if when_odd is None:
            return jnp.where(odd, zero, when_even)
        return jnp.where(odd, when_odd, when_even)

    def load(ref, *at):
        return ref[at].astype(F32)

    def pool_rows(line, up, down):
        first, last = line(0), line(height2 - 1)
        above = jnp.where(top, first, up[1])
        below = jnp.where(bottom, last, down[0])
        out = [jnp.where(top, zero, up[0] + 0.25 * first)]
        for j in range(height):
            before = above if j == 0 else line(2 * j - 1)
            after = below if j == height - 1 else line(2 * j + 2)
            out.append(0.75 * (line(2 * j) + line(2 * j + 1)) + 0.25 * (before + after))
        out.append(jnp.where(bottom, zero, down[1] + 0.25 * last))
        return out

    def per_image(i, carry):
        def ends(first_ref, second_ref):
            up = [mix(row_odd, load(first_ref, i, n), load(second_ref, i, n) if has_second else None) for n in range(2)]
            down = [mix(row_odd, load(second_ref, i, n) if has_second else None, load(first_ref, i, n)) for n in range(2)]
            return up, down

        def corner(first_ref, second_ref, n, is_left):
            one, two = load(first_ref, i, n), load(second_ref, i, n)
            return jnp.where(col_odd, one, two) if is_left else jnp.where(col_odd, two, one)

        def put(d, at, value):
            for h in range(channels // 128):
                rows_ref[h, d, at : at + value.shape[0], :] = value[:, h * 128 : (h + 1) * 128]

        up, down = ends(row_a, row_b)
        centre = pool_rows(lambda r: load(cot, i, r), up, down)
        for d, value in enumerate(centre):
            put(d, LEFT, value)
        for is_left in (True, False):
            def line(r):
                one, two = load(col_a, i, r), load(col_b, i, r)
                return jnp.where(col_odd, one, two) if is_left else jnp.where(col_odd, two, one)

            firsts = [corner(aa, ab, n, is_left) for n in range(2)]
            seconds = [corner(ba, bb, n, is_left) for n in range(2)] if has_second else [None, None]
            side_up = [mix(row_odd, firsts[n], seconds[n]) for n in range(2)]
            side_down = [mix(row_odd, seconds[n], firsts[n]) for n in range(2)]
            for d, value in enumerate(pool_rows(line, side_up, side_down)):
                if is_left:
                    value = jnp.where(left, jnp.broadcast_to(centre[d][0:1], value.shape), value)
                    put(d, LEFT - HALO, value)
                else:
                    value = jnp.where(right, jnp.broadcast_to(centre[d][width2 - 1 : width2], value.shape), value)
                    put(d, LEFT + width2, value)
        cells = width + 8
        column = lax.broadcasted_iota(jnp.int32, (cells, channels), 0)
        outside = jnp.logical_or(
            jnp.logical_and(column == 0, left), jnp.logical_and(column == width + 1, right)
        )
        for d in range(height + 2):
            taps = [
                jnp.concatenate(
                    [rows_ref[h, d, pl.ds(LEFT - 3 + n, cells, stride=2), :] for h in range(channels // 128)],
                    axis=1,
                )
                for n in range(4)
            ]
            pooled = 0.75 * (taps[1] + taps[2]) + 0.25 * (taps[0] + taps[3])
            cells_ref[d] = jnp.where(outside, 0.0, pooled)
        for d in range(height + 2):
            for v in range(3):
                block = cells_ref[d, pl.ds(2 - v, width), :].astype(BF16)
                for u in range(3):
                    h = d - 2 + u
                    if 0 <= h < height:
                        at = pl.multiple_of((i * height + h) * width, width)
                        patch_ref[pl.ds(at, width), pl.ds((u * 3 + v) * channels, channels)] = block
        return carry

    rows_ref[...] = jnp.zeros_like(rows_ref)
    lax.fori_loop(0, images, per_image, 0)
    gray = flags[6]
    for k in range(depths):
        for n in range(9):
            part = lax.dot_general(
                patch_ref[:, pl.ds(n * channels, channels)],
                weight[k, n // 3, n % 3],
                (((1,), (1,)), ((), ())),
                preferred_element_type=F32,
            )
            if n == 0:
                acc_ref[...] = part
            else:
                acc_ref[...] += part
        for i in range(images):
            for apart in range(height):
                at = pl.multiple_of((i * height + (gray ^ apart)) * width, width)
                igs[apart][i, k] = acc_ref[pl.ds(at, width), :].astype(BF16)
    split = late.shape[0]
    for k in range(depths):
        flat = saved[:, k].reshape(images * height * width, channels)
        flat_t = flat.T
        for n in range(9):
            part = jnp.dot(
                flat_t, patch_ref[:, pl.ds(n * channels, channels)], preferred_element_type=F32
            ).astype(BF16)
            at = (k * 9 + n) * channels
            if at < split:
                late[at : at + channels, :] = part
            else:
                full_ref[at - split : at - split + channels, :] = part
    deal(full_ref, split_refs, flags[7])


def deal(full_ref, split_refs, mine):
    if len(split_refs) == 1:
        split_refs[0][...] = full_ref[...]
        return
    kept, sent = split_refs
    count, rows = kept.shape[:2]
    for j in range(count):
        kept[j] = full_ref[pl.ds(pl.multiple_of((2 * j + mine) * rows, 16), rows), :]
        sent[j] = full_ref[pl.ds(pl.multiple_of((2 * j + 1 - mine) * rows, 16), rows), :]


def pack_kernel(has_second, flags, cot, *outs):
    width2 = cot.shape[2]
    row_odd, col_odd = flags[0] == 1, flags[1] == 1

    def line(r):
        return cot[:, r].astype(F32)

    end = cot.shape[1] - 1
    below = [0.25 * line(end - 2) + 0.75 * (line(end - 1) + line(end)), line(end)]
    above = [line(0), 0.75 * (line(0) + line(1)) + 0.25 * line(2)]
    for second in range(2 if has_second else 1):
        flip = second == 1
        for n in range(2):
            value = jnp.where(row_odd, below[n], above[n]) if flip else jnp.where(row_odd, above[n], below[n])
            low, high = value[:, :HALO], value[:, width2 - HALO :]
            outs[3 * second][:, n] = value.astype(BF16)
            outs[3 * second + 1][:, n] = jnp.where(col_odd, low, high).astype(BF16)
            outs[3 * second + 2][:, n] = jnp.where(col_odd, high, low).astype(BF16)
    low, high = cot[:, :, :HALO].astype(F32), cot[:, :, width2 - HALO :].astype(F32)
    outs[-2][...] = jnp.where(col_odd, low, high).astype(BF16)
    outs[-1][...] = jnp.where(col_odd, high, low).astype(BF16)


def proj_term_kernel(flags, *refs):
    came, (feats, conv_late) = refs[:TILE_COLS], refs[TILE_COLS : TILE_COLS + 2]
    split_refs, tokens, full_ref = refs[TILE_COLS + 2 : -2], refs[-2], refs[-1]
    images, depths, width, channels = came[0].shape
    gray = flags[6]
    for apart in range(TILE_COLS):
        sender = gray ^ apart
        column = sender ^ sender >> 1 ^ sender >> 2
        for k in range(depths):
            for i in range(images):
                at = pl.multiple_of((i * TILE_COLS + column) * width, width)
                tokens[k, pl.ds(at, width), :] = came[apart][i, k]
    dim = feats.shape[3]
    for k in range(depths):
        flat = feats[:, k].reshape(images * feats.shape[2], dim)
        part = lax.dot_general(
            flat, tokens[k], (((0,), (0,)), ((), ())), preferred_element_type=F32
        )
        full_ref[k * dim : (k + 1) * dim, :] = part.astype(BF16)
    full_ref[depths * dim :, :] = conv_late[...]
    deal(full_ref, split_refs, flags[7])


def feat_grad_kernel(tokens, weight, out):
    images, depths, count, dim = out.shape
    for k in range(depths):
        part = lax.dot_general(
            tokens[k], weight[k], (((1,), (1,)), ((), ())), preferred_element_type=F32
        )
        out[:, k] = part.astype(BF16).reshape(images, count, dim)


def round_kernel(parts, bits_at, bits, by_columns, flags, *refs):
    ins, outs = refs[:parts], refs[parts:]
    span = 1 << bits
    mine, dp = 0, flags[8]
    for b in range(bits):
        mine = mine + flags[9 + bits_at + b] * (1 << b)
    count = outs[0].shape[0]
    width = outs[0].shape[2]
    for n, out in enumerate(outs):
        across, apart = n // span, n % span
        for q in range(count):
            block = q * span + (mine ^ apart)
            if by_columns:
                columns = pl.ds(pl.multiple_of((dp ^ across) * width, width), width)
            else:
                columns = slice(None)
            total = ins[0][block, :, columns].astype(F32)
            for other in ins[1:]:
                total = total + other[block, :, columns].astype(F32)
            out[q] = total.astype(out.dtype)


def last_kernel(parts, flags, *refs):
    early, late, (sent, kept) = refs[:parts], refs[parts : 2 * parts], refs[2 * parts :]
    first = flags[8] == 0
    sums = []
    for group in (early, late):
        total = group[0][0].astype(F32)
        for other in group[1:]:
            total = total + other[0].astype(F32)
        sums.append(total)
    sent[...] = jnp.where(first, sums[0], sums[1]).astype(BF16)
    kept[...] = jnp.where(first, sums[1], sums[0])


def join_kernel(scale, flags, kept, came, out):
    width = kept.shape[1]
    at = pl.multiple_of(flags[8] * width, width)
    out[:, pl.ds(at, width)] = kept[...] * scale
    at = pl.multiple_of((1 - flags[8]) * width, width)
    out[:, pl.ds(at, width)] = came[...].astype(F32) * scale


def vmem_call(kernel, out_shape, operands, scratch=(), scalars=1, flops=0, limit=16):
    whole = pl.BlockSpec(memory_space=pltpu.VMEM)
    moved = sum(a.size * a.dtype.itemsize for a in operands)
    moved += sum(math.prod(s.shape) * s.dtype.itemsize for s in jax.tree.leaves(out_shape))
    return pl.pallas_call(
        kernel,
        out_shape=out_shape,
        in_specs=[pl.BlockSpec(memory_space=pltpu.SMEM)] * scalars + [whole] * (len(operands) - scalars),
        out_specs=jax.tree.map(lambda _: whole, out_shape),
        scratch_shapes=list(scratch),
        compiler_params=pltpu.CompilerParams(vmem_limit_bytes=limit << 20),
        cost_estimate=pl.CostEstimate(flops=flops, bytes_accessed=moved, transcendentals=0),
    )(*operands)


def sds(*shape, dtype=BF16):
    return jax.ShapeDtypeStruct(shape, dtype)


def xor_move(block, apart, across):
    tiles = lax.axis_size("tile")
    if not across:
        return lax.ppermute(block, "tile", [(t, t ^ apart) for t in range(tiles)])
    if not apart:
        return lax.ppermute(block, "dp", [(0, 1), (1, 0)])
    route = [(d * tiles + t, (1 - d) * tiles + (t ^ apart)) for d in range(2) for t in range(tiles)]
    return lax.ppermute(block, ("dp", "tile"), route)


def scatter_sum(dealt, flags, core):
    tiles = lax.axis_size("tile")
    if len(dealt) == 1:
        pairs = dealt[0].reshape(tiles // 2, 2, dealt[0].shape[0] // tiles, dealt[0].shape[1])
        kept = lax.dynamic_index_in_dim(pairs, core, 1, keepdims=False)
        sent = lax.dynamic_index_in_dim(pairs, 1 - core, 1, keepdims=False)
    else:
        kept, sent = dealt
    parts = [kept, xor_move(sent, 1, False)]
    total_bits = tiles.bit_length() - 1
    at = 1
    while at < total_bits:
        by_columns = at == 1
        bits = 1 if by_columns else min(2, total_bits - at)
        span = 1 << bits
        count, rows, channels = parts[0].shape
        if by_columns:
            channels //= 2
        outs = [
            sds(count // span, rows, channels, dtype=F32 if n == 0 else BF16)
            for n in range(span * (2 if by_columns else 1))
        ]
        pieces = vmem_call(
            functools.partial(round_kernel, len(parts), at, bits, by_columns), outs, [flags] + parts
        )
        parts = [pieces[0]] + [
            xor_move(pieces[n], (n % span) << at, n >= span) for n in range(1, len(pieces))
        ]
        at += bits
    return parts


def per_device(features, proj_weight, conv_weight, saved, cotangent):
    position = lax.axis_index("tile")
    tile_count = lax.axis_size("tile")
    rows = tile_count // TILE_COLS
    gray = position % TILE_COLS
    col = gray ^ gray >> 1 ^ gray >> 2
    row = position // TILE_COLS
    images, height2, width2, channels = cotangent.shape
    depths, dim = proj_weight.shape[:2]
    height, width = height2 // 2, width2 // 2
    patches = images * height * width
    has_second = rows > 2
    bits = tile_count.bit_length() - 1
    flags = jnp.stack(
        [row % 2, col % 2, row == 0, row == rows - 1, col == 0, col == TILE_COLS - 1, gray, position % 2]
        + [lax.axis_index("dp")]
        + [position >> b & 1 for b in range(bits)]
    ).astype(jnp.int32)

    def swap(block, row_pairs, col_pairs):
        return lax.ppermute(block, "tile", tile_route(row_pairs, col_pairs, rows))

    row_first, row_second = paired(rows, 0), paired(rows, 1)
    col_first, col_second = paired(TILE_COLS, 0), paired(TILE_COLS, 1)
    strip = [sds(images, 2, width2, channels)] + [sds(images, 2, HALO, channels)] * 2
    edges = vmem_call(
        functools.partial(pack_kernel, has_second),
        strip * (2 if has_second else 1) + [sds(images, height2, HALO, channels)] * 2,
        (flags, cotangent),
    )
    row_a = swap(edges[0], row_first, None)
    col_b = swap(edges[-1], None, col_second)
    col_a = swap(edges[-2], None, col_first)
    ab = swap(edges[2], row_first, col_second)
    aa = swap(edges[1], row_first, col_first)
    if has_second:
        row_b = swap(edges[3], row_second, None)
        bb = swap(edges[5], row_second, col_second)
        ba = swap(edges[4], row_second, col_first)
    else:
        row_b, ba, bb = row_a, aa, ab
    half_rows = depths * (dim + 9 * channels) // 2
    conv_late = half_rows - depths * dim
    block_rows = half_rows // tile_count
    if block_rows % 16:
        dealt = [sds(half_rows, channels)]
    else:
        dealt = [sds(tile_count // 2, block_rows, channels)] * 2
    conv_flops = 2 * patches * depths * 9 * channels * channels
    outs = vmem_call(
        functools.partial(pool_conv_kernel, has_second),
        [sds(images, depths, width, channels)] * height + dealt + [sds(conv_late, channels)],
        (flags, cotangent, row_a, row_b, col_a, col_b, aa, ab, ba, bb, conv_weight, saved),
        scratch=(
            pltpu.VMEM((channels // 128, height + 2, LEFT + width2 + 16, 128), F32),
            pltpu.VMEM((height + 2, width + 8, channels), F32),
            pltpu.VMEM((patches, 9 * channels), BF16),
            pltpu.VMEM((patches, channels), F32),
            pltpu.VMEM((half_rows, channels), BF16),
        ),
        flops=2 * conv_flops,
    )
    igs, early, late = outs[:height], outs[height:-1], outs[-1]
    came = [igs[0]] + [xor_move(igs[apart], apart, False) for apart in range(1, height)]
    early_parts = scatter_sum(early, flags, position % 2)
    tokens = features.shape[2]
    proj_flops = 2 * images * tokens * depths * dim * channels
    *terms, token_grad = vmem_call(
        proj_term_kernel,
        dealt + [sds(depths, images * tokens, channels)],
        [flags] + came + [features, late],
        scratch=(pltpu.VMEM((half_rows, channels), BF16),),
        flops=proj_flops,
    )
    feature_grad = vmem_call(
        feat_grad_kernel,
        sds(images, depths, tokens, dim),
        (token_grad, proj_weight),
        scalars=0,
        flops=proj_flops,
    )
    late_parts = scatter_sum(terms, flags, position % 2)
    half = sds(block_rows, channels // 2)
    sent, kept = vmem_call(
        functools.partial(last_kernel, len(early_parts)),
        [half, sds(block_rows, channels // 2, dtype=F32)],
        [flags] + early_parts + late_parts,
    )
    other = xor_move(sent, 0, True)
    scale = 1.0 / math.sqrt(images * lax.axis_size("dp") * tokens * tile_count)
    head_grad = vmem_call(
        functools.partial(join_kernel, scale), sds(block_rows, channels, dtype=F32), (flags, kept, other)
    )
    return feature_grad, head_grad


def solution(mesh):
    in_specs = (
        P("dp", None, "tile", None),
        P(),
        P(),
        P("dp", None, "tile", None, None),
        P("dp", "tile", None, None),
    )
    out_specs = (P("dp", None, "tile", None), P(("dp", "tile"), None))
    return jax.shard_map(
        per_device, mesh=mesh, in_specs=in_specs, out_specs=out_specs, check_vma=False
    )
```

```python
import functools
import math

import jax
import jax.numpy as jnp
from jax import lax
from jax.experimental import pallas as pl
from jax.experimental.pallas import tpu as pltpu
from jax.sharding import PartitionSpec as P

TILE_COLS = 8
HALO = 4
LEFT = 8
BF16 = jnp.bfloat16
F32 = jnp.float32


def gray_of(column):
    return column ^ column >> 1


def paired(count, first):
    pairs = []
    for low in range(first, count - 1, 2):
        pairs += [(low, low + 1), (low + 1, low)]
    return pairs


def tile_route(row_pairs, col_pairs, rows):
    row_moves = row_pairs if row_pairs is not None else [(r, r) for r in range(rows)]
    col_moves = col_pairs if col_pairs is not None else [(c, c) for c in range(TILE_COLS)]
    return [
        (r0 * TILE_COLS + gray_of(c0), r1 * TILE_COLS + gray_of(c1))
        for r0, r1 in row_moves
        for c0, c1 in col_moves
    ]


def pool_conv_kernel(
    has_second, flags, cot, row_a, row_b, col_a, col_b, aa, ab, ba, bb, weight,
    *outs_and_scratch,
):
    igs, patch_ref = outs_and_scratch[:TILE_COLS], outs_and_scratch[TILE_COLS]
    rows_ref, cells_ref, acc_ref, weight_ref, sems = outs_and_scratch[TILE_COLS + 1 :]
    images, height2, width2, channels = cot.shape
    height, width = height2 // 2, width2 // 2
    depths = weight.shape[0]
    copies = [pltpu.make_async_copy(weight.at[k], weight_ref.at[k], sems.at[k]) for k in range(depths)]
    for copy in copies:
        copy.start()
    row_odd, col_odd = flags[0] == 1, flags[1] == 1
    top, bottom, left, right = flags[2] == 1, flags[3] == 1, flags[4] == 1, flags[5] == 1
    zero = jnp.zeros((), F32)

    def mix(odd, when_odd, when_even):
        if when_even is None:
            return jnp.where(odd, when_odd, zero)
        if when_odd is None:
            return jnp.where(odd, zero, when_even)
        return jnp.where(odd, when_odd, when_even)

    def load(ref, *at):
        return ref[at].astype(F32)

    def pool_rows(line, up, down):
        first, last = line(0), line(height2 - 1)
        above = jnp.where(top, first, up[1])
        below = jnp.where(bottom, last, down[0])
        out = [jnp.where(top, zero, up[0] + 0.25 * first)]
        for j in range(height):
            before = above if j == 0 else line(2 * j - 1)
            after = below if j == height - 1 else line(2 * j + 2)
            out.append(0.75 * (line(2 * j) + line(2 * j + 1)) + 0.25 * (before + after))
        out.append(jnp.where(bottom, zero, down[1] + 0.25 * last))
        return out

    def per_image(i, carry):
        def ends(first_ref, second_ref):
            up = [mix(row_odd, load(first_ref, i, n), load(second_ref, i, n) if has_second else None) for n in range(2)]
            down = [mix(row_odd, load(second_ref, i, n) if has_second else None, load(first_ref, i, n)) for n in range(2)]
            return up, down

        def corner(first_ref, second_ref, n, is_left):
            one, two = load(first_ref, i, n), load(second_ref, i, n)
            return jnp.where(col_odd, one, two) if is_left else jnp.where(col_odd, two, one)

        def put(d, at, value):
            for h in range(channels // 128):
                rows_ref[h, d, at : at + value.shape[0], :] = value[:, h * 128 : (h + 1) * 128]

        up, down = ends(row_a, row_b)
        centre = pool_rows(lambda r: load(cot, i, r), up, down)
        for d, value in enumerate(centre):
            put(d, LEFT, value)
        for is_left in (True, False):
            def line(r):
                one, two = load(col_a, i, r), load(col_b, i, r)
                return jnp.where(col_odd, one, two) if is_left else jnp.where(col_odd, two, one)

            firsts = [corner(aa, ab, n, is_left) for n in range(2)]
            seconds = [corner(ba, bb, n, is_left) for n in range(2)] if has_second else [None, None]
            side_up = [mix(row_odd, firsts[n], seconds[n]) for n in range(2)]
            side_down = [mix(row_odd, seconds[n], firsts[n]) for n in range(2)]
            for d, value in enumerate(pool_rows(line, side_up, side_down)):
                if is_left:
                    value = jnp.where(left, jnp.broadcast_to(centre[d][0:1], value.shape), value)
                    put(d, LEFT - HALO, value)
                else:
                    value = jnp.where(right, jnp.broadcast_to(centre[d][width2 - 1 : width2], value.shape), value)
                    put(d, LEFT + width2, value)
        cells = width + 8
        column = lax.broadcasted_iota(jnp.int32, (cells, channels), 0)
        outside = jnp.logical_or(
            jnp.logical_and(column == 0, left), jnp.logical_and(column == width + 1, right)
        )
        for d in range(height + 2):
            taps = [
                jnp.concatenate(
                    [rows_ref[h, d, pl.ds(LEFT - 3 + n, cells, stride=2), :] for h in range(channels // 128)],
                    axis=1,
                )
                for n in range(4)
            ]
            pooled = 0.75 * (taps[1] + taps[2]) + 0.25 * (taps[0] + taps[3])
            cells_ref[d] = jnp.where(outside, 0.0, pooled)
        for d in range(height + 2):
            for v in range(3):
                block = cells_ref[d, pl.ds(2 - v, width), :].astype(BF16)
                for u in range(3):
                    h = d - 2 + u
                    if 0 <= h < height:
                        at = pl.multiple_of((i * height + h) * width, width)
                        patch_ref[pl.ds(at, width), pl.ds((u * 3 + v) * channels, channels)] = block
        return carry

    rows_ref[...] = jnp.zeros_like(rows_ref)
    lax.fori_loop(0, images, per_image, 0)
    gray = flags[6]
    for k in range(depths):
        copies[k].wait()
        for n in range(9):
            part = lax.dot_general(
                patch_ref[:, pl.ds(n * channels, channels)],
                weight_ref[k, n // 3, n % 3],
                (((1,), (1,)), ((), ())),
                preferred_element_type=F32,
            )
            if n == 0:
                acc_ref[...] = part
            else:
                acc_ref[...] += part
        for i in range(images):
            for apart in range(height):
                at = pl.multiple_of((i * height + (gray ^ apart)) * width, width)
                igs[apart][i, k] = acc_ref[pl.ds(at, width), :].astype(BF16)


def conv_term_kernel(flags, patches, saved_t, *refs):
    split_refs, late, full_ref = refs[:-2], refs[-2], refs[-1]
    depths, channels = saved_t.shape[:2]
    split = late.shape[0]
    for k in range(depths):
        for n in range(9):
            part = jnp.dot(
                saved_t[k], patches[:, pl.ds(n * channels, channels)], preferred_element_type=F32
            ).astype(BF16)
            at = (k * 9 + n) * channels
            if at < split:
                late[at : at + channels, :] = part
            else:
                full_ref[at - split : at - split + channels, :] = part
    deal(full_ref, split_refs, flags[7])


def turn_kernel(value, out):
    depths, channels, count = out.shape
    for k in range(depths):
        out[k] = value[:, k].reshape(count, channels).T


def deal(full_ref, split_refs, mine):
    if len(split_refs) == 1:
        split_refs[0][...] = full_ref[...]
        return
    kept, sent = split_refs
    count, rows = kept.shape[:2]
    for j in range(count):
        kept[j] = full_ref[pl.ds(pl.multiple_of((2 * j + mine) * rows, 16), rows), :]
        sent[j] = full_ref[pl.ds(pl.multiple_of((2 * j + 1 - mine) * rows, 16), rows), :]


def pack_kernel(has_second, flags, cot, *outs):
    width2 = cot.shape[2]
    row_odd, col_odd = flags[0] == 1, flags[1] == 1

    def line(r):
        return cot[:, r].astype(F32)

    end = cot.shape[1] - 1
    below = [0.25 * line(end - 2) + 0.75 * (line(end - 1) + line(end)), line(end)]
    above = [line(0), 0.75 * (line(0) + line(1)) + 0.25 * line(2)]
    for second in range(2 if has_second else 1):
        flip = second == 1
        for n in range(2):
            value = jnp.where(row_odd, below[n], above[n]) if flip else jnp.where(row_odd, above[n], below[n])
            outs[second][:, n] = value.astype(BF16)
    low, high = cot[:, :, :HALO].astype(F32), cot[:, :, width2 - HALO :].astype(F32)
    outs[-2][...] = jnp.where(col_odd, low, high).astype(BF16)
    outs[-1][...] = jnp.where(col_odd, high, low).astype(BF16)


def corner_kernel(flags, *refs):
    col_odd = flags[1] == 1
    for n in range(len(refs) // 3):
        rows, first, second = refs[n], refs[len(refs) // 3 + 2 * n], refs[len(refs) // 3 + 2 * n + 1]
        low = rows[:, :, :HALO].astype(F32)
        high = rows[:, :, rows.shape[2] - HALO :].astype(F32)
        first[...] = jnp.where(col_odd, low, high).astype(BF16)
        second[...] = jnp.where(col_odd, high, low).astype(BF16)


def proj_term_kernel(flags, *refs):
    came, (feats_t, conv_late) = refs[:TILE_COLS], refs[TILE_COLS : TILE_COLS + 2]
    split_refs, tokens, full_ref = refs[TILE_COLS + 2 : -2], refs[-2], refs[-1]
    images, depths, width, channels = came[0].shape
    gray = flags[6]
    for apart in range(TILE_COLS):
        sender = gray ^ apart
        column = sender ^ sender >> 1 ^ sender >> 2
        for k in range(depths):
            for i in range(images):
                at = pl.multiple_of((i * TILE_COLS + column) * width, width)
                tokens[k, pl.ds(at, width), :] = came[apart][i, k]
    dim = feats_t.shape[1]
    for k in range(depths):
        part = jnp.dot(feats_t[k], tokens[k], preferred_element_type=F32)
        full_ref[k * dim : (k + 1) * dim, :] = part.astype(BF16)
    full_ref[depths * dim :, :] = conv_late[...]
    deal(full_ref, split_refs, flags[7])


def feat_grad_kernel(tokens, weight, out):
    images, depths, count, dim = out.shape
    for k in range(depths):
        part = lax.dot_general(
            tokens[k], weight[k], (((1,), (1,)), ((), ())), preferred_element_type=F32
        )
        out[:, k] = part.astype(BF16).reshape(images, count, dim)


def round_kernel(parts, bits_at, bits, by_columns, flags, *refs):
    ins, outs = refs[:parts], refs[parts:]
    span = 1 << bits
    mine, dp = 0, flags[8]
    for b in range(bits):
        mine = mine + flags[9 + bits_at + b] * (1 << b)
    count = outs[0].shape[0]
    width = outs[0].shape[2]
    for n, out in enumerate(outs):
        across, apart = n // span, n % span
        for q in range(count):
            block = q * span + (mine ^ apart)
            if by_columns:
                columns = pl.ds(pl.multiple_of((dp ^ across) * width, width), width)
            else:
                columns = slice(None)
            total = ins[0][block, :, columns].astype(F32)
            for other in ins[1:]:
                total = total + other[block, :, columns].astype(F32)
            out[q] = total.astype(out.dtype)


def last_kernel(early_parts, late_parts, flags, *refs):
    early, late, (sent, kept) = refs[:early_parts], refs[early_parts:-2], refs[-2:]
    first = flags[8] == 0
    sums = []
    for group in (early, late):
        total = group[0][0].astype(F32)
        for other in group[1:]:
            total = total + other[0].astype(F32)
        sums.append(total)
    sent[...] = jnp.where(first, sums[0], sums[1]).astype(BF16)
    kept[...] = jnp.where(first, sums[1], sums[0])


def join_kernel(scale, flags, kept, came, out):
    width = kept.shape[1]
    at = pl.multiple_of(flags[8] * width, width)
    out[:, pl.ds(at, width)] = kept[...] * scale
    at = pl.multiple_of((1 - flags[8]) * width, width)
    out[:, pl.ds(at, width)] = came[...].astype(F32) * scale


def vmem_call(kernel, out_shape, operands, scratch=(), scalars=1, flops=0, limit=16, hbm=(), after=()):
    whole = pl.BlockSpec(memory_space=pltpu.VMEM)
    specs = [pl.BlockSpec(memory_space=pltpu.SMEM)] * scalars + [whole] * (len(operands) - scalars)
    for n in hbm:
        specs[n] = pl.BlockSpec(memory_space=pltpu.HBM)
    specs += [pl.BlockSpec(memory_space=pl.ANY)] * len(after)
    count = len(operands)

    def run(*refs):
        kernel(*refs[:count], *refs[count + len(after) :])

    moved = sum(a.size * a.dtype.itemsize for a in operands)
    moved += sum(math.prod(s.shape) * s.dtype.itemsize for s in jax.tree.leaves(out_shape))
    return pl.pallas_call(
        run,
        out_shape=out_shape,
        in_specs=specs,
        out_specs=jax.tree.map(lambda _: whole, out_shape),
        scratch_shapes=list(scratch),
        compiler_params=pltpu.CompilerParams(vmem_limit_bytes=limit << 20),
        cost_estimate=pl.CostEstimate(flops=flops, bytes_accessed=moved, transcendentals=0),
    )(*operands, *after)


def sds(*shape, dtype=BF16):
    return jax.ShapeDtypeStruct(shape, dtype)


def xor_move(block, apart, across):
    tiles = lax.axis_size("tile")
    if not across:
        return lax.ppermute(block, "tile", [(t, t ^ apart) for t in range(tiles)])
    if not apart:
        return lax.ppermute(block, "dp", [(0, 1), (1, 0)])
    route = [(d * tiles + t, (1 - d) * tiles + (t ^ apart)) for d in range(2) for t in range(tiles)]
    return lax.ppermute(block, ("dp", "tile"), route)


def core_sum(dealt, core):
    if len(dealt) == 1:
        tiles = lax.axis_size("tile")
        pairs = dealt[0].reshape(tiles // 2, 2, dealt[0].shape[0] // tiles, dealt[0].shape[1])
        kept = lax.dynamic_index_in_dim(pairs, core, 1, keepdims=False)
        sent = lax.dynamic_index_in_dim(pairs, 1 - core, 1, keepdims=False)
    else:
        kept, sent = dealt
    return [kept, xor_move(sent, 1, False)]


def deal_round(parts, flags, at, bits, by_columns):
    span = 1 << bits
    count, rows, channels = parts[0].shape
    if by_columns:
        channels //= 2
    outs = [
        sds(count // span, rows, channels, dtype=F32 if n == 0 else BF16)
        for n in range(span * (2 if by_columns else 1))
    ]
    return vmem_call(
        functools.partial(round_kernel, len(parts), at, bits, by_columns), outs, [flags] + parts
    )


def send_round(pieces, at, bits):
    span = 1 << bits
    return [pieces[0]] + [
        xor_move(pieces[n], (n % span) << at, n >= span) for n in range(1, len(pieces))
    ]


def per_device(features, proj_weight, conv_weight, saved, cotangent):
    position = lax.axis_index("tile")
    tile_count = lax.axis_size("tile")
    rows = tile_count // TILE_COLS
    gray = position % TILE_COLS
    col = gray ^ gray >> 1 ^ gray >> 2
    row = position // TILE_COLS
    images, height2, width2, channels = cotangent.shape
    depths, dim = proj_weight.shape[:2]
    height, width = height2 // 2, width2 // 2
    patches = images * height * width
    has_second = rows > 2
    bits = tile_count.bit_length() - 1
    flags = jnp.stack(
        [row % 2, col % 2, row == 0, row == rows - 1, col == 0, col == TILE_COLS - 1, gray, position % 2]
        + [lax.axis_index("dp")]
        + [position >> b & 1 for b in range(bits)]
    ).astype(jnp.int32)

    def swap(block, row_pairs, col_pairs):
        return lax.ppermute(block, "tile", tile_route(row_pairs, col_pairs, rows))

    row_first, row_second = paired(rows, 0), paired(rows, 1)
    col_first, col_second = paired(TILE_COLS, 0), paired(TILE_COLS, 1)
    sides = 2 if has_second else 1
    edges = vmem_call(
        functools.partial(pack_kernel, has_second),
        [sds(images, 2, width2, channels)] * sides + [sds(images, height2, HALO, channels)] * 2,
        (flags, cotangent),
    )
    row_a = swap(edges[0], row_first, None)
    col_b = swap(edges[-1], None, col_second)
    col_a = swap(edges[-2], None, col_first)
    row_b = swap(edges[1], row_second, None) if has_second else row_a
    came_rows = [row_a, row_b][:sides]
    corners = vmem_call(corner_kernel, [sds(images, 2, HALO, channels)] * (2 * sides), [flags] + came_rows)
    aa, ab = swap(corners[0], None, col_first), swap(corners[1], None, col_second)
    if has_second:
        ba, bb = swap(corners[2], None, col_first), swap(corners[3], None, col_second)
    else:
        ba, bb = aa, ab
    tokens = features.shape[2]
    saved_t = vmem_call(turn_kernel, sds(depths, channels, patches), (saved,), scalars=0)
    feats_t = vmem_call(turn_kernel, sds(depths, dim, images * tokens), (features,), scalars=0)
    half_rows = depths * (dim + 9 * channels) // 2
    conv_late = half_rows - depths * dim
    block_rows = half_rows // tile_count
    if block_rows % 16:
        dealt = [sds(half_rows, channels)]
    else:
        dealt = [sds(tile_count // 2, block_rows, channels)] * 2
    conv_flops = 2 * patches * depths * 9 * channels * channels
    outs = vmem_call(
        functools.partial(pool_conv_kernel, has_second),
        [sds(images, depths, width, channels)] * height + [sds(patches, 9 * channels)],
        (flags, cotangent, row_a, row_b, col_a, col_b, aa, ab, ba, bb, conv_weight),
        scratch=(
            pltpu.VMEM((channels // 128, height + 2, LEFT + width2 + 16, 128), F32),
            pltpu.VMEM((height + 2, width + 8, channels), F32),
            pltpu.VMEM((patches, channels), F32),
            pltpu.VMEM(conv_weight.shape, BF16),
            pltpu.SemaphoreType.DMA((depths,)),
        ),
        flops=conv_flops,
        hbm=(10,),
    )
    igs, windows = outs[:height], outs[height]
    came = [igs[0]] + [xor_move(igs[apart], apart, False) for apart in range(1, height)]
    *early, conv_top = vmem_call(
        conv_term_kernel,
        dealt + [sds(conv_late, channels)],
        (flags, windows, saved_t),
        scratch=(pltpu.VMEM((half_rows, channels), BF16),),
        flops=conv_flops,
    )
    early_parts = core_sum(early, position % 2)
    early_pieces = deal_round(early_parts, flags, 1, 0, True)
    proj_flops = 2 * images * tokens * depths * dim * channels
    *terms, token_grad = vmem_call(
        proj_term_kernel,
        dealt + [sds(depths, images * tokens, channels)],
        [flags] + came + [feats_t, conv_top],
        scratch=(pltpu.VMEM((half_rows, channels), BF16),),
        flops=proj_flops,
        after=(early_pieces[0],),
    )
    early_parts = send_round(early_pieces, 1, 0)
    for bit in range(1, bits):
        early_parts = send_round(deal_round(early_parts, flags, bit, 1, False), bit, 1)
    feature_grad = vmem_call(
        feat_grad_kernel,
        sds(images, depths, tokens, dim),
        (token_grad, proj_weight),
        scalars=0,
        flops=proj_flops,
    )
    late_parts = core_sum(terms, position % 2)
    at = 1
    while at < bits:
        step = 1 if at == 1 else min(2, bits - at)
        late_parts = send_round(deal_round(late_parts, flags, at, step, at == 1), at, step)
        at += step
    half = sds(block_rows, channels // 2)
    sent, kept = vmem_call(
        functools.partial(last_kernel, len(early_parts), len(late_parts)),
        [half, sds(block_rows, channels // 2, dtype=F32)],
        [flags] + early_parts + late_parts,
    )
    other = xor_move(sent, 0, True)
    scale = 1.0 / math.sqrt(images * lax.axis_size("dp") * tokens * tile_count)
    head_grad = vmem_call(
        functools.partial(join_kernel, scale), sds(block_rows, channels, dtype=F32), (flags, kept, other)
    )
    return feature_grad, head_grad


def solution(mesh):
    in_specs = (
        P("dp", None, "tile", None),
        P(),
        P(),
        P("dp", None, "tile", None, None),
        P("dp", "tile", None, None),
    )
    out_specs = (P("dp", None, "tile", None), P(("dp", "tile"), None))
    return jax.shard_map(
        per_device, mesh=mesh, in_specs=in_specs, out_specs=out_specs, check_vma=False
    )
```

```python
import functools
import math

import jax
import jax.numpy as jnp
from jax import lax
from jax.experimental import pallas as pl
from jax.experimental.pallas import tpu as pltpu
from jax.sharding import PartitionSpec as P

TILE_COLS = 8
HALO = 4
LEFT = 8
BF16 = jnp.bfloat16
F32 = jnp.float32
ROW_ODD, COL_ODD, TOP, BOTTOM, LEFT_END, RIGHT_END, CORE, DP, BITS = range(9)


def gray_of(column):
    return column ^ column >> 1


def column_of(code):
    return code ^ code >> 1 ^ code >> 2


def paired(count, first):
    pairs = []
    for low in range(first, count - 1, 2):
        pairs += [(low, low + 1), (low + 1, low)]
    return pairs


def tile_route(row_pairs, col_pairs, rows):
    row_moves = row_pairs if row_pairs is not None else [(r, r) for r in range(rows)]
    col_moves = col_pairs if col_pairs is not None else [(c, c) for c in range(TILE_COLS)]
    return [
        (r0 * TILE_COLS + gray_of(c0), r1 * TILE_COLS + gray_of(c1))
        for r0, r1 in row_moves
        for c0, c1 in col_moves
    ]


def nt_dot(left, right):
    return lax.dot_general(left, right, (((1,), (1,)), ((), ())), preferred_element_type=F32)


def column_pack_kernel(flags, cot, held, first, second, sems):
    col_odd = flags[COL_ODD] == 1
    images, _, width2, _ = cot.shape
    copies = [pltpu.make_async_copy(cot.at[i], held.at[i], sems.at[i]) for i in range(images)]
    for copy in copies:
        copy.start()
    for i in range(images):
        copies[i].wait()
        low, high = held[i, :, :HALO].astype(F32), held[i, :, width2 - HALO :].astype(F32)
        first[i] = jnp.where(col_odd, low, high).astype(BF16)
        second[i] = jnp.where(col_odd, high, low).astype(BF16)


def pool_columns(flags, held, col_a, col_b, wide, i, lines):
    width2, channels = held.shape[2:]
    width = width2 // 2
    col_odd, left, right = flags[COL_ODD] == 1, flags[LEFT_END] == 1, flags[RIGHT_END] == 1
    side = lax.broadcasted_iota(jnp.int32, (2, channels), 0)
    outside = jnp.logical_or(jnp.logical_and(side == 0, left), jnp.logical_and(side == 1, right))
    cells, beside = [], []
    for at, r in enumerate(lines):
        centre = held[i, r].astype(F32)
        one, two = col_a[i, r].astype(F32), col_b[i, r].astype(F32)
        before = jnp.where(left, jnp.broadcast_to(centre[:1], one.shape), jnp.where(col_odd, one, two))
        after = jnp.where(
            right, jnp.broadcast_to(centre[width2 - 1 :], one.shape), jnp.where(col_odd, two, one)
        )
        for h in range(channels // 128):
            lanes = slice(h * 128, (h + 1) * 128)
            wide[h, at, LEFT - HALO : LEFT, :] = before[:, lanes]
            wide[h, at, LEFT : LEFT + width2, :] = centre[:, lanes]
            wide[h, at, LEFT + width2 : LEFT + width2 + HALO, :] = after[:, lanes]
    for at in range(len(lines)):
        def taps(start, size, stride):
            got = [
                jnp.concatenate(
                    [wide[h, at, pl.ds(start + n, size, stride=stride), :] for h in range(channels // 128)], axis=1
                )
                for n in range(4)
            ]
            return 0.75 * (got[1] + got[2]) + 0.25 * (got[0] + got[3])

        cells.append(taps(LEFT - 1, width, 2))
        beside.append(jnp.where(outside, 0.0, taps(LEFT - 3, 2, 2 * width + 2)))
    return cells, beside


def place(cells, beside, pooled, window, at):
    width = cells.shape[0]
    pooled[LEFT : LEFT + width, :] = cells
    pooled[LEFT - 1 : LEFT, :] = beside[:1]
    pooled[LEFT + width : LEFT + width + 1, :] = beside[1:]
    for v in range(3):
        window[v, pl.ds(at, width), :] = pooled[pl.ds(LEFT + 1 - v, width), :].astype(BF16)


def row_pack_kernel(has_second, flags, held, col_a, col_b, *refs):
    outs, (cells_out, beside_out, wide, ends) = refs[: 2 if has_second else 1], refs[-4:]
    images, height2, width2, channels = held.shape
    width = width2 // 2
    row_odd = flags[ROW_ODD] == 1
    lines = [0, 1, 2, height2 - 3, height2 - 2, height2 - 1]
    for i in range(images):
        cells, beside = pool_columns(flags, held, col_a, col_b, wide, i, lines)
        for n in range(6):
            cells_out[i, n] = cells[n]
            beside_out[i, n] = beside[n]
        for group, is_end in ((cells, False), (beside, True)):
            above = [group[0], 0.75 * (group[0] + group[1]) + 0.25 * group[2]]
            below = [0.25 * group[3] + 0.75 * (group[4] + group[5]), group[5]]
            for second in range(len(outs)):
                for n in range(2):
                    odd, even = (below[n], above[n]) if second else (above[n], below[n])
                    value = jnp.where(row_odd, odd, even)
                    if is_end:
                        ends[second, (2 * i + n) * 2 : (2 * i + n) * 2 + 2, :] = value
                    else:
                        at = (2 * i + n) * width
                        outs[second][at : at + width, :] = value.astype(BF16)
    for second in range(len(outs)):
        outs[second][2 * images * width :, :] = ends[second].astype(BF16)


def main_kernel(
    flags, held, col_a, col_b, weight, saved, feats,
    window, acc, weight_out, saved_t, feats_t,
    wide, pooled, saved_in, feats_in, saved_flat, sems,
):
    images, height2, width2, channels = held.shape
    height, width = height2 // 2, width2 // 2
    depths = weight.shape[0]
    copies = [pltpu.make_async_copy(weight.at[k], weight_out.at[k], sems.at[k]) for k in range(depths)]
    copies.append(pltpu.make_async_copy(saved, saved_in, sems.at[depths]))
    copies.append(pltpu.make_async_copy(feats, feats_in, sems.at[depths + 1]))
    for copy in copies:
        copy.start()
    pooled[...] = jnp.zeros_like(pooled)

    def per_image(i, carry):
        cells, beside = pool_columns(flags, held, col_a, col_b, wide, i, range(1, height2 - 1))
        for p in range(1, height - 1):
            at = 2 * p - 2
            both = [
                0.75 * (group[at + 1] + group[at + 2]) + 0.25 * (group[at] + group[at + 3])
                for group in (cells, beside)
            ]
            where = pl.multiple_of((p - 1) * images * width + i * width, width)
            place(both[0], both[1], pooled.at[p], window, where)
        return carry

    lax.fori_loop(0, images, per_image, 0)
    line = images * width
    inner = (height - 2) * line
    for k in range(depths):
        copies[k].wait()
        for u in range(3):
            part = nt_dot(window[0], weight_out[k, u, 0])
            part = part + nt_dot(window[1], weight_out[k, u, 1])
            part = part + nt_dot(window[2], weight_out[k, u, 2])
            if u == 0:
                acc[k, :inner, :] = part
                acc[k, inner:, :] = jnp.zeros((2 * line, channels), F32)
            else:
                acc[k, u * line : u * line + inner, :] += part
    copies[depths].wait()
    for k in range(depths):
        for h in range(height):
            for i in range(images):
                at = (h * images + i) * width
                saved_flat[at : at + width, :] = saved_in[i, k, h]
        saved_t[k] = saved_flat[...].T
    copies[depths + 1].wait()
    for k in range(depths):
        feats_t[k] = feats_in[:, k].reshape(feats_t.shape[2], feats_t.shape[1]).T


def edge_kernel(has_second, flags, *refs):
    sides = 2 if has_second else 1
    rows, (cells, beside, inner, acc, weight) = refs[:sides], refs[sides : sides + 5]
    grads, window, pooled, ends, total = refs[sides + 5 :]
    images, width = cells.shape[0], cells.shape[2]
    depths, count = acc.shape[:2]
    line = images * width
    height = count // line
    row_odd, top, bottom = flags[ROW_ODD] == 1, flags[TOP] == 1, flags[BOTTOM] == 1
    for n in range(sides):
        ends[n] = rows[n][2 * line :, :].astype(F32)
    pooled[...] = jnp.zeros_like(pooled)
    for i in range(images):
        for_rows = []
        for is_end, own in ((False, cells), (True, beside)):
            def came(from_above, n):
                def of(ref_at):
                    if is_end:
                        at = (2 * i + n) * 2
                        return ends[ref_at, at : at + 2, :]
                    at = (2 * i + n) * width
                    return rows[ref_at][at : at + width, :].astype(F32)

                first = of(0)
                second = of(1) if has_second else jnp.zeros_like(first)
                return jnp.where(row_odd, first, second) if from_above else jnp.where(row_odd, second, first)

            edge = [own[i, n] for n in range(6)]
            zero = jnp.zeros_like(edge[0])
            for_rows.append(
                [
                    jnp.where(top, zero, came(True, 0) + 0.25 * edge[0]),
                    0.75 * (edge[0] + edge[1]) + 0.25 * (jnp.where(top, edge[0], came(True, 1)) + edge[2]),
                    0.75 * (edge[4] + edge[5]) + 0.25 * (jnp.where(bottom, edge[5], came(False, 0)) + edge[3]),
                    jnp.where(bottom, zero, came(False, 1) + 0.25 * edge[5]),
                ]
            )
        for n, p in enumerate((0, 1, height, height + 1)):
            place(for_rows[0][n], for_rows[1][n], pooled.at[n], window, p * line + i * width)
    for v in range(3):
        window[v, 2 * line : height * line, :] = inner[v]
    low, high = slice(0, 2 * line), slice(height * line, (height + 2) * line)
    for k in range(depths):
        total[...] = acc[k]
        for v in range(3):
            total[(height - 2) * line :, :] += nt_dot(window[v, high, :], weight[k, 0, v])
            total[: 2 * line, :] += nt_dot(window[v, low, :], weight[k, 2, v])
            middle = jnp.concatenate(
                [window[v, line : 2 * line, :], window[v, height * line : (height + 1) * line, :]], axis=0
            )
            part = nt_dot(middle, weight[k, 1, v])
            total[:line, :] += part[:line]
            total[(height - 1) * line :, :] += part[line:]
        for h in range(height):
            grads[h, k] = total[h * line : (h + 1) * line, :].astype(BF16)


def deal(full, split_refs, core):
    if len(split_refs) == 1:
        split_refs[0][...] = full[...]
        return
    kept, sent = split_refs
    count, rows = kept.shape[:2]
    for j in range(count):
        kept[j] = full[pl.ds(pl.multiple_of((2 * j + core) * rows, 16), rows), :]
        sent[j] = full[pl.ds(pl.multiple_of((2 * j + 1 - core) * rows, 16), rows), :]


def conv_term_kernel(flags, window, saved_t, *refs):
    split_refs, top, full = refs[:-2], refs[-2], refs[-1]
    depths, channels, count = saved_t.shape
    line = (window.shape[1] - count) // 2
    split = top.shape[0]
    for k in range(depths):
        for n in range(9):
            start = (2 - n // 3) * line
            part = jnp.dot(
                saved_t[k], window[n % 3, start : start + count, :], preferred_element_type=F32
            ).astype(BF16)
            at = (k * 9 + n) * channels
            if at < split:
                top[at : at + channels, :] = part
            else:
                full[at - split : at - split + channels, :] = part
    deal(full, split_refs, flags[CORE])


def proj_term_kernel(images, flags, came, feats_t, conv_top, *refs):
    split_refs, tokens, full = refs[:-2], refs[-2], refs[-1]
    groups, depths, line, channels = came.shape
    dim = feats_t.shape[1]
    width = line // images
    per_image = groups * width
    for k in range(depths):
        for g in range(groups):
            for i in range(images):
                at = i * per_image + column_of(g) * width
                tokens[k, at : at + width, :] = came[g, k, i * width : (i + 1) * width, :]
    for k in range(depths):
        part = jnp.dot(feats_t[k], tokens[k], preferred_element_type=F32)
        full[k * dim : (k + 1) * dim, :] = part.astype(BF16)
    full[depths * dim :, :] = conv_top[...]
    deal(full, split_refs, flags[CORE])


def feat_grad_kernel(tokens, weight, out):
    images, depths, count, dim = out.shape
    for k in range(depths):
        out[:, k] = nt_dot(tokens[k], weight[k]).astype(BF16).reshape(images, count, dim)


def round_kernel(parts, bits_at, bits, by_columns, flags, *refs):
    ins, outs = refs[:parts], refs[parts:]
    span = 1 << bits
    mine, dp = 0, flags[DP]
    for b in range(bits):
        mine = mine + flags[BITS + bits_at + b] * (1 << b)
    count, _, width = outs[0].shape
    for n, out in enumerate(outs):
        across, apart = n // span, n % span
        for q in range(count):
            block = q * span + (mine ^ apart)
            if by_columns:
                columns = pl.ds(pl.multiple_of((dp ^ across) * width, width), width)
            else:
                columns = slice(None)
            total = ins[0][block, :, columns].astype(F32)
            for other in ins[1:]:
                total = total + other[block, :, columns].astype(F32)
            out[q] = total.astype(out.dtype)


def last_kernel(early_parts, flags, *refs):
    early, late, (sent, kept) = refs[:early_parts], refs[early_parts:-2], refs[-2:]
    first = flags[DP] == 0
    sums = []
    for group in (early, late):
        total = group[0][0].astype(F32)
        for other in group[1:]:
            total = total + other[0].astype(F32)
        sums.append(total)
    sent[...] = jnp.where(first, sums[0], sums[1]).astype(BF16)
    kept[...] = jnp.where(first, sums[1], sums[0])


def join_kernel(scale, flags, kept, came, out):
    width = kept.shape[1]
    at = pl.multiple_of(flags[DP] * width, width)
    out[:, pl.ds(at, width)] = kept[...] * scale
    at = pl.multiple_of((1 - flags[DP]) * width, width)
    out[:, pl.ds(at, width)] = came[...].astype(F32) * scale


def vmem_call(kernel, out_shape, operands, scratch=(), scalars=1, flops=0, limit=16, hbm=(), after=()):
    whole = pl.BlockSpec(memory_space=pltpu.VMEM)
    specs = [pl.BlockSpec(memory_space=pltpu.SMEM)] * scalars + [whole] * (len(operands) - scalars)
    for n in hbm:
        specs[n] = pl.BlockSpec(memory_space=pltpu.HBM)
    specs += [pl.BlockSpec(memory_space=pl.ANY)] * len(after)
    count = len(operands)

    def run(*refs):
        kernel(*refs[:count], *refs[count + len(after) :])

    moved = sum(a.size * a.dtype.itemsize for a in operands)
    moved += sum(math.prod(s.shape) * s.dtype.itemsize for s in jax.tree.leaves(out_shape))
    return pl.pallas_call(
        run,
        out_shape=out_shape,
        in_specs=specs,
        out_specs=jax.tree.map(lambda _: whole, out_shape),
        scratch_shapes=list(scratch),
        compiler_params=pltpu.CompilerParams(vmem_limit_bytes=limit << 20),
        cost_estimate=pl.CostEstimate(flops=flops, bytes_accessed=moved, transcendentals=0),
    )(*operands, *after)


def sds(*shape, dtype=BF16):
    return jax.ShapeDtypeStruct(shape, dtype)


def xor_move(block, apart, across):
    tiles = lax.axis_size("tile")
    if not across:
        return lax.ppermute(block, "tile", [(t, t ^ apart) for t in range(tiles)])
    if not apart:
        return lax.ppermute(block, "dp", [(0, 1), (1, 0)])
    route = [(d * tiles + t, (1 - d) * tiles + (t ^ apart)) for d in range(2) for t in range(tiles)]
    return lax.ppermute(block, ("dp", "tile"), route)


def core_sum(dealt, core):
    if len(dealt) == 1:
        tiles = lax.axis_size("tile")
        pairs = dealt[0].reshape(tiles // 2, 2, dealt[0].shape[0] // tiles, dealt[0].shape[1])
        kept = lax.dynamic_index_in_dim(pairs, core, 1, keepdims=False)
        sent = lax.dynamic_index_in_dim(pairs, 1 - core, 1, keepdims=False)
    else:
        kept, sent = dealt
    return [kept, xor_move(sent, 1, False)]


def deal_round(parts, flags, at, bits, by_columns, after=()):
    span = 1 << bits
    count, rows, channels = parts[0].shape
    if by_columns:
        channels //= 2
    outs = [
        sds(count // span, rows, channels, dtype=F32 if n == 0 else BF16)
        for n in range(span * (2 if by_columns else 1))
    ]
    return vmem_call(
        functools.partial(round_kernel, len(parts), at, bits, by_columns), outs, [flags] + parts, after=after
    )


def send_round(pieces, at, bits):
    span = 1 << bits
    return [pieces[0]] + [
        xor_move(pieces[n], (n % span) << at, n >= span) for n in range(1, len(pieces))
    ]


def per_device(features, proj_weight, conv_weight, saved, cotangent):
    position = lax.axis_index("tile")
    tile_count = lax.axis_size("tile")
    rows = tile_count // TILE_COLS
    gray = position % TILE_COLS
    col, row = column_of(gray), position // TILE_COLS
    images, height2, width2, channels = cotangent.shape
    depths, dim = proj_weight.shape[:2]
    height, width = height2 // 2, width2 // 2
    patches = images * height * width
    line = images * width
    tokens = features.shape[2]
    has_second = rows > 2
    sides = 2 if has_second else 1
    bits = tile_count.bit_length() - 1
    flags = jnp.stack(
        [row % 2, col % 2, row == 0, row == rows - 1, col == 0, col == TILE_COLS - 1]
        + [position % 2, lax.axis_index("dp")]
        + [position >> b & 1 for b in range(bits)]
    ).astype(jnp.int32)

    def swap(block, row_pairs, col_pairs):
        return lax.ppermute(block, "tile", tile_route(row_pairs, col_pairs, rows))

    held, to_first, to_second = vmem_call(
        column_pack_kernel,
        [sds(*cotangent.shape)] + [sds(images, height2, HALO, channels)] * 2,
        (flags, cotangent),
        scratch=(pltpu.SemaphoreType.DMA((images,)),),
        hbm=(1,),
    )
    col_b = swap(to_second, None, paired(TILE_COLS, 1))
    col_a = swap(to_first, None, paired(TILE_COLS, 0))
    halves = channels // 128
    *row_out, cells, beside = vmem_call(
        functools.partial(row_pack_kernel, has_second),
        [sds(2 * images * (width + 2), channels)] * sides
        + [sds(images, 6, width, channels, dtype=F32), sds(images, 6, 2, channels, dtype=F32)],
        (flags, held, col_a, col_b),
        scratch=(
            pltpu.VMEM((halves, 6, LEFT + width2 + 8, 128), F32),
            pltpu.VMEM((sides, 4 * images, channels), F32),
        ),
    )
    came_rows = [swap(row_out[n], paired(rows, n), None) for n in range(sides)]
    conv_flops = 2 * patches * depths * 9 * channels * channels
    inner, acc, weight, saved_t, feats_t = vmem_call(
        main_kernel,
        [
            sds(3, (height - 2) * line, channels),
            sds(depths, patches, channels, dtype=F32),
            sds(*conv_weight.shape),
            sds(depths, channels, patches),
            sds(depths, dim, images * tokens),
        ],
        (flags, held, col_a, col_b, conv_weight, saved, features),
        scratch=(
            pltpu.VMEM((halves, height2 - 2, LEFT + width2 + 8, 128), F32),
            pltpu.VMEM((height, LEFT + width + 8, channels), F32),
            pltpu.VMEM(saved.shape, BF16),
            pltpu.VMEM(features.shape, BF16),
            pltpu.VMEM((patches, channels), BF16),
            pltpu.SemaphoreType.DMA((depths + 2,)),
        ),
        flops=conv_flops,
        hbm=(4, 5, 6),
        after=(row_out[0],),
    )
    grads, window = vmem_call(
        functools.partial(edge_kernel, has_second),
        [sds(height, depths, line, channels), sds(3, (height + 2) * line, channels)],
        [flags] + came_rows + [cells, beside, inner, acc, weight],
        scratch=(
            pltpu.VMEM((4, LEFT + width + 8, channels), F32),
            pltpu.VMEM((sides, 4 * images, channels), F32),
            pltpu.VMEM((patches, channels), F32),
        ),
        flops=conv_flops // 4,
    )
    groups = [[g * TILE_COLS + t for t in range(TILE_COLS)] for g in range(rows)]
    came = lax.all_to_all(grads, "tile", 0, 0, axis_index_groups=groups, tiled=True)

    half_rows = depths * (dim + 9 * channels) // 2
    conv_late = half_rows - depths * dim
    block_rows = half_rows // tile_count
    if block_rows % 16:
        dealt = [sds(half_rows, channels)]
    else:
        dealt = [sds(tile_count // 2, block_rows, channels)] * 2
    full = pltpu.VMEM((half_rows, channels), BF16)
    *early, conv_top = vmem_call(
        conv_term_kernel,
        dealt + [sds(conv_late, channels)],
        (flags, window, saved_t),
        scratch=(full,),
        flops=conv_flops,
    )
    early_pieces = deal_round(core_sum(early, position % 2), flags, 1, 0, True)
    early_parts = send_round(early_pieces, 1, 0)
    proj_flops = 2 * images * tokens * depths * dim * channels
    *terms, token_grad = vmem_call(
        functools.partial(proj_term_kernel, images),
        dealt + [sds(depths, images * tokens, channels)],
        (flags, came, feats_t, conv_top),
        scratch=(full,),
        flops=proj_flops,
        after=(early_pieces[0],),
    )
    early_pieces = deal_round(early_parts, flags, 1, 1, False, after=(token_grad,))
    early_parts = send_round(early_pieces, 1, 1)
    late_pieces = deal_round(core_sum(terms, position % 2), flags, 1, 1, True, after=(early_pieces[0],))
    late_parts = send_round(late_pieces, 1, 1)
    feature_grad = vmem_call(
        feat_grad_kernel,
        sds(images, depths, tokens, dim),
        (token_grad, proj_weight),
        scalars=0,
        flops=proj_flops,
        after=(late_pieces[0],),
    )
    before = feature_grad
    for bit in range(2, bits):
        early_pieces = deal_round(early_parts, flags, bit, 1, False, after=(before,))
        early_parts = send_round(early_pieces, bit, 1)
        before = early_pieces[0]
    at = 2
    while at < bits:
        step = min(2, bits - at)
        late_pieces = deal_round(late_parts, flags, at, step, False, after=(before,))
        late_parts = send_round(late_pieces, at, step)
        before = late_pieces[0]
        at += step
    half = sds(block_rows, channels // 2)
    sent, kept = vmem_call(
        functools.partial(last_kernel, len(early_parts)),
        [half, sds(block_rows, channels // 2, dtype=F32)],
        [flags] + early_parts + late_parts,
    )
    other = xor_move(sent, 0, True)
    scale = 1.0 / math.sqrt(images * lax.axis_size("dp") * tokens * tile_count)
    head_grad = vmem_call(
        functools.partial(join_kernel, scale), sds(block_rows, channels, dtype=F32), (flags, kept, other)
    )
    return feature_grad, head_grad


def solution(mesh):
    in_specs = (
        P("dp", None, "tile", None),
        P(),
        P(),
        P("dp", None, "tile", None, None),
        P("dp", "tile", None, None),
    )
    out_specs = (P("dp", None, "tile", None), P(("dp", "tile"), None))
    return jax.shard_map(
        per_device, mesh=mesh, in_specs=in_specs, out_specs=out_specs, check_vma=False
    )
```

```python
import functools
import math

import jax
import jax.numpy as jnp
from jax import lax
from jax.experimental import pallas as pl
from jax.experimental.pallas import tpu as pltpu
from jax.sharding import PartitionSpec as P

TILE_COLS = 8
HALO = 4
LEFT = 8
BF16 = jnp.bfloat16
F32 = jnp.float32
ROW_ODD, COL_ODD, TOP, BOTTOM, LEFT_END, RIGHT_END, CORE, DP, GRAY, BITS = range(10)
CHIPS = TILE_COLS // 2


def gray_of(column):
    return column ^ column >> 1


def column_of(code):
    return code ^ code >> 1 ^ code >> 2


def paired(count, first):
    pairs = []
    for low in range(first, count - 1, 2):
        pairs += [(low, low + 1), (low + 1, low)]
    return pairs


def tile_route(row_pairs, col_pairs, rows):
    row_moves = row_pairs if row_pairs is not None else [(r, r) for r in range(rows)]
    col_moves = col_pairs if col_pairs is not None else [(c, c) for c in range(TILE_COLS)]
    return [
        (r0 * TILE_COLS + gray_of(c0), r1 * TILE_COLS + gray_of(c1))
        for r0, r1 in row_moves
        for c0, c1 in col_moves
    ]


def nt_dot(left, right):
    return lax.dot_general(left, right, (((1,), (1,)), ((), ())), preferred_element_type=F32)


def centre_kernel(cot, pooled, wide):
    images, height2, width2, channels = cot.shape
    width = width2 // 2
    wide[...] = jnp.zeros_like(wide)

    def per_image(i, carry):
        for r in range(height2):
            value = cot[i, r].astype(F32)
            for h in range(channels // 128):
                wide[h, r, LEFT : LEFT + width2, :] = value[:, h * 128 : (h + 1) * 128]
        for r in range(height2):
            for h in range(channels // 128):
                taps = [wide[h, r, pl.ds(LEFT - 1 + n, width, stride=2), :] for n in range(4)]
                pooled[i, r, :, h * 128 : (h + 1) * 128] = 0.75 * (taps[1] + taps[2]) + 0.25 * (taps[0] + taps[3])
        return carry

    lax.fori_loop(0, images, per_image, 0)


def pool_columns(flags, cot, centre, col_a, col_b, i, lines):
    width2 = cot.shape[2]
    width, channels = centre.shape[2:]
    col_odd, left, right = flags[COL_ODD] == 1, flags[LEFT_END] == 1, flags[RIGHT_END] == 1
    cell = lax.broadcasted_iota(jnp.int32, (width, channels), 0)
    is_first, is_last = cell == 0, cell == width - 1
    cells, beside = [], []
    for r in lines:
        own_first, own_last = cot[i, r, 0:1].astype(F32), cot[i, r, width2 - 1 : width2].astype(F32)
        one, two = col_a[i, r].astype(F32), col_b[i, r].astype(F32)
        before, after = jnp.where(col_odd, one, two), jnp.where(col_odd, two, one)
        near_before = jnp.where(left, own_first, before[3:4])
        near_after = jnp.where(right, own_last, after[0:1])
        cells.append(
            centre[i, r] + 0.25 * (jnp.where(is_first, near_before, 0.0) + jnp.where(is_last, near_after, 0.0))
        )
        first = 0.75 * (before[2:3] + before[3:4]) + 0.25 * (before[1:2] + own_first)
        last = 0.75 * (after[0:1] + after[1:2]) + 0.25 * (own_last + after[2:3])
        beside.append(
            jnp.concatenate([jnp.where(left, 0.0, first), jnp.where(right, 0.0, last)], axis=0)
        )
    return cells, beside


def place(cells, beside, pooled, window, at):
    width = cells.shape[0]
    pooled[LEFT : LEFT + width, :] = cells
    pooled[LEFT - 1 : LEFT, :] = beside[:1]
    pooled[LEFT + width : LEFT + width + 1, :] = beside[1:]
    for v in range(3):
        window[v, pl.ds(at, width), :] = pooled[pl.ds(LEFT + 1 - v, width), :].astype(BF16)


def row_pack_kernel(has_second, flags, cot, centre, col_a, col_b, *refs):
    outs, (cells_out, beside_out, ends) = refs[: 2 if has_second else 1], refs[-3:]
    images, height2, width, _ = centre.shape
    row_odd = flags[ROW_ODD] == 1
    lines = [0, 1, 2, height2 - 3, height2 - 2, height2 - 1]
    for i in range(images):
        cells, beside = pool_columns(flags, cot, centre, col_a, col_b, i, lines)
        for n in range(6):
            cells_out[i, n] = cells[n]
            beside_out[i, n] = beside[n]
        for group, is_end in ((cells, False), (beside, True)):
            above = [group[0], 0.75 * (group[0] + group[1]) + 0.25 * group[2]]
            below = [0.25 * group[3] + 0.75 * (group[4] + group[5]), group[5]]
            for second in range(len(outs)):
                for n in range(2):
                    odd, even = (below[n], above[n]) if second else (above[n], below[n])
                    value = jnp.where(row_odd, odd, even)
                    if is_end:
                        ends[second, (2 * i + n) * 2 : (2 * i + n) * 2 + 2, :] = value
                    else:
                        at = (2 * i + n) * width
                        outs[second][at : at + width, :] = value.astype(BF16)
    for second in range(len(outs)):
        outs[second][2 * images * width :, :] = ends[second].astype(BF16)


def main_kernel(flags, cot, centre, col_a, col_b, weight, window, acc, pooled):
    images, height2, width, channels = centre.shape
    height, depths = height2 // 2, weight.shape[0]
    pooled[...] = jnp.zeros_like(pooled)

    def per_image(i, carry):
        cells, beside = pool_columns(flags, cot, centre, col_a, col_b, i, range(1, height2 - 1))
        for p in range(1, height - 1):
            at = 2 * p - 2
            both = [
                0.75 * (group[at + 1] + group[at + 2]) + 0.25 * (group[at] + group[at + 3])
                for group in (cells, beside)
            ]
            where = pl.multiple_of((p + 1) * images * width + i * width, width)
            place(both[0], both[1], pooled.at[p], window, where)
        return carry

    lax.fori_loop(0, images, per_image, 0)
    line = images * width
    inner = (height - 2) * line
    rows = slice(2 * line, 2 * line + inner)
    for k in range(depths):
        for u in range(3):
            part = nt_dot(window[0, rows, :], weight[k, u, 0])
            part = part + nt_dot(window[1, rows, :], weight[k, u, 1])
            part = part + nt_dot(window[2, rows, :], weight[k, u, 2])
            if u == 0:
                acc[k, :inner, :] = part
                acc[k, inner:, :] = jnp.zeros((2 * line, channels), F32)
            else:
                acc[k, u * line : u * line + inner, :] += part


def edge_kernel(has_second, flags, *refs):
    sides = 2 if has_second else 1
    rows, (cells, beside, _, acc, weight) = refs[:sides], refs[sides : sides + 5]
    *grads, window, pooled, ends, total = refs[sides + 5 :]
    images, width = cells.shape[0], cells.shape[2]
    depths, count = acc.shape[:2]
    line = images * width
    height = count // line
    row_odd, top, bottom = flags[ROW_ODD] == 1, flags[TOP] == 1, flags[BOTTOM] == 1
    for n in range(sides):
        ends[n] = rows[n][2 * line :, :].astype(F32)
    pooled[...] = jnp.zeros_like(pooled)
    for i in range(images):
        for_rows = []
        for is_end, own in ((False, cells), (True, beside)):
            def came(from_above, n):
                def of(ref_at):
                    if is_end:
                        at = (2 * i + n) * 2
                        return ends[ref_at, at : at + 2, :]
                    at = (2 * i + n) * width
                    return rows[ref_at][at : at + width, :].astype(F32)

                first = of(0)
                second = of(1) if has_second else jnp.zeros_like(first)
                return jnp.where(row_odd, first, second) if from_above else jnp.where(row_odd, second, first)

            edge = [own[i, n] for n in range(6)]
            zero = jnp.zeros_like(edge[0])
            for_rows.append(
                [
                    jnp.where(top, zero, came(True, 0) + 0.25 * edge[0]),
                    0.75 * (edge[0] + edge[1]) + 0.25 * (jnp.where(top, edge[0], came(True, 1)) + edge[2]),
                    0.75 * (edge[4] + edge[5]) + 0.25 * (jnp.where(bottom, edge[5], came(False, 0)) + edge[3]),
                    jnp.where(bottom, zero, came(False, 1) + 0.25 * edge[5]),
                ]
            )
        for n, p in enumerate((0, 1, height, height + 1)):
            place(for_rows[0][n], for_rows[1][n], pooled.at[n], window, p * line + i * width)
    low, high = slice(0, 2 * line), slice(height * line, (height + 2) * line)
    for k in range(depths):
        total[...] = acc[k]
        for v in range(3):
            total[(height - 2) * line :, :] += nt_dot(window[v, high, :], weight[k, 0, v])
            total[: 2 * line, :] += nt_dot(window[v, low, :], weight[k, 2, v])
            middle = jnp.concatenate(
                [window[v, line : 2 * line, :], window[v, height * line : (height + 1) * line, :]], axis=0
            )
            part = nt_dot(middle, weight[k, 1, v])
            total[:line, :] += part[:line]
            total[(height - 1) * line :, :] += part[line:]
        for apart in range(2 * CHIPS):
            at = pl.multiple_of((flags[GRAY] ^ apart) * line, line)
            grads[apart // 2][apart % 2, k] = total[pl.ds(at, line), :].astype(BF16)


def deal(full, split_refs, core):
    if len(split_refs) == 1:
        split_refs[0][...] = full[...]
        return
    kept, sent = split_refs
    count, rows = kept.shape[:2]
    for j in range(count):
        kept[j] = full[pl.ds(pl.multiple_of((2 * j + core) * rows, 16), rows), :]
        sent[j] = full[pl.ds(pl.multiple_of((2 * j + 1 - core) * rows, 16), rows), :]


def conv_term_kernel(flags, window, saved, *refs):
    split_refs, top, full, flat = refs[:-3], refs[-3], refs[-2], refs[-1]
    images, depths, height, width, channels = saved.shape
    line = images * width
    count = height * line
    split = top.shape[0]
    for k in range(depths):
        for h in range(height):
            for i in range(images):
                at = (h * images + i) * width
                flat[at : at + width, :] = saved[i, k, h]
        flat_t = flat[...].T
        for n in range(9):
            start = (2 - n // 3) * line
            part = jnp.dot(
                flat_t, window[n % 3, start : start + count, :], preferred_element_type=F32
            ).astype(BF16)
            at = (k * 9 + n) * channels
            if at < split:
                top[at : at + channels, :] = part
            else:
                full[at - split : at - split + channels, :] = part
    deal(full, split_refs, flags[CORE])


def pass_on_kernel(*refs):
    for n, piece in enumerate(refs[:-1]):
        refs[-1][n] = piece[1]


def proj_term_kernel(flags, *refs):
    came, (passed, feats, conv_top) = refs[:CHIPS], refs[CHIPS : CHIPS + 3]
    split_refs, tokens, full = refs[CHIPS + 3 : -2], refs[-2], refs[-1]
    images, depths, _, dim = feats.shape
    line = passed.shape[2]
    width = line // images
    for apart in range(2 * CHIPS):
        column = column_of(flags[GRAY] ^ apart)
        for k in range(depths):
            for i in range(images):
                at = pl.multiple_of((i * TILE_COLS + column) * width, width)
                rows = slice(i * width, (i + 1) * width)
                piece = passed[apart // 2, k, rows, :] if apart % 2 else came[apart // 2][0, k, rows, :]
                tokens[k, pl.ds(at, width), :] = piece
    for k in range(depths):
        flat = feats[:, k].reshape(tokens.shape[1], dim)
        part = lax.dot_general(
            flat, tokens[k], (((0,), (0,)), ((), ())), preferred_element_type=F32
        )
        full[k * dim : (k + 1) * dim, :] = part.astype(BF16)
    full[depths * dim :, :] = conv_top[...]
    deal(full, split_refs, flags[CORE])


def feat_grad_kernel(tokens, weight, out, done):
    done[...] = jnp.zeros_like(done)
    images, depths, count, dim = out.shape
    for k in range(depths):
        out[:, k] = nt_dot(tokens[k], weight[k]).astype(BF16).reshape(images, count, dim)


def round_kernel(parts, bits_at, bits, by_columns, flags, *refs):
    ins, outs = refs[:parts], refs[parts:]
    span = 1 << bits
    mine, dp = 0, flags[DP]
    for b in range(bits):
        mine = mine + flags[BITS + bits_at + b] * (1 << b)
    count, _, width = outs[0].shape
    for n, out in enumerate(outs):
        across, apart = n // span, n % span
        for q in range(count):
            block = q * span + (mine ^ apart)
            if by_columns:
                columns = pl.ds(pl.multiple_of((dp ^ across) * width, width), width)
            else:
                columns = slice(None)
            total = ins[0][block, :, columns].astype(F32)
            for other in ins[1:]:
                total = total + other[block, :, columns].astype(F32)
            out[q] = total.astype(out.dtype)


def last_kernel(early_parts, flags, *refs):
    early, late, (sent, kept) = refs[:early_parts], refs[early_parts:-2], refs[-2:]
    first = flags[DP] == 0
    sums = []
    for group in (early, late):
        total = group[0][0].astype(F32)
        for other in group[1:]:
            total = total + other[0].astype(F32)
        sums.append(total)
    sent[...] = jnp.where(first, sums[0], sums[1]).astype(BF16)
    kept[...] = jnp.where(first, sums[1], sums[0])


def join_kernel(scale, flags, kept, came, out):
    width = kept.shape[1]
    at = pl.multiple_of(flags[DP] * width, width)
    out[:, pl.ds(at, width)] = kept[...] * scale
    at = pl.multiple_of((1 - flags[DP]) * width, width)
    out[:, pl.ds(at, width)] = came[...].astype(F32) * scale


def vmem_call(kernel, out_shape, operands, scratch=(), scalars=1, flops=0, limit=16, after=(), aliases=()):
    whole = pl.BlockSpec(memory_space=pltpu.VMEM)
    specs = [pl.BlockSpec(memory_space=pltpu.SMEM)] * scalars + [whole] * (len(operands) - scalars)
    specs += [pl.BlockSpec(memory_space=pl.ANY)] * len(after)
    count = len(operands)

    def run(*refs):
        kernel(*refs[:count], *refs[count + len(after) :])

    moved = sum(a.size * a.dtype.itemsize for a in operands)
    moved += sum(math.prod(s.shape) * s.dtype.itemsize for s in jax.tree.leaves(out_shape))
    return pl.pallas_call(
        run,
        out_shape=out_shape,
        in_specs=specs,
        out_specs=jax.tree.map(lambda _: whole, out_shape),
        scratch_shapes=list(scratch),
        input_output_aliases=dict(aliases),
        compiler_params=pltpu.CompilerParams(vmem_limit_bytes=limit << 20),
        cost_estimate=pl.CostEstimate(flops=flops, bytes_accessed=moved, transcendentals=0),
    )(*operands, *after)


def sds(*shape, dtype=BF16):
    return jax.ShapeDtypeStruct(shape, dtype)


def xor_move(block, apart, across):
    tiles = lax.axis_size("tile")
    if not across:
        return lax.ppermute(block, "tile", [(t, t ^ apart) for t in range(tiles)])
    if not apart:
        return lax.ppermute(block, "dp", [(0, 1), (1, 0)])
    route = [(d * tiles + t, (1 - d) * tiles + (t ^ apart)) for d in range(2) for t in range(tiles)]
    return lax.ppermute(block, ("dp", "tile"), route)


def core_sum(dealt, core):
    if len(dealt) == 1:
        tiles = lax.axis_size("tile")
        pairs = dealt[0].reshape(tiles // 2, 2, dealt[0].shape[0] // tiles, dealt[0].shape[1])
        kept = lax.dynamic_index_in_dim(pairs, core, 1, keepdims=False)
        sent = lax.dynamic_index_in_dim(pairs, 1 - core, 1, keepdims=False)
    else:
        kept, sent = dealt
    return [kept, xor_move(sent, 1, False)]


def deal_round(parts, flags, at, bits, by_columns, after=()):
    span = 1 << bits
    count, rows, channels = parts[0].shape
    if by_columns:
        channels //= 2
    outs = [
        sds(count // span, rows, channels, dtype=F32 if n == 0 else BF16)
        for n in range(span * (2 if by_columns else 1))
    ]
    return vmem_call(
        functools.partial(round_kernel, len(parts), at, bits, by_columns), outs, [flags] + parts, after=after
    )


def send_round(pieces, at, bits):
    span = 1 << bits
    return [pieces[0]] + [
        xor_move(pieces[n], (n % span) << at, n >= span) for n in range(1, len(pieces))
    ]


def per_device(features, proj_weight, conv_weight, saved, cotangent):
    position = lax.axis_index("tile")
    tile_count = lax.axis_size("tile")
    rows = tile_count // TILE_COLS
    gray = position % TILE_COLS
    col, row = column_of(gray), position // TILE_COLS
    images, height2, width2, channels = cotangent.shape
    depths, dim = proj_weight.shape[:2]
    height, width = height2 // 2, width2 // 2
    patches = images * height * width
    line = images * width
    tokens = features.shape[2]
    has_second = rows > 2
    sides = 2 if has_second else 1
    bits = tile_count.bit_length() - 1
    flags = jnp.stack(
        [row % 2, col % 2, row == 0, row == rows - 1, col == 0, col == TILE_COLS - 1]
        + [position % 2, lax.axis_index("dp"), gray]
        + [position >> b & 1 for b in range(bits)]
    ).astype(jnp.int32)

    def swap(block, row_pairs, col_pairs):
        return lax.ppermute(block, "tile", tile_route(row_pairs, col_pairs, rows))

    low, high = cotangent[:, :, :HALO], cotangent[:, :, width2 - HALO :]
    around = paired(TILE_COLS, 1) + [(0, TILE_COLS - 1), (TILE_COLS - 1, 0)]
    col_b = swap(jnp.where(col % 2 == 1, high, low), None, around)
    col_a = swap(jnp.where(col % 2 == 1, low, high), None, paired(TILE_COLS, 0))
    centre = vmem_call(
        centre_kernel,
        sds(images, height2, width, channels, dtype=F32),
        (cotangent,),
        scratch=(pltpu.VMEM((channels // 128, height2, LEFT + width2 + 8, 128), F32),),
        scalars=0,
    )
    *row_out, cells, beside = vmem_call(
        functools.partial(row_pack_kernel, has_second),
        [sds(2 * images * (width + 2), channels)] * sides
        + [sds(images, 6, width, channels, dtype=F32), sds(images, 6, 2, channels, dtype=F32)],
        (flags, cotangent, centre, col_a, col_b),
        scratch=(pltpu.VMEM((sides, 4 * images, channels), F32),),
    )
    came_rows = [swap(row_out[n], paired(rows, n), None) for n in range(sides)]
    conv_flops = 2 * patches * depths * 9 * channels * channels
    window, acc = vmem_call(
        main_kernel,
        [sds(3, (height + 2) * line, channels), sds(depths, patches, channels, dtype=F32)],
        (flags, cotangent, centre, col_a, col_b, conv_weight),
        scratch=(pltpu.VMEM((height, LEFT + width + 8, channels), F32),),
        flops=conv_flops,
        after=(row_out[0],),
    )
    *grads, window = vmem_call(
        functools.partial(edge_kernel, has_second),
        [sds(2, depths, line, channels)] * CHIPS + [sds(3, (height + 2) * line, channels)],
        [flags] + came_rows + [cells, beside, window, acc, conv_weight],
        scratch=(
            pltpu.VMEM((4, LEFT + width + 8, channels), F32),
            pltpu.VMEM((sides, 4 * images, channels), F32),
            pltpu.VMEM((patches, channels), F32),
        ),
        flops=conv_flops // 4,
        aliases={sides + 3: CHIPS},
    )
    came = [grads[0]] + [xor_move(grads[chip], 2 * chip, False) for chip in range(1, CHIPS)]
    to_pass = vmem_call(pass_on_kernel, sds(CHIPS, depths, line, channels), came, scalars=0)
    passed = xor_move(to_pass, 1, False)

    half_rows = depths * (dim + 9 * channels) // 2
    conv_late = half_rows - depths * dim
    block_rows = half_rows // tile_count
    if block_rows % 16:
        dealt = [sds(half_rows, channels)]
    else:
        dealt = [sds(tile_count // 2, block_rows, channels)] * 2
    full = pltpu.VMEM((half_rows, channels), BF16)
    *early, conv_top = vmem_call(
        conv_term_kernel,
        dealt + [sds(conv_late, channels)],
        (flags, window, saved),
        scratch=(full, pltpu.VMEM((patches, channels), BF16)),
        flops=conv_flops,
        after=(to_pass,),
    )
    early_parts = core_sum(early, position % 2)
    proj_flops = 2 * images * tokens * depths * dim * channels
    *terms, token_grad = vmem_call(
        proj_term_kernel,
        dealt + [sds(depths, images * tokens, channels)],
        [flags] + came + [passed, features, conv_top],
        scratch=(full,),
        flops=proj_flops,
    )
    early_pieces = deal_round(early_parts, flags, 1, 0, True, after=(token_grad,))
    early_parts = send_round(early_pieces, 1, 0)
    feature_grad, done = vmem_call(
        feat_grad_kernel,
        [sds(images, depths, tokens, dim), sds(8, 128, dtype=F32)],
        (token_grad, proj_weight),
        scalars=0,
        flops=proj_flops,
        after=(early_pieces[0],),
    )
    late_parts = core_sum(terms, position % 2)
    at, before = 1, done
    while at < bits:
        late_step = 1 if at == 1 else min(2, bits - at)
        late_pieces = deal_round(late_parts, flags, at, late_step, at == 1, after=(before,))
        late_parts = send_round(late_pieces, at, late_step)
        before = late_pieces[0]
        for bit in range(at, at + late_step):
            early_pieces = deal_round(early_parts, flags, bit, 1, False, after=(before,))
            early_parts = send_round(early_pieces, bit, 1)
            before = early_pieces[0]
        at += late_step
    half = sds(block_rows, channels // 2)
    sent, kept = vmem_call(
        functools.partial(last_kernel, len(early_parts)),
        [half, sds(block_rows, channels // 2, dtype=F32)],
        [flags] + early_parts + late_parts,
    )
    other = xor_move(sent, 0, True)
    scale = 1.0 / math.sqrt(images * lax.axis_size("dp") * tokens * tile_count)
    head_grad = vmem_call(
        functools.partial(join_kernel, scale), sds(block_rows, channels, dtype=F32), (flags, kept, other)
    )
    return feature_grad, head_grad


def solution(mesh):
    in_specs = (
        P("dp", None, "tile", None),
        P(),
        P(),
        P("dp", None, "tile", None, None),
        P("dp", "tile", None, None),
    )
    out_specs = (P("dp", None, "tile", None), P(("dp", "tile"), None))
    return jax.shard_map(
        per_device, mesh=mesh, in_specs=in_specs, out_specs=out_specs, check_vma=False
    )
```

```python
import functools
import math

import jax
import jax.numpy as jnp
from jax import lax
from jax.experimental import pallas as pl
from jax.experimental.pallas import tpu as pltpu
from jax.sharding import PartitionSpec as P

TILE_COLS = 8
HALO = 4
LEFT = 8
BF16 = jnp.bfloat16
F32 = jnp.float32
ROW_ODD, COL_ODD, TOP, BOTTOM, LEFT_END, RIGHT_END, CORE, DP, GRAY, BITS = range(10)
CHIPS = TILE_COLS // 2


def gray_of(column):
    return column ^ column >> 1


def column_of(code):
    return code ^ code >> 1 ^ code >> 2


def paired(count, first):
    pairs = []
    for low in range(first, count - 1, 2):
        pairs += [(low, low + 1), (low + 1, low)]
    return pairs


def tile_route(row_pairs, col_pairs, rows):
    row_moves = row_pairs if row_pairs is not None else [(r, r) for r in range(rows)]
    col_moves = col_pairs if col_pairs is not None else [(c, c) for c in range(TILE_COLS)]
    return [
        (r0 * TILE_COLS + gray_of(c0), r1 * TILE_COLS + gray_of(c1))
        for r0, r1 in row_moves
        for c0, c1 in col_moves
    ]


def nt_dot(left, right):
    return lax.dot_general(left, right, (((1,), (1,)), ((), ())), preferred_element_type=F32)


def centre_kernel(cot, pooled, own, wide):
    images, height2, width2, channels = cot.shape
    width = width2 // 2
    wide[...] = jnp.zeros_like(wide)

    def per_image(i, carry):
        for r in range(height2):
            value = cot[i, r].astype(F32)
            for h in range(channels // 128):
                wide[h, r, LEFT : LEFT + width2, :] = value[:, h * 128 : (h + 1) * 128]
            own[i, r, 0:1, :] = value[:1]
            own[i, r, 1:2, :] = value[width2 - 1 :]
        for r in range(height2):
            for h in range(channels // 128):
                taps = [wide[h, r, pl.ds(LEFT - 1 + n, width, stride=2), :] for n in range(4)]
                pooled[i, r, :, h * 128 : (h + 1) * 128] = 0.75 * (taps[1] + taps[2]) + 0.25 * (taps[0] + taps[3])
        return carry

    lax.fori_loop(0, images, per_image, 0)


def pool_columns(flags, centre, own, col_a, col_b, i, lines):
    width, channels = centre.shape[2:]
    col_odd, left, right = flags[COL_ODD] == 1, flags[LEFT_END] == 1, flags[RIGHT_END] == 1
    cell = lax.broadcasted_iota(jnp.int32, (width, channels), 0)
    is_first, is_last = cell == 0, cell == width - 1
    cells, beside = [], []
    for r in lines:
        own_first, own_last = own[i, r, 0:1, :], own[i, r, 1:2, :]
        one, two = col_a[i, r].astype(F32), col_b[i, r].astype(F32)
        before, after = jnp.where(col_odd, one, two), jnp.where(col_odd, two, one)
        near_before = jnp.where(left, own_first, before[3:4])
        near_after = jnp.where(right, own_last, after[0:1])
        cells.append(
            centre[i, r] + 0.25 * (jnp.where(is_first, near_before, 0.0) + jnp.where(is_last, near_after, 0.0))
        )
        first = 0.75 * (before[2:3] + before[3:4]) + 0.25 * (before[1:2] + own_first)
        last = 0.75 * (after[0:1] + after[1:2]) + 0.25 * (own_last + after[2:3])
        beside.append(
            jnp.concatenate([jnp.where(left, 0.0, first), jnp.where(right, 0.0, last)], axis=0)
        )
    return cells, beside


def place(cells, beside, pooled, window, at):
    width = cells.shape[0]
    pooled[LEFT : LEFT + width, :] = cells
    pooled[LEFT - 1 : LEFT, :] = beside[:1]
    pooled[LEFT + width : LEFT + width + 1, :] = beside[1:]
    for v in range(3):
        window[v, pl.ds(at, width), :] = pooled[pl.ds(LEFT + 1 - v, width), :].astype(BF16)


def row_pack_kernel(has_second, flags, centre, own, col_a, col_b, *refs):
    outs, (cells_out, beside_out, ends) = refs[: 2 if has_second else 1], refs[-3:]
    images, height2, width, _ = centre.shape
    row_odd = flags[ROW_ODD] == 1
    lines = [0, 1, 2, height2 - 3, height2 - 2, height2 - 1]
    for i in range(images):
        cells, beside = pool_columns(flags, centre, own, col_a, col_b, i, lines)
        for n in range(6):
            cells_out[i, n] = cells[n]
            beside_out[i, n] = beside[n]
        for group, is_end in ((cells, False), (beside, True)):
            above = [group[0], 0.75 * (group[0] + group[1]) + 0.25 * group[2]]
            below = [0.25 * group[3] + 0.75 * (group[4] + group[5]), group[5]]
            for second in range(len(outs)):
                for n in range(2):
                    odd, even = (below[n], above[n]) if second else (above[n], below[n])
                    value = jnp.where(row_odd, odd, even)
                    if is_end:
                        ends[second, (2 * i + n) * 2 : (2 * i + n) * 2 + 2, :] = value
                    else:
                        at = (2 * i + n) * width
                        outs[second][at : at + width, :] = value.astype(BF16)
    for second in range(len(outs)):
        outs[second][2 * images * width :, :] = ends[second].astype(BF16)


def main_kernel(flags, centre, own, col_a, col_b, weight, window, acc, pooled):
    images, height2, width, channels = centre.shape
    height, depths = height2 // 2, weight.shape[0]
    pooled[...] = jnp.zeros_like(pooled)

    def per_image(i, carry):
        cells, beside = pool_columns(flags, centre, own, col_a, col_b, i, range(1, height2 - 1))
        for p in range(1, height - 1):
            at = 2 * p - 2
            both = [
                0.75 * (group[at + 1] + group[at + 2]) + 0.25 * (group[at] + group[at + 3])
                for group in (cells, beside)
            ]
            where = pl.multiple_of((p + 1) * images * width + i * width, width)
            place(both[0], both[1], pooled.at[p], window, where)
        return carry

    lax.fori_loop(0, images, per_image, 0)
    line = images * width
    inner = (height - 2) * line
    rows = slice(2 * line, 2 * line + inner)
    for k in range(depths):
        for u in range(3):
            part = nt_dot(window[0, rows, :], weight[k, u, 0])
            part = part + nt_dot(window[1, rows, :], weight[k, u, 1])
            part = part + nt_dot(window[2, rows, :], weight[k, u, 2])
            if u == 0:
                acc[k, :inner, :] = part
                acc[k, inner:, :] = jnp.zeros((2 * line, channels), F32)
            else:
                acc[k, u * line : u * line + inner, :] += part


def edge_kernel(has_second, flags, *refs):
    sides = 2 if has_second else 1
    rows, (cells, beside, _, acc, weight) = refs[:sides], refs[sides : sides + 5]
    *grads, window, pooled, ends, total = refs[sides + 5 :]
    images, width = cells.shape[0], cells.shape[2]
    depths, count = acc.shape[:2]
    line = images * width
    height = count // line
    row_odd, top, bottom = flags[ROW_ODD] == 1, flags[TOP] == 1, flags[BOTTOM] == 1
    for n in range(sides):
        ends[n] = rows[n][2 * line :, :].astype(F32)
    pooled[...] = jnp.zeros_like(pooled)
    for i in range(images):
        for_rows = []
        for is_end, own in ((False, cells), (True, beside)):
            def came(from_above, n):
                def of(ref_at):
                    if is_end:
                        at = (2 * i + n) * 2
                        return ends[ref_at, at : at + 2, :]
                    at = (2 * i + n) * width
                    return rows[ref_at][at : at + width, :].astype(F32)

                first = of(0)
                second = of(1) if has_second else jnp.zeros_like(first)
                return jnp.where(row_odd, first, second) if from_above else jnp.where(row_odd, second, first)

            edge = [own[i, n] for n in range(6)]
            zero = jnp.zeros_like(edge[0])
            for_rows.append(
                [
                    jnp.where(top, zero, came(True, 0) + 0.25 * edge[0]),
                    0.75 * (edge[0] + edge[1]) + 0.25 * (jnp.where(top, edge[0], came(True, 1)) + edge[2]),
                    0.75 * (edge[4] + edge[5]) + 0.25 * (jnp.where(bottom, edge[5], came(False, 0)) + edge[3]),
                    jnp.where(bottom, zero, came(False, 1) + 0.25 * edge[5]),
                ]
            )
        for n, p in enumerate((0, 1, height, height + 1)):
            place(for_rows[0][n], for_rows[1][n], pooled.at[n], window, p * line + i * width)
    low, high = slice(0, 2 * line), slice(height * line, (height + 2) * line)
    for k in range(depths):
        total[...] = acc[k]
        for v in range(3):
            total[(height - 2) * line :, :] += nt_dot(window[v, high, :], weight[k, 0, v])
            total[: 2 * line, :] += nt_dot(window[v, low, :], weight[k, 2, v])
            middle = jnp.concatenate(
                [window[v, line : 2 * line, :], window[v, height * line : (height + 1) * line, :]], axis=0
            )
            part = nt_dot(middle, weight[k, 1, v])
            total[:line, :] += part[:line]
            total[(height - 1) * line :, :] += part[line:]
        for apart in range(2 * CHIPS):
            at = pl.multiple_of((flags[GRAY] ^ apart) * line, line)
            grads[apart // 2][apart % 2, k] = total[pl.ds(at, line), :].astype(BF16)


def deal(full, split_refs, core):
    if len(split_refs) == 1:
        split_refs[0][...] = full[...]
        return
    kept, *sent = split_refs
    count, rows = kept.shape[:2]
    size = sent[0].shape[0]
    for j in range(count):
        kept[j] = full[pl.ds(pl.multiple_of((2 * j + core) * rows, 16), rows), :]
        sent[j // size][j % size] = full[pl.ds(pl.multiple_of((2 * j + 1 - core) * rows, 16), rows), :]


def conv_term_kernel(flags, window, saved, *refs):
    split_refs, top, full, flat = refs[:-3], refs[-3], refs[-2], refs[-1]
    images, depths, height, width, channels = saved.shape
    line = images * width
    count = height * line
    split = top.shape[0]
    for k in range(depths):
        for h in range(height):
            for i in range(images):
                at = (h * images + i) * width
                flat[at : at + width, :] = saved[i, k, h]
        flat_t = flat[...].T
        for n in range(9):
            start = (2 - n // 3) * line
            part = jnp.dot(
                flat_t, window[n % 3, start : start + count, :], preferred_element_type=F32
            ).astype(BF16)
            at = (k * 9 + n) * channels
            if at < split:
                top[at : at + channels, :] = part
            else:
                full[at - split : at - split + channels, :] = part
    deal(full, split_refs, flags[CORE])


def pass_on_kernel(*refs):
    for n, piece in enumerate(refs[:-1]):
        refs[-1][n] = piece[1]


def proj_term_kernel(flags, *refs):
    came, (passed, feats, conv_top) = refs[:CHIPS], refs[CHIPS : CHIPS + 3]
    split_refs, tokens, full = refs[CHIPS + 3 : -2], refs[-2], refs[-1]
    images, depths, _, dim = feats.shape
    line = passed.shape[2]
    width = line // images
    for apart in range(2 * CHIPS):
        column = column_of(flags[GRAY] ^ apart)
        for k in range(depths):
            for i in range(images):
                at = pl.multiple_of((i * TILE_COLS + column) * width, width)
                rows = slice(i * width, (i + 1) * width)
                piece = passed[apart // 2, k, rows, :] if apart % 2 else came[apart // 2][0, k, rows, :]
                tokens[k, pl.ds(at, width), :] = piece
    for k in range(depths):
        flat = feats[:, k].reshape(tokens.shape[1], dim)
        part = lax.dot_general(
            flat, tokens[k], (((0,), (0,)), ((), ())), preferred_element_type=F32
        )
        full[k * dim : (k + 1) * dim, :] = part.astype(BF16)
    full[depths * dim :, :] = conv_top[...]
    deal(full, split_refs, flags[CORE])


def feat_grad_kernel(tokens, weight, out):
    images, depths, count, dim = out.shape
    for k in range(depths):
        out[:, k] = nt_dot(tokens[k], weight[k]).astype(BF16).reshape(images, count, dim)


def take(part, block, at, columns=None):
    size = part[0].shape[0]
    return part[block // size][block % size + at, :, slice(None) if columns is None else columns].astype(F32)


def round_kernel(jobs, flags, *refs):
    ins, outs, dp = list(refs[: sum(sum(job[0]) for job in jobs)]), refs, flags[DP]
    outs = list(refs[len(ins) :])
    for sizes, at, bits, by_columns, cut in jobs:
        parts = []
        for size in sizes:
            parts.append(ins[:size])
            del ins[:size]
        span = 1 << bits
        mine = 0
        for b in range(bits):
            mine = mine + flags[BITS + at + b] * (1 << b)
        for n in range(span * (2 if by_columns else 1)):
            across, apart = n // span, n % span
            pieces = outs[: cut if n else 1]
            del outs[: len(pieces)]
            count, _, width = pieces[0].shape
            columns = None
            if by_columns:
                columns = pl.ds(pl.multiple_of((dp ^ across) * width, width), width)
            for q in range(count):
                total = take(parts[0], q * span, mine ^ apart, columns)
                for other in parts[1:]:
                    total = total + take(other, q * span, mine ^ apart, columns)
                for p, piece in enumerate(pieces):
                    piece[q] = total[:, p * width : (p + 1) * width].astype(piece.dtype)


def last_kernel(early_parts, flags, *refs):
    ins, (sent, kept) = list(refs[:-2]), refs[-2:]
    first = flags[DP] == 0
    sums = []
    for sizes in (early_parts, (1,) * (len(ins) - sum(early_parts))):
        total = 0.0
        for size in sizes:
            total = total + take(ins[:size], 0, 0)
            del ins[:size]
        sums.append(total)
    wide = jnp.concatenate([sums[1], sums[1]], axis=1)
    sent[...] = jnp.where(first, sums[0], wide).astype(BF16)
    kept[...] = jnp.where(first, wide, sums[0])


def join_kernel(scale, flags, kept, came, out):
    half = kept.shape[1] // 2
    first = flags[DP] == 0
    mine, other = kept[...], came[...].astype(F32)
    beside = jnp.concatenate([mine[:, :half], other[:, :half]], axis=1)
    out[...] = jnp.where(first, beside, mine + other) * scale


def vmem_call(kernel, out_shape, operands, scratch=(), scalars=1, flops=0, limit=16, after=(), aliases=()):
    whole = pl.BlockSpec(memory_space=pltpu.VMEM)
    specs = [pl.BlockSpec(memory_space=pltpu.SMEM)] * scalars + [whole] * (len(operands) - scalars)
    specs += [pl.BlockSpec(memory_space=pl.ANY)] * len(after)
    count = len(operands)

    def run(*refs):
        kernel(*refs[:count], *refs[count + len(after) :])

    moved = sum(a.size * a.dtype.itemsize for a in operands)
    moved += sum(math.prod(s.shape) * s.dtype.itemsize for s in jax.tree.leaves(out_shape))
    return pl.pallas_call(
        run,
        out_shape=out_shape,
        in_specs=specs,
        out_specs=jax.tree.map(lambda _: whole, out_shape),
        scratch_shapes=list(scratch),
        input_output_aliases=dict(aliases),
        compiler_params=pltpu.CompilerParams(vmem_limit_bytes=limit << 20),
        cost_estimate=pl.CostEstimate(flops=flops, bytes_accessed=moved, transcendentals=0),
    )(*operands, *after)


def sds(*shape, dtype=BF16):
    return jax.ShapeDtypeStruct(shape, dtype)


def xor_move(block, apart, across):
    tiles = lax.axis_size("tile")
    if not across:
        return lax.ppermute(block, "tile", [(t, t ^ apart) for t in range(tiles)])
    if not apart:
        return lax.ppermute(block, "dp", [(0, 1), (1, 0)])
    route = [(d * tiles + t, (1 - d) * tiles + (t ^ apart)) for d in range(2) for t in range(tiles)]
    return lax.ppermute(block, ("dp", "tile"), route)


def core_sum(dealt, core, pieces=1):
    if len(dealt) == 1:
        tiles = lax.axis_size("tile")
        pairs = dealt[0].reshape(tiles // 2, 2, dealt[0].shape[0] // tiles, dealt[0].shape[1])
        kept = lax.dynamic_index_in_dim(pairs, core, 1, keepdims=False)
        sent = lax.dynamic_index_in_dim(pairs, 1 - core, 1, keepdims=False)
        size = sent.shape[0] // pieces
        sent = [sent[n * size : (n + 1) * size] for n in range(pieces)]
    else:
        kept, *sent = dealt
    return [[kept], [xor_move(piece, 1, False) for piece in sent]]


def deal_rounds(jobs, flags, after=()):
    outs, plans, operands = [], [], [flags]
    for parts, at, bits, by_columns, cut in jobs:
        span = 1 << bits
        count, rows, channels = parts[0][0].shape
        channels = channels // 2 if by_columns else channels
        for n in range(span * (2 if by_columns else 1)):
            if n == 0:
                outs.append(sds(count // span, rows, channels, dtype=F32))
            else:
                outs += [sds(count // span, rows, channels // cut)] * cut
        plans.append((tuple(len(part) for part in parts), at, bits, by_columns, cut))
        operands += [piece for part in parts for piece in part]
    pieces = list(vmem_call(functools.partial(round_kernel, plans), outs, operands, after=after))
    token, sums = pieces[0], []
    for _, at, bits, by_columns, cut in plans:
        span = 1 << bits
        parts = [[pieces.pop(0)]]
        for n in range(1, span * (2 if by_columns else 1)):
            parts.append([xor_move(pieces.pop(0), (n % span) << at, n >= span) for _ in range(cut)])
        sums.append(parts)
    return sums, token


def per_device(features, proj_weight, conv_weight, saved, cotangent):
    position = lax.axis_index("tile")
    tile_count = lax.axis_size("tile")
    rows = tile_count // TILE_COLS
    gray = position % TILE_COLS
    col, row = column_of(gray), position // TILE_COLS
    images, height2, width2, channels = cotangent.shape
    depths, dim = proj_weight.shape[:2]
    height, width = height2 // 2, width2 // 2
    patches = images * height * width
    line = images * width
    tokens = features.shape[2]
    has_second = rows > 2
    sides = 2 if has_second else 1
    bits = tile_count.bit_length() - 1
    flags = jnp.stack(
        [row % 2, col % 2, row == 0, row == rows - 1, col == 0, col == TILE_COLS - 1]
        + [position % 2, lax.axis_index("dp"), gray]
        + [position >> b & 1 for b in range(bits)]
    ).astype(jnp.int32)

    def swap(block, row_pairs, col_pairs):
        return lax.ppermute(block, "tile", tile_route(row_pairs, col_pairs, rows))

    low, high = cotangent[:, :, :HALO], cotangent[:, :, width2 - HALO :]
    around = paired(TILE_COLS, 1) + [(0, TILE_COLS - 1), (TILE_COLS - 1, 0)]
    col_b = swap(jnp.where(col % 2 == 1, high, low), None, around)
    col_a = swap(jnp.where(col % 2 == 1, low, high), None, paired(TILE_COLS, 0))
    centre, own = vmem_call(
        centre_kernel,
        [sds(images, height2, width, channels, dtype=F32), sds(images, height2, 2, channels, dtype=F32)],
        (cotangent,),
        scratch=(pltpu.VMEM((channels // 128, height2, LEFT + width2 + 8, 128), F32),),
        scalars=0,
    )
    *row_out, cells, beside = vmem_call(
        functools.partial(row_pack_kernel, has_second),
        [sds(2 * images * (width + 2), channels)] * sides
        + [sds(images, 6, width, channels, dtype=F32), sds(images, 6, 2, channels, dtype=F32)],
        (flags, centre, own, col_a, col_b),
        scratch=(pltpu.VMEM((sides, 4 * images, channels), F32),),
    )
    came_rows = [swap(row_out[n], paired(rows, n), None) for n in range(sides)]
    conv_flops = 2 * patches * depths * 9 * channels * channels
    window, acc = vmem_call(
        main_kernel,
        [sds(3, (height + 2) * line, channels), sds(depths, patches, channels, dtype=F32)],
        (flags, centre, own, col_a, col_b, conv_weight),
        scratch=(pltpu.VMEM((height, LEFT + width + 8, channels), F32),),
        flops=conv_flops,
        after=(row_out[0],),
    )
    *grads, window = vmem_call(
        functools.partial(edge_kernel, has_second),
        [sds(2, depths, line, channels)] * CHIPS + [sds(3, (height + 2) * line, channels)],
        [flags] + came_rows + [cells, beside, window, acc, conv_weight],
        scratch=(
            pltpu.VMEM((4, LEFT + width + 8, channels), F32),
            pltpu.VMEM((sides, 4 * images, channels), F32),
            pltpu.VMEM((patches, channels), F32),
        ),
        flops=conv_flops // 4,
        aliases={sides + 3: CHIPS},
    )
    came = [grads[0]] + [xor_move(grads[chip], 2 * chip, False) for chip in range(1, CHIPS)]
    to_pass = vmem_call(pass_on_kernel, sds(CHIPS, depths, line, channels), came, scalars=0)
    passed = xor_move(to_pass, 1, False)

    half_rows = depths * (dim + 9 * channels) // 2
    conv_late = half_rows - depths * dim
    block_rows = half_rows // tile_count
    pieces = 4
    if block_rows % 16:
        dealt = [sds(half_rows, channels)]
    else:
        dealt = [sds(tile_count // 2, block_rows, channels)]
        dealt += [sds(tile_count // 2 // pieces, block_rows, channels)] * pieces
    full = pltpu.VMEM((half_rows, channels), BF16)
    *early, conv_top = vmem_call(
        conv_term_kernel,
        dealt + [sds(conv_late, channels)],
        (flags, window, saved),
        scratch=(full, pltpu.VMEM((patches, channels), BF16)),
        flops=conv_flops,
    )
    (early_parts,), before = deal_rounds([(core_sum(early, position % 2, pieces), 1, 1, False, 1)], flags)
    proj_flops = 2 * images * tokens * depths * dim * channels
    *terms, token_grad = vmem_call(
        proj_term_kernel,
        dealt + [sds(depths, images * tokens, channels)],
        [flags] + came + [passed, features, conv_top],
        scratch=(full,),
        flops=proj_flops,
        after=(before,),
    )
    (late_parts,), before = deal_rounds(
        [(core_sum(terms, position % 2, pieces), 1, 1, True, 1)], flags, after=(token_grad,)
    )
    at = 2
    while at < bits:
        step = min(2, bits - at)
        if step == 2:
            (early_parts,), before = deal_rounds([(early_parts, at, 1, False, 1)], flags, after=(before,))
        (late_parts, early_parts), before = deal_rounds(
            [(late_parts, at, step, False, 1), (early_parts, at + step - 1, 1, False, 1)], flags, after=(before,)
        )
        at += step
    feature_grad = vmem_call(
        feat_grad_kernel,
        sds(images, depths, tokens, dim),
        (token_grad, proj_weight),
        scalars=0,
        flops=proj_flops,
        after=(before,),
    )
    sent, kept = vmem_call(
        functools.partial(last_kernel, tuple(len(part) for part in early_parts)),
        [sds(block_rows, channels), sds(block_rows, channels, dtype=F32)],
        [flags] + [piece for part in early_parts + late_parts for piece in part],
    )
    other = xor_move(sent, 0, True)
    scale = 1.0 / math.sqrt(images * lax.axis_size("dp") * tokens * tile_count)
    head_grad = vmem_call(
        functools.partial(join_kernel, scale), sds(block_rows, channels, dtype=F32), (flags, kept, other)
    )
    return feature_grad, head_grad


def solution(mesh):
    in_specs = (
        P("dp", None, "tile", None),
        P(),
        P(),
        P("dp", None, "tile", None, None),
        P("dp", "tile", None, None),
    )
    out_specs = (P("dp", None, "tile", None), P(("dp", "tile"), None))
    return jax.shard_map(
        per_device, mesh=mesh, in_specs=in_specs, out_specs=out_specs, check_vma=False
    )
```

```python
import functools
import math

import jax
import jax.numpy as jnp
from jax import lax
from jax.experimental import pallas as pl
from jax.experimental.pallas import tpu as pltpu
from jax.sharding import PartitionSpec as P

TILE_COLS = 8
HALO = 4
LEFT = 8
BF16 = jnp.bfloat16
F32 = jnp.float32
ROW_ODD, COL_ODD, TOP, BOTTOM, LEFT_END, RIGHT_END, CORE, DP, GRAY, BITS = range(10)
CHIPS = TILE_COLS // 2


def gray_of(column):
    return column ^ column >> 1


def column_of(code):
    return code ^ code >> 1 ^ code >> 2


def paired(count, first):
    pairs = []
    for low in range(first, count - 1, 2):
        pairs += [(low, low + 1), (low + 1, low)]
    return pairs


def tile_route(row_pairs, col_pairs, rows):
    row_moves = row_pairs if row_pairs is not None else [(r, r) for r in range(rows)]
    col_moves = col_pairs if col_pairs is not None else [(c, c) for c in range(TILE_COLS)]
    return [
        (r0 * TILE_COLS + gray_of(c0), r1 * TILE_COLS + gray_of(c1))
        for r0, r1 in row_moves
        for c0, c1 in col_moves
    ]


def nt_dot(left, right):
    return lax.dot_general(left, right, (((1,), (1,)), ((), ())), preferred_element_type=F32)


def centre_kernel(cot, pooled, wide):
    images, height2, width2, channels = cot.shape
    width = width2 // 2
    wide[...] = jnp.zeros_like(wide)

    def per_image(i, carry):
        for r in range(height2):
            value = cot[i, r].astype(F32)
            for h in range(channels // 128):
                wide[h, r, LEFT : LEFT + width2, :] = value[:, h * 128 : (h + 1) * 128]
            pooled[i, r, width : width + 1, :] = value[:1]
            pooled[i, r, width + 1 : width + 2, :] = value[width2 - 1 :]
        for r in range(height2):
            for h in range(channels // 128):
                taps = [wide[h, r, pl.ds(LEFT - 1 + n, width, stride=2), :] for n in range(4)]
                pooled[i, r, :width, h * 128 : (h + 1) * 128] = 0.75 * (taps[1] + taps[2]) + 0.25 * (taps[0] + taps[3])
        return carry

    lax.fori_loop(0, images, per_image, 0)


def pool_columns(flags, centre, col_a, col_b, i, lines):
    width, channels = centre.shape[2] - 8, centre.shape[3]
    col_odd, left, right = flags[COL_ODD] == 1, flags[LEFT_END] == 1, flags[RIGHT_END] == 1
    cell = lax.broadcasted_iota(jnp.int32, (width, channels), 0)
    is_first, is_last = cell == 0, cell == width - 1
    cells, beside = [], []
    for r in lines:
        own_first, own_last = centre[i, r, width : width + 1, :], centre[i, r, width + 1 : width + 2, :]
        one, two = col_a[i, r].astype(F32), col_b[i, r].astype(F32)
        before, after = jnp.where(col_odd, one, two), jnp.where(col_odd, two, one)
        near_before = jnp.where(left, own_first, before[3:4])
        near_after = jnp.where(right, own_last, after[0:1])
        cells.append(
            centre[i, r, :width, :] + 0.25 * (jnp.where(is_first, near_before, 0.0) + jnp.where(is_last, near_after, 0.0))
        )
        first = 0.75 * (before[2:3] + before[3:4]) + 0.25 * (before[1:2] + own_first)
        last = 0.75 * (after[0:1] + after[1:2]) + 0.25 * (own_last + after[2:3])
        beside.append(
            jnp.concatenate([jnp.where(left, 0.0, first), jnp.where(right, 0.0, last)], axis=0)
        )
    return cells, beside


def place(cells, beside, pooled, window, at):
    width = cells.shape[0]
    pooled[LEFT : LEFT + width, :] = cells
    pooled[LEFT - 1 : LEFT, :] = beside[:1]
    pooled[LEFT + width : LEFT + width + 1, :] = beside[1:]
    for v in range(3):
        window[v, pl.ds(at, width), :] = pooled[pl.ds(LEFT + 1 - v, width), :].astype(BF16)


def row_pack_kernel(has_second, flags, centre, col_a, col_b, *refs):
    outs, (cells_out, beside_out, ends) = refs[: 2 if has_second else 1], refs[-3:]
    images, height2, width = centre.shape[0], centre.shape[1], centre.shape[2] - 8
    row_odd = flags[ROW_ODD] == 1
    lines = [0, 1, 2, height2 - 3, height2 - 2, height2 - 1]
    for i in range(images):
        cells, beside = pool_columns(flags, centre, col_a, col_b, i, lines)
        for n in range(6):
            cells_out[i, n] = cells[n]
            beside_out[i, n] = beside[n]
        for group, is_end in ((cells, False), (beside, True)):
            above = [group[0], 0.75 * (group[0] + group[1]) + 0.25 * group[2]]
            below = [0.25 * group[3] + 0.75 * (group[4] + group[5]), group[5]]
            for second in range(len(outs)):
                for n in range(2):
                    odd, even = (below[n], above[n]) if second else (above[n], below[n])
                    value = jnp.where(row_odd, odd, even)
                    if is_end:
                        ends[second, (2 * i + n) * 2 : (2 * i + n) * 2 + 2, :] = value
                    else:
                        at = (2 * i + n) * width
                        outs[second][at : at + width, :] = value.astype(BF16)
    for second in range(len(outs)):
        outs[second][2 * images * width :, :] = ends[second].astype(BF16)


def main_kernel(flags, centre, col_a, col_b, weight, window, acc, pooled):
    images, height2, width, channels = centre.shape[0], centre.shape[1], centre.shape[2] - 8, centre.shape[3]
    height, depths = height2 // 2, weight.shape[0]
    pooled[...] = jnp.zeros_like(pooled)

    def per_image(i, carry):
        cells, beside = pool_columns(flags, centre, col_a, col_b, i, range(1, height2 - 1))
        for p in range(1, height - 1):
            at = 2 * p - 2
            both = [
                0.75 * (group[at + 1] + group[at + 2]) + 0.25 * (group[at] + group[at + 3])
                for group in (cells, beside)
            ]
            where = pl.multiple_of((p + 1) * images * width + i * width, width)
            place(both[0], both[1], pooled.at[p], window, where)
        return carry

    lax.fori_loop(0, images, per_image, 0)
    line = images * width
    inner = (height - 2) * line
    rows = slice(2 * line, 2 * line + inner)
    for k in range(depths):
        for u in range(3):
            part = nt_dot(window[0, rows, :], weight[k, u, 0])
            part = part + nt_dot(window[1, rows, :], weight[k, u, 1])
            part = part + nt_dot(window[2, rows, :], weight[k, u, 2])
            if u == 0:
                acc[k, :inner, :] = part
                acc[k, inner:, :] = jnp.zeros((2 * line, channels), F32)
            else:
                acc[k, u * line : u * line + inner, :] += part


def edge_kernel(has_second, flags, *refs):
    sides = 2 if has_second else 1
    rows, (cells, beside, _, acc, weight) = refs[:sides], refs[sides : sides + 5]
    *grads, window, pooled, ends, total = refs[sides + 5 :]
    images, width = cells.shape[0], cells.shape[2]
    depths, count = acc.shape[:2]
    line = images * width
    height = count // line
    row_odd, top, bottom = flags[ROW_ODD] == 1, flags[TOP] == 1, flags[BOTTOM] == 1
    for n in range(sides):
        ends[n] = rows[n][2 * line :, :].astype(F32)
    pooled[...] = jnp.zeros_like(pooled)
    for i in range(images):
        for_rows = []
        for is_end, own in ((False, cells), (True, beside)):
            def came(from_above, n):
                def of(ref_at):
                    if is_end:
                        at = (2 * i + n) * 2
                        return ends[ref_at, at : at + 2, :]
                    at = (2 * i + n) * width
                    return rows[ref_at][at : at + width, :].astype(F32)

                first = of(0)
                second = of(1) if has_second else jnp.zeros_like(first)
                return jnp.where(row_odd, first, second) if from_above else jnp.where(row_odd, second, first)

            edge = [own[i, n] for n in range(6)]
            zero = jnp.zeros_like(edge[0])
            for_rows.append(
                [
                    jnp.where(top, zero, came(True, 0) + 0.25 * edge[0]),
                    0.75 * (edge[0] + edge[1]) + 0.25 * (jnp.where(top, edge[0], came(True, 1)) + edge[2]),
                    0.75 * (edge[4] + edge[5]) + 0.25 * (jnp.where(bottom, edge[5], came(False, 0)) + edge[3]),
                    jnp.where(bottom, zero, came(False, 1) + 0.25 * edge[5]),
                ]
            )
        for n, p in enumerate((0, 1, height, height + 1)):
            place(for_rows[0][n], for_rows[1][n], pooled.at[n], window, p * line + i * width)
    low, high = slice(0, 2 * line), slice(height * line, (height + 2) * line)
    for k in range(depths):
        total[...] = acc[k]
        for v in range(3):
            total[(height - 2) * line :, :] += nt_dot(window[v, high, :], weight[k, 0, v])
            total[: 2 * line, :] += nt_dot(window[v, low, :], weight[k, 2, v])
            middle = jnp.concatenate(
                [window[v, line : 2 * line, :], window[v, height * line : (height + 1) * line, :]], axis=0
            )
            part = nt_dot(middle, weight[k, 1, v])
            total[:line, :] += part[:line]
            total[(height - 1) * line :, :] += part[line:]
        for apart in range(2 * CHIPS):
            at = pl.multiple_of((flags[GRAY] ^ apart) * line, line)
            grads[apart // 2][apart % 2, k] = total[pl.ds(at, line), :].astype(BF16)


def deal(full, split_refs, core, turned):
    if len(split_refs) == 1:
        split_refs[0][...] = full[...]
        return
    kept, *sent = split_refs
    count, rows = kept.shape[:2]
    size = sent[0].shape[0]
    for j in range(count):
        p = j >> 1 | (j & 1) * (count >> 1) if turned else j
        kept[p] = full[pl.ds(pl.multiple_of((2 * j + core) * rows, 16), rows), :]
        sent[p // size][p % size] = full[pl.ds(pl.multiple_of((2 * j + 1 - core) * rows, 16), rows), :]


def conv_term_kernel(flags, window, saved, *refs):
    split_refs, top, full, flat = refs[:-3], refs[-3], refs[-2], refs[-1]
    images, depths, height, width, channels = saved.shape
    line = images * width
    count = height * line
    split = top.shape[0]
    for k in range(depths):
        for h in range(height):
            for i in range(images):
                at = (h * images + i) * width
                flat[at : at + width, :] = saved[i, k, h]
        flat_t = flat[...].T
        for n in range(9):
            start = (2 - n // 3) * line
            part = jnp.dot(
                flat_t, window[n % 3, start : start + count, :], preferred_element_type=F32
            ).astype(BF16)
            at = (k * 9 + n) * channels
            if at < split:
                top[at : at + channels, :] = part
            else:
                full[at - split : at - split + channels, :] = part
    deal(full, split_refs, flags[CORE], True)


def pass_on_kernel(*refs):
    for n, piece in enumerate(refs[:-1]):
        refs[-1][n] = piece[1]


def proj_term_kernel(flags, *refs):
    came, (passed, feats, conv_top) = refs[:CHIPS], refs[CHIPS : CHIPS + 3]
    split_refs, tokens, full = refs[CHIPS + 3 : -2], refs[-2], refs[-1]
    images, depths, _, dim = feats.shape
    line = passed.shape[2]
    width = line // images
    for apart in range(2 * CHIPS):
        column = column_of(flags[GRAY] ^ apart)
        for k in range(depths):
            for i in range(images):
                at = pl.multiple_of((i * TILE_COLS + column) * width, width)
                rows = slice(i * width, (i + 1) * width)
                piece = passed[apart // 2, k, rows, :] if apart % 2 else came[apart // 2][0, k, rows, :]
                tokens[k, pl.ds(at, width), :] = piece
    for k in range(depths):
        flat = feats[:, k].reshape(tokens.shape[1], dim)
        part = lax.dot_general(
            flat, tokens[k], (((0,), (0,)), ((), ())), preferred_element_type=F32
        )
        full[k * dim : (k + 1) * dim, :] = part.astype(BF16)
    full[depths * dim :, :] = conv_top[...]
    deal(full, split_refs, flags[CORE], False)


def feat_grad_kernel(tokens, weight, out):
    images, depths, count, dim = out.shape
    for k in range(depths):
        out[:, k] = nt_dot(tokens[k], weight[k]).astype(BF16).reshape(images, count, dim)


def take(part, block, at, columns=None):
    size = part[0].shape[0]
    return part[block // size][block % size + at, :, slice(None) if columns is None else columns].astype(F32)


def round_kernel(jobs, flags, *refs):
    ins, outs, dp = list(refs[: sum(sum(job[0]) for job in jobs)]), refs, flags[DP]
    outs = list(refs[len(ins) :])
    for sizes, at, bits, by_columns, heights in jobs:
        parts = []
        for size in sizes:
            parts.append(ins[:size])
            del ins[:size]
        span = 1 << bits
        mine = 0
        for b in range(bits):
            mine = mine + flags[BITS + at + b] * (1 << b)
        for n in range(span * (2 if by_columns else 1)):
            across, apart = n // span, n % span
            pieces = outs[: len(heights) if n else 1]
            del outs[: len(pieces)]
            count, _, width = pieces[0].shape
            columns = None
            if by_columns:
                columns = pl.ds(pl.multiple_of((dp ^ across) * width, width), width)
            for q in range(count):
                total = take(parts[0], q * span, mine ^ apart, columns)
                for other in parts[1:]:
                    total = total + take(other, q * span, mine ^ apart, columns)
                start = 0
                for piece in pieces:
                    piece[q] = total[start : start + piece.shape[1]].astype(piece.dtype)
                    start += piece.shape[1]


def last_kernel(early_parts, flags, *refs):
    ins, (sent, kept) = list(refs[:-2]), refs[-2:]
    first = flags[DP] == 0
    sums = []
    for sizes in (early_parts, (1,) * (len(ins) - sum(early_parts))):
        total = 0.0
        for size in sizes:
            rows = [piece[0].astype(F32) for piece in ins[:size]]
            total = total + (jnp.concatenate(rows, axis=0) if size > 1 else rows[0])
            del ins[:size]
        sums.append(total)
    wide = jnp.concatenate([sums[1], sums[1]], axis=1)
    sent[...] = jnp.where(first, sums[0], wide).astype(BF16)
    kept[...] = jnp.where(first, wide, sums[0])


def join_kernel(scale, flags, kept, came, out):
    half = kept.shape[1] // 2
    first = flags[DP] == 0
    mine, other = kept[...], came[...].astype(F32)
    beside = jnp.concatenate([mine[:, :half], other[:, :half]], axis=1)
    out[...] = jnp.where(first, beside, mine + other) * scale


def vmem_call(kernel, out_shape, operands, scratch=(), scalars=1, flops=0, limit=16, after=(), aliases=()):
    whole = pl.BlockSpec(memory_space=pltpu.VMEM)
    specs = [pl.BlockSpec(memory_space=pltpu.SMEM)] * scalars + [whole] * (len(operands) - scalars)
    specs += [pl.BlockSpec(memory_space=pl.ANY)] * len(after)
    count = len(operands)

    def run(*refs):
        kernel(*refs[:count], *refs[count + len(after) :])

    moved = sum(a.size * a.dtype.itemsize for a in operands)
    moved += sum(math.prod(s.shape) * s.dtype.itemsize for s in jax.tree.leaves(out_shape))
    return pl.pallas_call(
        run,
        out_shape=out_shape,
        in_specs=specs,
        out_specs=jax.tree.map(lambda _: whole, out_shape),
        scratch_shapes=list(scratch),
        input_output_aliases=dict(aliases),
        compiler_params=pltpu.CompilerParams(vmem_limit_bytes=limit << 20),
        cost_estimate=pl.CostEstimate(flops=flops, bytes_accessed=moved, transcendentals=0),
    )(*operands, *after)


def sds(*shape, dtype=BF16):
    return jax.ShapeDtypeStruct(shape, dtype)


def xor_move(block, apart, across):
    tiles = lax.axis_size("tile")
    if not across:
        return lax.ppermute(block, "tile", [(t, t ^ apart) for t in range(tiles)])
    if not apart:
        return lax.ppermute(block, "dp", [(0, 1), (1, 0)])
    route = [(d * tiles + t, (1 - d) * tiles + (t ^ apart)) for d in range(2) for t in range(tiles)]
    return lax.ppermute(block, ("dp", "tile"), route)


def core_sum(dealt, core, pieces, turned):
    if len(dealt) == 1:
        tiles = lax.axis_size("tile")
        rows, channels = dealt[0].shape[0] // tiles, dealt[0].shape[1]
        pairs = dealt[0].reshape(tiles // 2, 2, rows, channels)
        if turned:
            pairs = pairs.reshape(tiles // 4, 2, 2, rows, channels).swapaxes(0, 1).reshape(pairs.shape)
        kept = lax.dynamic_index_in_dim(pairs, core, 1, keepdims=False)
        sent = lax.dynamic_index_in_dim(pairs, 1 - core, 1, keepdims=False)
        size = sent.shape[0] // pieces
        sent = [sent[n * size : (n + 1) * size] for n in range(pieces)]
    else:
        kept, *sent = dealt
    return [[kept], [xor_move(piece, 1, False) for piece in sent]]


def deal_rounds(jobs, flags, after=()):
    outs, plans, operands = [], [], [flags]
    for parts, at, bits, by_columns, cut in jobs:
        span = 1 << bits
        count, rows, channels = parts[0][0].shape
        channels = channels // 2 if by_columns else channels
        tiles = rows // 16
        heights = [rows]
        if rows % 16 == 0 and cut > 1:
            heights = [16 * (tiles * (n + 1) // cut - tiles * n // cut) for n in range(cut)]
        for n in range(span * (2 if by_columns else 1)):
            if n == 0:
                outs.append(sds(count // span, rows, channels, dtype=F32))
            else:
                outs += [sds(count // span, height, channels) for height in heights]
        plans.append((tuple(len(part) for part in parts), at, bits, by_columns, tuple(heights)))
        operands += [piece for part in parts for piece in part]
    pieces = list(vmem_call(functools.partial(round_kernel, plans), outs, operands, after=after))
    token, sums = pieces[0], []
    for _, at, bits, by_columns, heights in plans:
        span = 1 << bits
        parts = [[pieces.pop(0)]]
        for n in range(1, span * (2 if by_columns else 1)):
            parts.append([xor_move(pieces.pop(0), (n % span) << at, n >= span) for _ in heights])
        sums.append(parts)
    return sums, token


def per_device(features, proj_weight, conv_weight, saved, cotangent):
    position = lax.axis_index("tile")
    tile_count = lax.axis_size("tile")
    rows = tile_count // TILE_COLS
    gray = position % TILE_COLS
    col, row = column_of(gray), position // TILE_COLS
    images, height2, width2, channels = cotangent.shape
    depths, dim = proj_weight.shape[:2]
    height, width = height2 // 2, width2 // 2
    patches = images * height * width
    line = images * width
    tokens = features.shape[2]
    has_second = rows > 2
    sides = 2 if has_second else 1
    bits = tile_count.bit_length() - 1
    flags = jnp.stack(
        [row % 2, col % 2, row == 0, row == rows - 1, col == 0, col == TILE_COLS - 1]
        + [position % 2, lax.axis_index("dp"), gray]
        + [position >> b & 1 for b in range(bits)]
    ).astype(jnp.int32)

    def swap(block, row_pairs, col_pairs):
        return lax.ppermute(block, "tile", tile_route(row_pairs, col_pairs, rows))

    low, high = cotangent[:, :, :HALO], cotangent[:, :, width2 - HALO :]
    around = paired(TILE_COLS, 1) + [(0, TILE_COLS - 1), (TILE_COLS - 1, 0)]
    col_b = swap(jnp.where(col % 2 == 1, high, low), None, around)
    col_a = swap(jnp.where(col % 2 == 1, low, high), None, paired(TILE_COLS, 0))
    centre = vmem_call(
        centre_kernel,
        sds(images, height2, width + 8, channels, dtype=F32),
        (cotangent,),
        scratch=(pltpu.VMEM((channels // 128, height2, LEFT + width2 + 8, 128), F32),),
        scalars=0,
    )
    *row_out, cells, beside = vmem_call(
        functools.partial(row_pack_kernel, has_second),
        [sds(2 * images * (width + 2), channels)] * sides
        + [sds(images, 6, width, channels, dtype=F32), sds(images, 6, 2, channels, dtype=F32)],
        (flags, centre, col_a, col_b),
        scratch=(pltpu.VMEM((sides, 4 * images, channels), F32),),
    )
    came_rows = [swap(row_out[n], paired(rows, n), None) for n in range(sides)]
    conv_flops = 2 * patches * depths * 9 * channels * channels
    window, acc = vmem_call(
        main_kernel,
        [sds(3, (height + 2) * line, channels), sds(depths, patches, channels, dtype=F32)],
        (flags, centre, col_a, col_b, conv_weight),
        scratch=(pltpu.VMEM((height, LEFT + width + 8, channels), F32),),
        flops=conv_flops,
        after=(row_out[0],),
    )
    *grads, window = vmem_call(
        functools.partial(edge_kernel, has_second),
        [sds(2, depths, line, channels)] * CHIPS + [sds(3, (height + 2) * line, channels)],
        [flags] + came_rows + [cells, beside, window, acc, conv_weight],
        scratch=(
            pltpu.VMEM((4, LEFT + width + 8, channels), F32),
            pltpu.VMEM((sides, 4 * images, channels), F32),
            pltpu.VMEM((patches, channels), F32),
        ),
        flops=conv_flops // 4,
        aliases={sides + 3: CHIPS},
    )
    came = [grads[0]] + [xor_move(grads[chip], 2 * chip, False) for chip in range(1, CHIPS)]
    to_pass = vmem_call(pass_on_kernel, sds(CHIPS, depths, line, channels), came, scalars=0)
    passed = xor_move(to_pass, 1, False)

    half_rows = depths * (dim + 9 * channels) // 2
    conv_late = half_rows - depths * dim
    block_rows = half_rows // tile_count
    pieces = 4
    if block_rows % 16:
        dealt = [sds(half_rows, channels)]
    else:
        dealt = [sds(tile_count // 2, block_rows, channels)]
        dealt += [sds(tile_count // 2 // pieces, block_rows, channels)] * pieces
    full = pltpu.VMEM((half_rows, channels), BF16)
    *early, conv_top = vmem_call(
        conv_term_kernel,
        dealt + [sds(conv_late, channels)],
        (flags, window, saved),
        scratch=(full, pltpu.VMEM((patches, channels), BF16)),
        flops=conv_flops,
    )
    (early_parts,), before = deal_rounds([(core_sum(early, position % 2, pieces, True), 2, 1, False, 1)], flags)
    proj_flops = 2 * images * tokens * depths * dim * channels
    *terms, token_grad = vmem_call(
        proj_term_kernel,
        dealt + [sds(depths, images * tokens, channels)],
        [flags] + came + [passed, features, conv_top],
        scratch=(full,),
        flops=proj_flops,
        after=(before,),
    )
    (late_parts,), before = deal_rounds(
        [(core_sum(terms, position % 2, pieces, False), 1, 1, True, 1)], flags, after=(token_grad,)
    )
    at, early_bits = 2, list(range(3, bits)) + [1]
    while at < bits:
        step = min(2, bits - at)
        if len(early_bits) > 1:
            (early_parts,), before = deal_rounds([(early_parts, early_bits.pop(0), 1, False, 1)], flags, after=(before,))
        (late_parts,), before = deal_rounds([(late_parts, at, step, False, 1)], flags, after=(before,))
        at += step
    while early_bits:
        bit = early_bits.pop(0)
        (early_parts,), before = deal_rounds(
            [(early_parts, bit, 1, False, 3 if bit == 1 else 1)], flags, after=(before,)
        )
    feature_grad = vmem_call(
        feat_grad_kernel,
        sds(images, depths, tokens, dim),
        (token_grad, proj_weight),
        scalars=0,
        flops=proj_flops,
        after=(before,),
    )
    sent, kept = vmem_call(
        functools.partial(last_kernel, tuple(len(part) for part in early_parts)),
        [sds(block_rows, channels), sds(block_rows, channels, dtype=F32)],
        [flags] + [piece for part in early_parts + late_parts for piece in part],
    )
    other = xor_move(sent, 0, True)
    scale = 1.0 / math.sqrt(images * lax.axis_size("dp") * tokens * tile_count)
    head_grad = vmem_call(
        functools.partial(join_kernel, scale), sds(block_rows, channels, dtype=F32), (flags, kept, other)
    )
    return feature_grad, head_grad


def solution(mesh):
    in_specs = (
        P("dp", None, "tile", None),
        P(),
        P(),
        P("dp", None, "tile", None, None),
        P("dp", "tile", None, None),
    )
    out_specs = (P("dp", None, "tile", None), P(("dp", "tile"), None))
    return jax.shard_map(
        per_device, mesh=mesh, in_specs=in_specs, out_specs=out_specs, check_vma=False
    )
```

```python
import functools
import math

import jax
import jax.numpy as jnp
from jax import lax
from jax.experimental import pallas as pl
from jax.experimental.pallas import tpu as pltpu
from jax.sharding import PartitionSpec as P

TILE_COLS = 8
HALO = 4
LEFT = 8
BF16 = jnp.bfloat16
F32 = jnp.float32
ROW_ODD, COL_ODD, TOP, BOTTOM, LEFT_END, RIGHT_END, CORE, DP, GRAY, BITS = range(10)
CHIPS = TILE_COLS // 2


def gray_of(column):
    return column ^ column >> 1


def column_of(code):
    return code ^ code >> 1 ^ code >> 2


def paired(count, first):
    pairs = []
    for low in range(first, count - 1, 2):
        pairs += [(low, low + 1), (low + 1, low)]
    return pairs


def tile_route(row_pairs, col_pairs, rows):
    row_moves = row_pairs if row_pairs is not None else [(r, r) for r in range(rows)]
    col_moves = col_pairs if col_pairs is not None else [(c, c) for c in range(TILE_COLS)]
    return [
        (r0 * TILE_COLS + gray_of(c0), r1 * TILE_COLS + gray_of(c1))
        for r0, r1 in row_moves
        for c0, c1 in col_moves
    ]


def nt_dot(left, right):
    return lax.dot_general(left, right, (((1,), (1,)), ((), ())), preferred_element_type=F32)


def centre_kernel(cot, pooled, wide):
    images, height2, width2, channels = cot.shape
    width = width2 // 2
    wide[...] = jnp.zeros_like(wide)

    def per_image(i, carry):
        for r in range(height2):
            value = cot[i, r].astype(F32)
            for h in range(channels // 128):
                wide[h, r, LEFT : LEFT + width2, :] = value[:, h * 128 : (h + 1) * 128]
            pooled[i, r, width : width + 1, :] = value[:1]
            pooled[i, r, width + 1 : width + 2, :] = value[width2 - 1 :]
        for r in range(height2):
            for h in range(channels // 128):
                taps = [wide[h, r, pl.ds(LEFT - 1 + n, width, stride=2), :] for n in range(4)]
                pooled[i, r, :width, h * 128 : (h + 1) * 128] = 0.75 * (taps[1] + taps[2]) + 0.25 * (taps[0] + taps[3])
        return carry

    lax.fori_loop(0, images, per_image, 0)


def pool_columns(flags, centre, col_a, col_b, i, lines):
    width, channels = centre.shape[2] - 8, centre.shape[3]
    col_odd, left, right = flags[COL_ODD] == 1, flags[LEFT_END] == 1, flags[RIGHT_END] == 1
    cell = lax.broadcasted_iota(jnp.int32, (width, channels), 0)
    is_first, is_last = cell == 0, cell == width - 1
    cells, beside = [], []
    for r in lines:
        own_first, own_last = centre[i, r, width : width + 1, :], centre[i, r, width + 1 : width + 2, :]
        one, two = col_a[i, r].astype(F32), col_b[i, r].astype(F32)
        before, after = jnp.where(col_odd, one, two), jnp.where(col_odd, two, one)
        near_before = jnp.where(left, own_first, before[3:4])
        near_after = jnp.where(right, own_last, after[0:1])
        cells.append(
            centre[i, r, :width, :] + 0.25 * (jnp.where(is_first, near_before, 0.0) + jnp.where(is_last, near_after, 0.0))
        )
        first = 0.75 * (before[2:3] + before[3:4]) + 0.25 * (before[1:2] + own_first)
        last = 0.75 * (after[0:1] + after[1:2]) + 0.25 * (own_last + after[2:3])
        beside.append(
            jnp.concatenate([jnp.where(left, 0.0, first), jnp.where(right, 0.0, last)], axis=0)
        )
    return cells, beside


def place(cells, beside, pooled, window, at):
    width = cells.shape[0]
    pooled[LEFT : LEFT + width, :] = cells
    pooled[LEFT - 1 : LEFT, :] = beside[:1]
    pooled[LEFT + width : LEFT + width + 1, :] = beside[1:]
    for v in range(3):
        window[v, pl.ds(at, width), :] = pooled[pl.ds(LEFT + 1 - v, width), :].astype(BF16)


def row_pack_kernel(has_second, flags, centre, col_a, col_b, *refs):
    outs, (cells_out, beside_out, ends) = refs[: 2 if has_second else 1], refs[-3:]
    images, height2, width = centre.shape[0], centre.shape[1], centre.shape[2] - 8
    row_odd = flags[ROW_ODD] == 1
    lines = [0, 1, 2, height2 - 3, height2 - 2, height2 - 1]
    for i in range(images):
        cells, beside = pool_columns(flags, centre, col_a, col_b, i, lines)
        for n in range(6):
            cells_out[i, n] = cells[n]
            beside_out[i, n] = beside[n]
        for group, is_end in ((cells, False), (beside, True)):
            above = [group[0], 0.75 * (group[0] + group[1]) + 0.25 * group[2]]
            below = [0.25 * group[3] + 0.75 * (group[4] + group[5]), group[5]]
            for second in range(len(outs)):
                for n in range(2):
                    odd, even = (below[n], above[n]) if second else (above[n], below[n])
                    value = jnp.where(row_odd, odd, even)
                    if is_end:
                        ends[second, (2 * i + n) * 2 : (2 * i + n) * 2 + 2, :] = value
                    else:
                        at = (2 * i + n) * width
                        outs[second][at : at + width, :] = value.astype(BF16)
    for second in range(len(outs)):
        outs[second][2 * images * width :, :] = ends[second].astype(BF16)


def main_kernel(flags, centre, col_a, col_b, weight, window, acc, pooled):
    images, height2, width, channels = centre.shape[0], centre.shape[1], centre.shape[2] - 8, centre.shape[3]
    height, depths = height2 // 2, weight.shape[0]
    pooled[...] = jnp.zeros_like(pooled)

    def per_image(i, carry):
        cells, beside = pool_columns(flags, centre, col_a, col_b, i, range(1, height2 - 1))
        for p in range(1, height - 1):
            at = 2 * p - 2
            both = [
                0.75 * (group[at + 1] + group[at + 2]) + 0.25 * (group[at] + group[at + 3])
                for group in (cells, beside)
            ]
            where = pl.multiple_of((p + 1) * images * width + i * width, width)
            place(both[0], both[1], pooled.at[p], window, where)
        return carry

    lax.fori_loop(0, images, per_image, 0)
    line = images * width
    inner = (height - 2) * line
    rows = slice(2 * line, 2 * line + inner)
    for k in range(depths):
        for u in range(3):
            part = nt_dot(window[0, rows, :], weight[k, u, 0])
            part = part + nt_dot(window[1, rows, :], weight[k, u, 1])
            part = part + nt_dot(window[2, rows, :], weight[k, u, 2])
            if u == 0:
                acc[k, :inner, :] = part
                acc[k, inner:, :] = jnp.zeros((2 * line, channels), F32)
            else:
                acc[k, u * line : u * line + inner, :] += part


def edge_kernel(has_second, flags, *refs):
    sides = 2 if has_second else 1
    rows, (cells, beside, _, acc, weight) = refs[:sides], refs[sides : sides + 5]
    *grads, window, pooled, ends, total = refs[sides + 5 :]
    images, width = cells.shape[0], cells.shape[2]
    depths, count = acc.shape[:2]
    line = images * width
    height = count // line
    row_odd, top, bottom = flags[ROW_ODD] == 1, flags[TOP] == 1, flags[BOTTOM] == 1
    for n in range(sides):
        ends[n] = rows[n][2 * line :, :].astype(F32)
    pooled[...] = jnp.zeros_like(pooled)
    for i in range(images):
        for_rows = []
        for is_end, own in ((False, cells), (True, beside)):
            def came(from_above, n):
                def of(ref_at):
                    if is_end:
                        at = (2 * i + n) * 2
                        return ends[ref_at, at : at + 2, :]
                    at = (2 * i + n) * width
                    return rows[ref_at][at : at + width, :].astype(F32)

                first = of(0)
                second = of(1) if has_second else jnp.zeros_like(first)
                return jnp.where(row_odd, first, second) if from_above else jnp.where(row_odd, second, first)

            edge = [own[i, n] for n in range(6)]
            zero = jnp.zeros_like(edge[0])
            for_rows.append(
                [
                    jnp.where(top, zero, came(True, 0) + 0.25 * edge[0]),
                    0.75 * (edge[0] + edge[1]) + 0.25 * (jnp.where(top, edge[0], came(True, 1)) + edge[2]),
                    0.75 * (edge[4] + edge[5]) + 0.25 * (jnp.where(bottom, edge[5], came(False, 0)) + edge[3]),
                    jnp.where(bottom, zero, came(False, 1) + 0.25 * edge[5]),
                ]
            )
        for n, p in enumerate((0, 1, height, height + 1)):
            place(for_rows[0][n], for_rows[1][n], pooled.at[n], window, p * line + i * width)
    low, high = slice(0, 2 * line), slice(height * line, (height + 2) * line)
    for k in range(depths):
        total[...] = acc[k]
        for v in range(3):
            total[(height - 2) * line :, :] += nt_dot(window[v, high, :], weight[k, 0, v])
            total[: 2 * line, :] += nt_dot(window[v, low, :], weight[k, 2, v])
            middle = jnp.concatenate(
                [window[v, line : 2 * line, :], window[v, height * line : (height + 1) * line, :]], axis=0
            )
            part = nt_dot(middle, weight[k, 1, v])
            total[:line, :] += part[:line]
            total[(height - 1) * line :, :] += part[line:]
        for apart in range(2 * CHIPS):
            at = pl.multiple_of((flags[GRAY] ^ apart) * line, line)
            grads[apart // 2][apart % 2, k] = total[pl.ds(at, line), :].astype(BF16)


def deal(full, split_refs, core, turned):
    if len(split_refs) == 1:
        split_refs[0][...] = full[...]
        return
    kept, *sent = split_refs
    count, rows = kept.shape[:2]
    size = sent[0].shape[0]
    for j in range(count):
        p = (j & ~3 | (j & 1) << 1 | j >> 1 & 1) if turned else j
        kept[p] = full[pl.ds(pl.multiple_of((2 * j + core) * rows, 16), rows), :]
        sent[p // size][p % size] = full[pl.ds(pl.multiple_of((2 * j + 1 - core) * rows, 16), rows), :]


def conv_term_kernel(flags, window, saved, *refs):
    split_refs, top, full, flat = refs[:-3], refs[-3], refs[-2], refs[-1]
    images, depths, height, width, channels = saved.shape
    line = images * width
    count = height * line
    split = top.shape[0]
    for k in range(depths):
        for h in range(height):
            for i in range(images):
                at = (h * images + i) * width
                flat[at : at + width, :] = saved[i, k, h]
        flat_t = flat[...].T
        for n in range(9):
            start = (2 - n // 3) * line
            part = jnp.dot(
                flat_t, window[n % 3, start : start + count, :], preferred_element_type=F32
            ).astype(BF16)
            at = (k * 9 + n) * channels
            if at < split:
                top[at : at + channels, :] = part
            else:
                full[at - split : at - split + channels, :] = part
    deal(full, split_refs, flags[CORE], True)


def pass_on_kernel(*refs):
    for n, piece in enumerate(refs[:-1]):
        refs[-1][n] = piece[1]


def proj_term_kernel(flags, *refs):
    came, (passed, feats, conv_top) = refs[:CHIPS], refs[CHIPS : CHIPS + 3]
    split_refs, tokens, full = refs[CHIPS + 3 : -2], refs[-2], refs[-1]
    images, depths, _, dim = feats.shape
    line = passed.shape[2]
    width = line // images
    for apart in range(2 * CHIPS):
        column = column_of(flags[GRAY] ^ apart)
        for k in range(depths):
            for i in range(images):
                at = pl.multiple_of((i * TILE_COLS + column) * width, width)
                rows = slice(i * width, (i + 1) * width)
                piece = passed[apart // 2, k, rows, :] if apart % 2 else came[apart // 2][0, k, rows, :]
                tokens[k, pl.ds(at, width), :] = piece
    for k in range(depths):
        flat = feats[:, k].reshape(tokens.shape[1], dim)
        part = lax.dot_general(
            flat, tokens[k], (((0,), (0,)), ((), ())), preferred_element_type=F32
        )
        full[k * dim : (k + 1) * dim, :] = part.astype(BF16)
    full[depths * dim :, :] = conv_top[...]
    deal(full, split_refs, flags[CORE], False)


def feat_grad_kernel(tokens, weight, out):
    images, depths, count, dim = out.shape
    for k in range(depths):
        out[:, k] = nt_dot(tokens[k], weight[k]).astype(BF16).reshape(images, count, dim)


def take(part, block, at, columns=None):
    size = part[0].shape[0]
    return part[block // size][block % size + at, :, slice(None) if columns is None else columns].astype(F32)


def round_kernel(jobs, flags, *refs):
    ins, outs, dp = list(refs[: sum(sum(job[0]) for job in jobs)]), refs, flags[DP]
    outs = list(refs[len(ins) :])
    for sizes, at, bits, by_columns, heights in jobs:
        parts = []
        for size in sizes:
            parts.append(ins[:size])
            del ins[:size]
        span = 1 << bits
        mine = 0
        for b in range(bits):
            mine = mine + flags[BITS + at + b] * (1 << b)
        for n in range(span * (2 if by_columns else 1)):
            across, apart = n // span, n % span
            pieces = outs[: len(heights) if n else 1]
            del outs[: len(pieces)]
            count, _, width = pieces[0].shape
            columns = None
            if by_columns:
                columns = pl.ds(pl.multiple_of((dp ^ across) * width, width), width)
            for q in range(count):
                total = take(parts[0], q * span, mine ^ apart, columns)
                for other in parts[1:]:
                    total = total + take(other, q * span, mine ^ apart, columns)
                start = 0
                for piece in pieces:
                    piece[q] = total[start : start + piece.shape[1]].astype(piece.dtype)
                    start += piece.shape[1]


def last_kernel(early_parts, flags, *refs):
    ins, (sent, kept) = list(refs[:-2]), refs[-2:]
    first = flags[DP] == 0
    sums = []
    for sizes in (early_parts, (1,) * (len(ins) - sum(early_parts))):
        total = 0.0
        for size in sizes:
            rows = [piece[0].astype(F32) for piece in ins[:size]]
            total = total + (jnp.concatenate(rows, axis=0) if size > 1 else rows[0])
            del ins[:size]
        sums.append(total)
    sent[...] = jnp.where(first, sums[0], sums[1]).astype(BF16)
    kept[...] = jnp.where(first, sums[1], sums[0])


def join_kernel(scale, flags, kept, came, out):
    width = kept.shape[1]
    at = pl.multiple_of(flags[DP] * width, width)
    out[:, pl.ds(at, width)] = kept[...] * scale
    at = pl.multiple_of((1 - flags[DP]) * width, width)
    out[:, pl.ds(at, width)] = came[...].astype(F32) * scale


def vmem_call(kernel, out_shape, operands, scratch=(), scalars=1, flops=0, limit=16, after=(), aliases=()):
    whole = pl.BlockSpec(memory_space=pltpu.VMEM)
    specs = [pl.BlockSpec(memory_space=pltpu.SMEM)] * scalars + [whole] * (len(operands) - scalars)
    specs += [pl.BlockSpec(memory_space=pl.ANY)] * len(after)
    count = len(operands)

    def run(*refs):
        kernel(*refs[:count], *refs[count + len(after) :])

    moved = sum(a.size * a.dtype.itemsize for a in operands)
    moved += sum(math.prod(s.shape) * s.dtype.itemsize for s in jax.tree.leaves(out_shape))
    return pl.pallas_call(
        run,
        out_shape=out_shape,
        in_specs=specs,
        out_specs=jax.tree.map(lambda _: whole, out_shape),
        scratch_shapes=list(scratch),
        input_output_aliases=dict(aliases),
        compiler_params=pltpu.CompilerParams(vmem_limit_bytes=limit << 20),
        cost_estimate=pl.CostEstimate(flops=flops, bytes_accessed=moved, transcendentals=0),
    )(*operands, *after)


def sds(*shape, dtype=BF16):
    return jax.ShapeDtypeStruct(shape, dtype)


def xor_move(block, apart, across):
    tiles = lax.axis_size("tile")
    if not across:
        return lax.ppermute(block, "tile", [(t, t ^ apart) for t in range(tiles)])
    if not apart:
        return lax.ppermute(block, "dp", [(0, 1), (1, 0)])
    route = [(d * tiles + t, (1 - d) * tiles + (t ^ apart)) for d in range(2) for t in range(tiles)]
    return lax.ppermute(block, ("dp", "tile"), route)


def core_sum(dealt, core, pieces, turned):
    if len(dealt) == 1:
        tiles = lax.axis_size("tile")
        rows, channels = dealt[0].shape[0] // tiles, dealt[0].shape[1]
        pairs = dealt[0].reshape(tiles // 2, 2, rows, channels)
        if turned:
            pairs = pairs.reshape(tiles // 8, 2, 2, 2, rows, channels).swapaxes(1, 2).reshape(pairs.shape)
        kept = lax.dynamic_index_in_dim(pairs, core, 1, keepdims=False)
        sent = lax.dynamic_index_in_dim(pairs, 1 - core, 1, keepdims=False)
        size = sent.shape[0] // pieces
        sent = [sent[n * size : (n + 1) * size] for n in range(pieces)]
    else:
        kept, *sent = dealt
    return [[kept], [xor_move(piece, 1, False) for piece in sent]]


def deal_rounds(jobs, flags, after=()):
    outs, plans, operands = [], [], [flags]
    for parts, at, bits, by_columns, cut in jobs:
        span = 1 << bits
        count, rows, channels = parts[0][0].shape
        channels = channels // 2 if by_columns else channels
        tiles = rows // 16
        heights = [rows]
        if rows % 16 == 0 and cut > 1:
            heights = [16 * (tiles * (n + 1) // cut - tiles * n // cut) for n in range(cut)]
        for n in range(span * (2 if by_columns else 1)):
            if n == 0:
                outs.append(sds(count // span, rows, channels, dtype=F32))
            else:
                outs += [sds(count // span, height, channels) for height in heights]
        plans.append((tuple(len(part) for part in parts), at, bits, by_columns, tuple(heights)))
        operands += [piece for part in parts for piece in part]
    pieces = list(vmem_call(functools.partial(round_kernel, plans), outs, operands, after=after))
    token, sums = pieces[0], []
    for _, at, bits, by_columns, heights in plans:
        span = 1 << bits
        parts = [[pieces.pop(0)]]
        for n in range(1, span * (2 if by_columns else 1)):
            parts.append([xor_move(pieces.pop(0), (n % span) << at, n >= span) for _ in heights])
        sums.append(parts)
    return sums, token


def per_device(features, proj_weight, conv_weight, saved, cotangent):
    position = lax.axis_index("tile")
    tile_count = lax.axis_size("tile")
    rows = tile_count // TILE_COLS
    gray = position % TILE_COLS
    col, row = column_of(gray), position // TILE_COLS
    images, height2, width2, channels = cotangent.shape
    depths, dim = proj_weight.shape[:2]
    height, width = height2 // 2, width2 // 2
    patches = images * height * width
    line = images * width
    tokens = features.shape[2]
    has_second = rows > 2
    sides = 2 if has_second else 1
    bits = tile_count.bit_length() - 1
    flags = jnp.stack(
        [row % 2, col % 2, row == 0, row == rows - 1, col == 0, col == TILE_COLS - 1]
        + [position % 2, lax.axis_index("dp"), gray]
        + [position >> b & 1 for b in range(bits)]
    ).astype(jnp.int32)

    def swap(block, row_pairs, col_pairs):
        return lax.ppermute(block, "tile", tile_route(row_pairs, col_pairs, rows))

    low, high = cotangent[:, :, :HALO], cotangent[:, :, width2 - HALO :]
    around = paired(TILE_COLS, 1) + [(0, TILE_COLS - 1), (TILE_COLS - 1, 0)]
    col_b = swap(jnp.where(col % 2 == 1, high, low), None, around)
    col_a = swap(jnp.where(col % 2 == 1, low, high), None, paired(TILE_COLS, 0))
    centre = vmem_call(
        centre_kernel,
        sds(images, height2, width + 8, channels, dtype=F32),
        (cotangent,),
        scratch=(pltpu.VMEM((channels // 128, height2, LEFT + width2 + 8, 128), F32),),
        scalars=0,
    )
    *row_out, cells, beside = vmem_call(
        functools.partial(row_pack_kernel, has_second),
        [sds(2 * images * (width + 2), channels)] * sides
        + [sds(images, 6, width, channels, dtype=F32), sds(images, 6, 2, channels, dtype=F32)],
        (flags, centre, col_a, col_b),
        scratch=(pltpu.VMEM((sides, 4 * images, channels), F32),),
    )
    came_rows = [swap(row_out[n], paired(rows, n), None) for n in range(sides)]
    conv_flops = 2 * patches * depths * 9 * channels * channels
    window, acc = vmem_call(
        main_kernel,
        [sds(3, (height + 2) * line, channels), sds(depths, patches, channels, dtype=F32)],
        (flags, centre, col_a, col_b, conv_weight),
        scratch=(pltpu.VMEM((height, LEFT + width + 8, channels), F32),),
        flops=conv_flops,
        after=(row_out[0],),
    )
    *grads, window = vmem_call(
        functools.partial(edge_kernel, has_second),
        [sds(2, depths, line, channels)] * CHIPS + [sds(3, (height + 2) * line, channels)],
        [flags] + came_rows + [cells, beside, window, acc, conv_weight],
        scratch=(
            pltpu.VMEM((4, LEFT + width + 8, channels), F32),
            pltpu.VMEM((sides, 4 * images, channels), F32),
            pltpu.VMEM((patches, channels), F32),
        ),
        flops=conv_flops // 4,
        aliases={sides + 3: CHIPS},
    )
    came = [grads[0]] + [xor_move(grads[chip], 2 * chip, False) for chip in range(1, CHIPS)]
    to_pass = vmem_call(pass_on_kernel, sds(CHIPS, depths, line, channels), came, scalars=0)
    passed = xor_move(to_pass, 1, False)

    half_rows = depths * (dim + 9 * channels) // 2
    conv_late = half_rows - depths * dim
    block_rows = half_rows // tile_count
    pieces = 4
    if block_rows % 16:
        dealt = [sds(half_rows, channels)]
    else:
        dealt = [sds(tile_count // 2, block_rows, channels)]
        dealt += [sds(tile_count // 2 // pieces, block_rows, channels)] * pieces
    full = pltpu.VMEM((half_rows, channels), BF16)
    *early, conv_top = vmem_call(
        conv_term_kernel,
        dealt + [sds(conv_late, channels)],
        (flags, window, saved),
        scratch=(full, pltpu.VMEM((patches, channels), BF16)),
        flops=conv_flops,
    )
    (early_parts,), before = deal_rounds([(core_sum(early, position % 2, pieces, True), 1, 0, True, 1)], flags)
    proj_flops = 2 * images * tokens * depths * dim * channels
    *terms, token_grad = vmem_call(
        proj_term_kernel,
        dealt + [sds(depths, images * tokens, channels)],
        [flags] + came + [passed, features, conv_top],
        scratch=(full,),
        flops=proj_flops,
        after=(before,),
    )
    (late_parts,), before = deal_rounds(
        [(core_sum(terms, position % 2, pieces, False), 1, 1, True, 1)], flags, after=(token_grad,)
    )
    at, early_bits = 2, [2, 1] + list(range(3, bits))
    while at < bits:
        step = min(2, bits - at)
        (early_parts,), before = deal_rounds([(early_parts, early_bits.pop(0), 1, False, 1)], flags, after=(before,))
        (late_parts, early_parts), before = deal_rounds(
            [(late_parts, at, step, False, 1), (early_parts, early_bits.pop(0), 1, False, 1)], flags, after=(before,)
        )
        at += step
    while early_bits:
        (early_parts,), before = deal_rounds([(early_parts, early_bits.pop(0), 1, False, 1)], flags, after=(before,))
    feature_grad = vmem_call(
        feat_grad_kernel,
        sds(images, depths, tokens, dim),
        (token_grad, proj_weight),
        scalars=0,
        flops=proj_flops,
        after=(before,),
    )
    sent, kept = vmem_call(
        functools.partial(last_kernel, tuple(len(part) for part in early_parts)),
        [sds(block_rows, channels // 2), sds(block_rows, channels // 2, dtype=F32)],
        [flags] + [piece for part in early_parts + late_parts for piece in part],
    )
    other = xor_move(sent, 0, True)
    scale = 1.0 / math.sqrt(images * lax.axis_size("dp") * tokens * tile_count)
    head_grad = vmem_call(
        functools.partial(join_kernel, scale), sds(block_rows, channels, dtype=F32), (flags, kept, other)
    )
    return feature_grad, head_grad


def solution(mesh):
    in_specs = (
        P("dp", None, "tile", None),
        P(),
        P(),
        P("dp", None, "tile", None, None),
        P("dp", "tile", None, None),
    )
    out_specs = (P("dp", None, "tile", None), P(("dp", "tile"), None))
    return jax.shard_map(
        per_device, mesh=mesh, in_specs=in_specs, out_specs=out_specs, check_vma=False
    )
```

```python
import functools
import math

import jax
import jax.numpy as jnp
from jax import lax
from jax.experimental import pallas as pl
from jax.experimental.pallas import tpu as pltpu
from jax.sharding import PartitionSpec as P

TILE_COLS = 8
HALO = 4
LEFT = 8
BF16 = jnp.bfloat16
F32 = jnp.float32
ROW_ODD, COL_ODD, TOP, BOTTOM, LEFT_END, RIGHT_END, CORE, DP, GRAY, BITS = range(10)
CHIPS = TILE_COLS // 2


def gray_of(column):
    return column ^ column >> 1


def column_of(code):
    return code ^ code >> 1 ^ code >> 2


def paired(count, first):
    pairs = []
    for low in range(first, count - 1, 2):
        pairs += [(low, low + 1), (low + 1, low)]
    return pairs


def tile_route(row_pairs, col_pairs, rows):
    row_moves = row_pairs if row_pairs is not None else [(r, r) for r in range(rows)]
    col_moves = col_pairs if col_pairs is not None else [(c, c) for c in range(TILE_COLS)]
    return [
        (r0 * TILE_COLS + gray_of(c0), r1 * TILE_COLS + gray_of(c1))
        for r0, r1 in row_moves
        for c0, c1 in col_moves
    ]


def nt_dot(left, right):
    return lax.dot_general(left, right, (((1,), (1,)), ((), ())), preferred_element_type=F32)


def centre_kernel(cot, pooled, wide):
    images, height2, width2, channels = cot.shape
    width = width2 // 2
    wide[...] = jnp.zeros_like(wide)

    def per_image(i, carry):
        for r in range(height2):
            value = cot[i, r].astype(F32)
            for h in range(channels // 128):
                wide[h, r, LEFT : LEFT + width2, :] = value[:, h * 128 : (h + 1) * 128]
            pooled[i, r, width : width + 1, :] = value[:1]
            pooled[i, r, width + 1 : width + 2, :] = value[width2 - 1 :]
        for r in range(height2):
            for h in range(channels // 128):
                taps = [wide[h, r, pl.ds(LEFT - 1 + n, width, stride=2), :] for n in range(4)]
                pooled[i, r, :width, h * 128 : (h + 1) * 128] = 0.75 * (taps[1] + taps[2]) + 0.25 * (taps[0] + taps[3])
        return carry

    lax.fori_loop(0, images, per_image, 0)


def pool_columns(flags, centre, col_a, col_b, i, lines):
    width, channels = centre.shape[2] - 8, centre.shape[3]
    col_odd, left, right = flags[COL_ODD] == 1, flags[LEFT_END] == 1, flags[RIGHT_END] == 1
    cell = lax.broadcasted_iota(jnp.int32, (width, channels), 0)
    is_first, is_last = cell == 0, cell == width - 1
    cells, beside = [], []
    for r in lines:
        own_first, own_last = centre[i, r, width : width + 1, :], centre[i, r, width + 1 : width + 2, :]
        one, two = col_a[i, r].astype(F32), col_b[i, r].astype(F32)
        before, after = jnp.where(col_odd, one, two), jnp.where(col_odd, two, one)
        near_before = jnp.where(left, own_first, before[3:4])
        near_after = jnp.where(right, own_last, after[0:1])
        cells.append(
            centre[i, r, :width, :] + 0.25 * (jnp.where(is_first, near_before, 0.0) + jnp.where(is_last, near_after, 0.0))
        )
        first = 0.75 * (before[2:3] + before[3:4]) + 0.25 * (before[1:2] + own_first)
        last = 0.75 * (after[0:1] + after[1:2]) + 0.25 * (own_last + after[2:3])
        beside.append(
            jnp.concatenate([jnp.where(left, 0.0, first), jnp.where(right, 0.0, last)], axis=0)
        )
    return cells, beside


def place(cells, beside, pooled, window, at):
    width = cells.shape[0]
    pooled[LEFT : LEFT + width, :] = cells
    pooled[LEFT - 1 : LEFT, :] = beside[:1]
    pooled[LEFT + width : LEFT + width + 1, :] = beside[1:]
    for v in range(3):
        window[v, pl.ds(at, width), :] = pooled[pl.ds(LEFT + 1 - v, width), :].astype(BF16)


def row_pack_kernel(has_second, flags, centre, col_a, col_b, *refs):
    outs, (cells_out, beside_out, ends) = refs[: 2 if has_second else 1], refs[-3:]
    images, height2, width = centre.shape[0], centre.shape[1], centre.shape[2] - 8
    row_odd = flags[ROW_ODD] == 1
    lines = [0, 1, 2, height2 - 3, height2 - 2, height2 - 1]
    for i in range(images):
        cells, beside = pool_columns(flags, centre, col_a, col_b, i, lines)
        for n in range(6):
            cells_out[i, n] = cells[n]
            beside_out[i, n] = beside[n]
        for group, is_end in ((cells, False), (beside, True)):
            above = [group[0], 0.75 * (group[0] + group[1]) + 0.25 * group[2]]
            below = [0.25 * group[3] + 0.75 * (group[4] + group[5]), group[5]]
            for second in range(len(outs)):
                for n in range(2):
                    odd, even = (below[n], above[n]) if second else (above[n], below[n])
                    value = jnp.where(row_odd, odd, even)
                    if is_end:
                        ends[second, (2 * i + n) * 2 : (2 * i + n) * 2 + 2, :] = value
                    else:
                        at = (2 * i + n) * width
                        outs[second][at : at + width, :] = value.astype(BF16)
    for second in range(len(outs)):
        outs[second][2 * images * width :, :] = ends[second].astype(BF16)


def main_kernel(flags, centre, col_a, col_b, weight, window, acc, pooled):
    images, height2, width, channels = centre.shape[0], centre.shape[1], centre.shape[2] - 8, centre.shape[3]
    height, depths = height2 // 2, weight.shape[0]
    pooled[...] = jnp.zeros_like(pooled)

    def per_image(i, carry):
        cells, beside = pool_columns(flags, centre, col_a, col_b, i, range(1, height2 - 1))
        for p in range(1, height - 1):
            at = 2 * p - 2
            both = [
                0.75 * (group[at + 1] + group[at + 2]) + 0.25 * (group[at] + group[at + 3])
                for group in (cells, beside)
            ]
            where = pl.multiple_of((p + 1) * images * width + i * width, width)
            place(both[0], both[1], pooled.at[p], window, where)
        return carry

    lax.fori_loop(0, images, per_image, 0)
    line = images * width
    inner = (height - 2) * line
    rows = slice(2 * line, 2 * line + inner)
    for k in range(depths):
        for u in range(3):
            part = nt_dot(window[0, rows, :], weight[k, u, 0])
            part = part + nt_dot(window[1, rows, :], weight[k, u, 1])
            part = part + nt_dot(window[2, rows, :], weight[k, u, 2])
            if u == 0:
                acc[k, :inner, :] = part
                acc[k, inner:, :] = jnp.zeros((2 * line, channels), F32)
            else:
                acc[k, u * line : u * line + inner, :] += part


def edge_kernel(has_second, flags, *refs):
    sides = 2 if has_second else 1
    rows, (cells, beside, _, acc, weight) = refs[:sides], refs[sides : sides + 5]
    *grads, window, pooled, ends, total = refs[sides + 5 :]
    images, width = cells.shape[0], cells.shape[2]
    depths, count = acc.shape[:2]
    line = images * width
    height = count // line
    row_odd, top, bottom = flags[ROW_ODD] == 1, flags[TOP] == 1, flags[BOTTOM] == 1
    for n in range(sides):
        ends[n] = rows[n][2 * line :, :].astype(F32)
    pooled[...] = jnp.zeros_like(pooled)
    for i in range(images):
        for_rows = []
        for is_end, own in ((False, cells), (True, beside)):
            def came(from_above, n):
                def of(ref_at):
                    if is_end:
                        at = (2 * i + n) * 2
                        return ends[ref_at, at : at + 2, :]
                    at = (2 * i + n) * width
                    return rows[ref_at][at : at + width, :].astype(F32)

                first = of(0)
                second = of(1) if has_second else jnp.zeros_like(first)
                return jnp.where(row_odd, first, second) if from_above else jnp.where(row_odd, second, first)

            edge = [own[i, n] for n in range(6)]
            zero = jnp.zeros_like(edge[0])
            for_rows.append(
                [
                    jnp.where(top, zero, came(True, 0) + 0.25 * edge[0]),
                    0.75 * (edge[0] + edge[1]) + 0.25 * (jnp.where(top, edge[0], came(True, 1)) + edge[2]),
                    0.75 * (edge[4] + edge[5]) + 0.25 * (jnp.where(bottom, edge[5], came(False, 0)) + edge[3]),
                    jnp.where(bottom, zero, came(False, 1) + 0.25 * edge[5]),
                ]
            )
        for n, p in enumerate((0, 1, height, height + 1)):
            place(for_rows[0][n], for_rows[1][n], pooled.at[n], window, p * line + i * width)
    low, high = slice(0, 2 * line), slice(height * line, (height + 2) * line)
    for k in range(depths):
        total[...] = acc[k]
        for v in range(3):
            total[(height - 2) * line :, :] += nt_dot(window[v, high, :], weight[k, 0, v])
            total[: 2 * line, :] += nt_dot(window[v, low, :], weight[k, 2, v])
            middle = jnp.concatenate(
                [window[v, line : 2 * line, :], window[v, height * line : (height + 1) * line, :]], axis=0
            )
            part = nt_dot(middle, weight[k, 1, v])
            total[:line, :] += part[:line]
            total[(height - 1) * line :, :] += part[line:]
        for apart in range(2 * CHIPS):
            at = pl.multiple_of((flags[GRAY] ^ apart) * line, line)
            grads[apart // 2][apart % 2, k] = total[pl.ds(at, line), :].astype(BF16)


def deal(full, split_refs, core, turned):
    if len(split_refs) == 1:
        split_refs[0][...] = full[...]
        return
    kept, *sent = split_refs
    count, rows = kept.shape[:2]
    size = sent[0].shape[0]
    for j in range(count):
        p = (j & ~3 | (j & 1) << 1 | j >> 1 & 1) if turned else j
        kept[p] = full[pl.ds(pl.multiple_of((2 * j + core) * rows, 16), rows), :]
        sent[p // size][p % size] = full[pl.ds(pl.multiple_of((2 * j + 1 - core) * rows, 16), rows), :]


def conv_term_kernel(flags, window, saved, *refs):
    split_refs, top, full, flat = refs[:-3], refs[-3], refs[-2], refs[-1]
    images, depths, height, width, channels = saved.shape
    line = images * width
    count = height * line
    split = top.shape[0]
    for k in range(depths):
        for h in range(height):
            for i in range(images):
                at = (h * images + i) * width
                flat[at : at + width, :] = saved[i, k, h]
        flat_t = flat[...].T
        for n in range(9):
            start = (2 - n // 3) * line
            part = jnp.dot(
                flat_t, window[n % 3, start : start + count, :], preferred_element_type=F32
            ).astype(BF16)
            at = (k * 9 + n) * channels
            if at < split:
                top[at : at + channels, :] = part
            else:
                full[at - split : at - split + channels, :] = part
    deal(full, split_refs, flags[CORE], True)


def pass_on_kernel(*refs):
    for n, piece in enumerate(refs[:-1]):
        refs[-1][n] = piece[1]


def proj_term_kernel(flags, *refs):
    came, (passed, feats, conv_top) = refs[:CHIPS], refs[CHIPS : CHIPS + 3]
    split_refs, tokens, full = refs[CHIPS + 3 : -2], refs[-2], refs[-1]
    images, depths, _, dim = feats.shape
    line = passed.shape[2]
    width = line // images
    for apart in range(2 * CHIPS):
        column = column_of(flags[GRAY] ^ apart)
        for k in range(depths):
            for i in range(images):
                at = pl.multiple_of((i * TILE_COLS + column) * width, width)
                rows = slice(i * width, (i + 1) * width)
                piece = passed[apart // 2, k, rows, :] if apart % 2 else came[apart // 2][0, k, rows, :]
                tokens[k, pl.ds(at, width), :] = piece
    for k in range(depths):
        flat = feats[:, k].reshape(tokens.shape[1], dim)
        part = lax.dot_general(
            flat, tokens[k], (((0,), (0,)), ((), ())), preferred_element_type=F32
        )
        full[k * dim : (k + 1) * dim, :] = part.astype(BF16)
    full[depths * dim :, :] = conv_top[...]
    deal(full, split_refs, flags[CORE], False)


def feat_grad_kernel(tokens, weight, out):
    images, depths, count, dim = out.shape
    for k in range(depths):
        out[:, k] = nt_dot(tokens[k], weight[k]).astype(BF16).reshape(images, count, dim)


def take(part, block, at, columns=None):
    size = part[0].shape[0]
    return part[block // size][block % size + at, :, slice(None) if columns is None else columns].astype(F32)


def round_kernel(jobs, flags, *refs):
    ins, outs, dp = list(refs[: sum(sum(job[0]) for job in jobs)]), refs, flags[DP]
    outs = list(refs[len(ins) :])
    for sizes, at, bits, by_columns, heights in jobs:
        parts = []
        for size in sizes:
            parts.append(ins[:size])
            del ins[:size]
        span = 1 << bits
        mine = 0
        for b in range(bits):
            mine = mine + flags[BITS + at + b] * (1 << b)
        last = span * (2 if by_columns else 1)
        for n in [0] + list(range(last - 1, 0, -1)):
            across, apart = n // span, n % span
            pieces = outs[: len(heights) if n else 1]
            del outs[: len(pieces)]
            count, _, width = pieces[0].shape
            columns = None
            if by_columns:
                columns = pl.ds(pl.multiple_of((dp ^ across) * width, width), width)
            for q in range(count):
                total = take(parts[0], q * span, mine ^ apart, columns)
                for other in parts[1:]:
                    total = total + take(other, q * span, mine ^ apart, columns)
                start = 0
                for piece in pieces:
                    piece[q] = total[start : start + piece.shape[1]].astype(piece.dtype)
                    start += piece.shape[1]


def last_kernel(early_parts, flags, *refs):
    ins, (sent, kept) = list(refs[:-2]), refs[-2:]
    first = flags[DP] == 0
    sums = []
    for sizes in (early_parts, (1,) * (len(ins) - sum(early_parts))):
        total = 0.0
        for size in sizes:
            rows = [piece[0].astype(F32) for piece in ins[:size]]
            total = total + (jnp.concatenate(rows, axis=0) if size > 1 else rows[0])
            del ins[:size]
        sums.append(total)
    sent[...] = jnp.where(first, sums[0], sums[1]).astype(BF16)
    kept[...] = jnp.where(first, sums[1], sums[0])


def join_kernel(scale, flags, kept, came, out):
    width = kept.shape[1]
    at = pl.multiple_of(flags[DP] * width, width)
    out[:, pl.ds(at, width)] = kept[...] * scale
    at = pl.multiple_of((1 - flags[DP]) * width, width)
    out[:, pl.ds(at, width)] = came[...].astype(F32) * scale


def vmem_call(kernel, out_shape, operands, scratch=(), scalars=1, flops=0, limit=16, after=(), aliases=()):
    whole = pl.BlockSpec(memory_space=pltpu.VMEM)
    specs = [pl.BlockSpec(memory_space=pltpu.SMEM)] * scalars + [whole] * (len(operands) - scalars)
    specs += [pl.BlockSpec(memory_space=pl.ANY)] * len(after)
    count = len(operands)

    def run(*refs):
        kernel(*refs[:count], *refs[count + len(after) :])

    moved = sum(a.size * a.dtype.itemsize for a in operands)
    moved += sum(math.prod(s.shape) * s.dtype.itemsize for s in jax.tree.leaves(out_shape))
    return pl.pallas_call(
        run,
        out_shape=out_shape,
        in_specs=specs,
        out_specs=jax.tree.map(lambda _: whole, out_shape),
        scratch_shapes=list(scratch),
        input_output_aliases=dict(aliases),
        compiler_params=pltpu.CompilerParams(vmem_limit_bytes=limit << 20),
        cost_estimate=pl.CostEstimate(flops=flops, bytes_accessed=moved, transcendentals=0),
    )(*operands, *after)


def sds(*shape, dtype=BF16):
    return jax.ShapeDtypeStruct(shape, dtype)


def xor_move(block, apart, across):
    tiles = lax.axis_size("tile")
    if not across:
        return lax.ppermute(block, "tile", [(t, t ^ apart) for t in range(tiles)])
    if not apart:
        return lax.ppermute(block, "dp", [(0, 1), (1, 0)])
    route = [(d * tiles + t, (1 - d) * tiles + (t ^ apart)) for d in range(2) for t in range(tiles)]
    return lax.ppermute(block, ("dp", "tile"), route)


def core_sum(dealt, core, pieces, turned):
    if len(dealt) == 1:
        tiles = lax.axis_size("tile")
        rows, channels = dealt[0].shape[0] // tiles, dealt[0].shape[1]
        pairs = dealt[0].reshape(tiles // 2, 2, rows, channels)
        if turned:
            pairs = pairs.reshape(tiles // 8, 2, 2, 2, rows, channels).swapaxes(1, 2).reshape(pairs.shape)
        kept = lax.dynamic_index_in_dim(pairs, core, 1, keepdims=False)
        sent = lax.dynamic_index_in_dim(pairs, 1 - core, 1, keepdims=False)
        size = sent.shape[0] // pieces
        sent = [sent[n * size : (n + 1) * size] for n in range(pieces)]
    else:
        kept, *sent = dealt
    return [[kept], [xor_move(piece, 1, False) for piece in sent]]


def deal_rounds(jobs, flags, after=()):
    outs, plans, operands = [], [], [flags]
    for parts, at, bits, by_columns, cut in jobs:
        span = 1 << bits
        count, rows, channels = parts[0][0].shape
        channels = channels // 2 if by_columns else channels
        tiles = rows // 16
        heights = [rows]
        if rows % 16 == 0 and cut > 1:
            heights = [16 * (tiles * (n + 1) // cut - tiles * n // cut) for n in range(cut)]
        for n in range(span * (2 if by_columns else 1)):
            if n == 0:
                outs.append(sds(count // span, rows, channels, dtype=F32))
            else:
                outs += [sds(count // span, height, channels) for height in heights]
        plans.append((tuple(len(part) for part in parts), at, bits, by_columns, tuple(heights)))
        operands += [piece for part in parts for piece in part]
    pieces = list(vmem_call(functools.partial(round_kernel, plans), outs, operands, after=after))
    token, sums = pieces[0], []
    for _, at, bits, by_columns, heights in plans:
        span = 1 << bits
        parts = [[pieces.pop(0)]]
        for n in range(span * (2 if by_columns else 1) - 1, 0, -1):
            parts.append([xor_move(pieces.pop(0), (n % span) << at, n >= span) for _ in heights])
        sums.append(parts)
    return sums, token


def per_device(features, proj_weight, conv_weight, saved, cotangent):
    position = lax.axis_index("tile")
    tile_count = lax.axis_size("tile")
    rows = tile_count // TILE_COLS
    gray = position % TILE_COLS
    col, row = column_of(gray), position // TILE_COLS
    images, height2, width2, channels = cotangent.shape
    depths, dim = proj_weight.shape[:2]
    height, width = height2 // 2, width2 // 2
    patches = images * height * width
    line = images * width
    tokens = features.shape[2]
    has_second = rows > 2
    sides = 2 if has_second else 1
    bits = tile_count.bit_length() - 1
    flags = jnp.stack(
        [row % 2, col % 2, row == 0, row == rows - 1, col == 0, col == TILE_COLS - 1]
        + [position % 2, lax.axis_index("dp"), gray]
        + [position >> b & 1 for b in range(bits)]
    ).astype(jnp.int32)

    def swap(block, row_pairs, col_pairs):
        return lax.ppermute(block, "tile", tile_route(row_pairs, col_pairs, rows))

    low, high = cotangent[:, :, :HALO], cotangent[:, :, width2 - HALO :]
    around = paired(TILE_COLS, 1) + [(0, TILE_COLS - 1), (TILE_COLS - 1, 0)]
    col_b = swap(jnp.where(col % 2 == 1, high, low), None, around)
    col_a = swap(jnp.where(col % 2 == 1, low, high), None, paired(TILE_COLS, 0))
    centre = vmem_call(
        centre_kernel,
        sds(images, height2, width + 8, channels, dtype=F32),
        (cotangent,),
        scratch=(pltpu.VMEM((channels // 128, height2, LEFT + width2 + 8, 128), F32),),
        scalars=0,
    )
    *row_out, cells, beside = vmem_call(
        functools.partial(row_pack_kernel, has_second),
        [sds(2 * images * (width + 2), channels)] * sides
        + [sds(images, 6, width, channels, dtype=F32), sds(images, 6, 2, channels, dtype=F32)],
        (flags, centre, col_a, col_b),
        scratch=(pltpu.VMEM((sides, 4 * images, channels), F32),),
    )
    came_rows = [swap(row_out[n], paired(rows, n), None) for n in range(sides)]
    conv_flops = 2 * patches * depths * 9 * channels * channels
    window, acc = vmem_call(
        main_kernel,
        [sds(3, (height + 2) * line, channels), sds(depths, patches, channels, dtype=F32)],
        (flags, centre, col_a, col_b, conv_weight),
        scratch=(pltpu.VMEM((height, LEFT + width + 8, channels), F32),),
        flops=conv_flops,
        after=(row_out[0],),
    )
    *grads, window = vmem_call(
        functools.partial(edge_kernel, has_second),
        [sds(2, depths, line, channels)] * CHIPS + [sds(3, (height + 2) * line, channels)],
        [flags] + came_rows + [cells, beside, window, acc, conv_weight],
        scratch=(
            pltpu.VMEM((4, LEFT + width + 8, channels), F32),
            pltpu.VMEM((sides, 4 * images, channels), F32),
            pltpu.VMEM((patches, channels), F32),
        ),
        flops=conv_flops // 4,
        aliases={sides + 3: CHIPS},
    )
    came = [xor_move(grads[chip], 2 * chip, False) for chip in range(CHIPS - 1, 0, -1)]
    came = [grads[0]] + came[::-1]
    to_pass = vmem_call(pass_on_kernel, sds(CHIPS, depths, line, channels), came, scalars=0)
    passed = xor_move(to_pass, 1, False)

    half_rows = depths * (dim + 9 * channels) // 2
    conv_late = half_rows - depths * dim
    block_rows = half_rows // tile_count
    pieces = 4
    if block_rows % 16:
        dealt = [sds(half_rows, channels)]
    else:
        dealt = [sds(tile_count // 2, block_rows, channels)]
        dealt += [sds(tile_count // 2 // pieces, block_rows, channels)] * pieces
    full = pltpu.VMEM((half_rows, channels), BF16)
    *early, conv_top = vmem_call(
        conv_term_kernel,
        dealt + [sds(conv_late, channels)],
        (flags, window, saved),
        scratch=(full, pltpu.VMEM((patches, channels), BF16)),
        flops=conv_flops,
    )
    (early_parts,), before = deal_rounds([(core_sum(early, position % 2, pieces, True), 1, 0, True, 1)], flags)
    proj_flops = 2 * images * tokens * depths * dim * channels
    *terms, token_grad = vmem_call(
        proj_term_kernel,
        dealt + [sds(depths, images * tokens, channels)],
        [flags] + came + [passed, features, conv_top],
        scratch=(full,),
        flops=proj_flops,
        after=(before,),
    )
    (late_parts,), before = deal_rounds(
        [(core_sum(terms, position % 2, pieces, False), 1, 1, True, 1)], flags, after=(token_grad,)
    )
    at, early_bits = 2, [2, 1] + list(range(3, bits))
    while at < bits:
        step = min(2, bits - at)
        (early_parts,), before = deal_rounds([(early_parts, early_bits.pop(0), 1, False, 1)], flags, after=(before,))
        (late_parts, early_parts), before = deal_rounds(
            [(late_parts, at, step, False, 1), (early_parts, early_bits.pop(0), 1, False, 1)], flags, after=(before,)
        )
        at += step
    while early_bits:
        (early_parts,), before = deal_rounds([(early_parts, early_bits.pop(0), 1, False, 1)], flags, after=(before,))
    feature_grad = vmem_call(
        feat_grad_kernel,
        sds(images, depths, tokens, dim),
        (token_grad, proj_weight),
        scalars=0,
        flops=proj_flops,
        after=(before,),
    )
    sent, kept = vmem_call(
        functools.partial(last_kernel, tuple(len(part) for part in early_parts)),
        [sds(block_rows, channels // 2), sds(block_rows, channels // 2, dtype=F32)],
        [flags] + [piece for part in early_parts + late_parts for piece in part],
    )
    other = xor_move(sent, 0, True)
    scale = 1.0 / math.sqrt(images * lax.axis_size("dp") * tokens * tile_count)
    head_grad = vmem_call(
        functools.partial(join_kernel, scale), sds(block_rows, channels, dtype=F32), (flags, kept, other)
    )
    return feature_grad, head_grad


def solution(mesh):
    in_specs = (
        P("dp", None, "tile", None),
        P(),
        P(),
        P("dp", None, "tile", None, None),
        P("dp", "tile", None, None),
    )
    out_specs = (P("dp", None, "tile", None), P(("dp", "tile"), None))
    return jax.shard_map(
        per_device, mesh=mesh, in_specs=in_specs, out_specs=out_specs, check_vma=False
    )
```

```python
import functools
import math

import jax
import jax.numpy as jnp
from jax import lax
from jax.experimental import pallas as pl
from jax.experimental.pallas import tpu as pltpu
from jax.sharding import PartitionSpec as P

TILE_COLS = 8
HALO = 4
LEFT = 8
BF16 = jnp.bfloat16
F32 = jnp.float32
ROW_ODD, COL_ODD, TOP, BOTTOM, LEFT_END, RIGHT_END, CORE, DP, GRAY, BITS = range(10)
CHIPS = TILE_COLS // 2


def gray_of(column):
    return column ^ column >> 1


def column_of(code):
    return code ^ code >> 1 ^ code >> 2


def paired(count, first):
    pairs = []
    for low in range(first, count - 1, 2):
        pairs += [(low, low + 1), (low + 1, low)]
    return pairs


def tile_route(row_pairs, col_pairs, rows):
    row_moves = row_pairs if row_pairs is not None else [(r, r) for r in range(rows)]
    col_moves = col_pairs if col_pairs is not None else [(c, c) for c in range(TILE_COLS)]
    return [
        (r0 * TILE_COLS + gray_of(c0), r1 * TILE_COLS + gray_of(c1))
        for r0, r1 in row_moves
        for c0, c1 in col_moves
    ]


def nt_dot(left, right):
    return lax.dot_general(left, right, (((1,), (1,)), ((), ())), preferred_element_type=F32)


def centre_kernel(cot, pooled, wide):
    images, height2, width2, channels = cot.shape
    width = width2 // 2
    wide[...] = jnp.zeros_like(wide)

    def per_image(i, carry):
        for r in range(height2):
            value = cot[i, r].astype(F32)
            for h in range(channels // 128):
                wide[h, r, LEFT : LEFT + width2, :] = value[:, h * 128 : (h + 1) * 128]
            pooled[i, r, width : width + 1, :] = value[:1]
            pooled[i, r, width + 1 : width + 2, :] = value[width2 - 1 :]
        for r in range(height2):
            for h in range(channels // 128):
                taps = [wide[h, r, pl.ds(LEFT - 1 + n, width, stride=2), :] for n in range(4)]
                pooled[i, r, :width, h * 128 : (h + 1) * 128] = 0.75 * (taps[1] + taps[2]) + 0.25 * (taps[0] + taps[3])
        return carry

    lax.fori_loop(0, images, per_image, 0)


def pool_columns(flags, centre, col_a, col_b, i, lines):
    width, channels = centre.shape[2] - 8, centre.shape[3]
    col_odd, left, right = flags[COL_ODD] == 1, flags[LEFT_END] == 1, flags[RIGHT_END] == 1
    cell = lax.broadcasted_iota(jnp.int32, (width, channels), 0)
    is_first, is_last = cell == 0, cell == width - 1
    cells, beside = [], []
    for r in lines:
        own_first, own_last = centre[i, r, width : width + 1, :], centre[i, r, width + 1 : width + 2, :]
        one, two = col_a[i, r].astype(F32), col_b[i, r].astype(F32)
        before, after = jnp.where(col_odd, one, two), jnp.where(col_odd, two, one)
        near_before = jnp.where(left, own_first, before[3:4])
        near_after = jnp.where(right, own_last, after[0:1])
        cells.append(
            centre[i, r, :width, :] + 0.25 * (jnp.where(is_first, near_before, 0.0) + jnp.where(is_last, near_after, 0.0))
        )
        first = 0.75 * (before[2:3] + before[3:4]) + 0.25 * (before[1:2] + own_first)
        last = 0.75 * (after[0:1] + after[1:2]) + 0.25 * (own_last + after[2:3])
        beside.append(
            jnp.concatenate([jnp.where(left, 0.0, first), jnp.where(right, 0.0, last)], axis=0)
        )
    return cells, beside


def place(cells, beside, pooled, window, at):
    width = cells.shape[0]
    pooled[LEFT : LEFT + width, :] = cells
    pooled[LEFT - 1 : LEFT, :] = beside[:1]
    pooled[LEFT + width : LEFT + width + 1, :] = beside[1:]
    for v in range(3):
        window[v, pl.ds(at, width), :] = pooled[pl.ds(LEFT + 1 - v, width), :].astype(BF16)


def row_pack_kernel(has_second, flags, centre, col_a, col_b, *refs):
    outs, (cells_out, beside_out, ends) = refs[: 2 if has_second else 1], refs[-3:]
    images, height2, width = centre.shape[0], centre.shape[1], centre.shape[2] - 8
    row_odd = flags[ROW_ODD] == 1
    lines = [0, 1, 2, height2 - 3, height2 - 2, height2 - 1]
    for i in range(images):
        cells, beside = pool_columns(flags, centre, col_a, col_b, i, lines)
        for n in range(6):
            cells_out[i, n] = cells[n]
            beside_out[i, n] = beside[n]
        for group, is_end in ((cells, False), (beside, True)):
            above = [group[0], 0.75 * (group[0] + group[1]) + 0.25 * group[2]]
            below = [0.25 * group[3] + 0.75 * (group[4] + group[5]), group[5]]
            for second in range(len(outs)):
                for n in range(2):
                    odd, even = (below[n], above[n]) if second else (above[n], below[n])
                    value = jnp.where(row_odd, odd, even)
                    if is_end:
                        ends[second, (2 * i + n) * 2 : (2 * i + n) * 2 + 2, :] = value
                    else:
                        at = (2 * i + n) * width
                        outs[second][at : at + width, :] = value.astype(BF16)
    for second in range(len(outs)):
        outs[second][2 * images * width :, :] = ends[second].astype(BF16)


def main_kernel(flags, centre, col_a, col_b, weight, window, acc, pooled):
    images, height2, width, channels = centre.shape[0], centre.shape[1], centre.shape[2] - 8, centre.shape[3]
    height, depths = height2 // 2, weight.shape[0]
    pooled[...] = jnp.zeros_like(pooled)

    def per_image(i, carry):
        cells, beside = pool_columns(flags, centre, col_a, col_b, i, range(1, height2 - 1))
        for p in range(1, height - 1):
            at = 2 * p - 2
            both = [
                0.75 * (group[at + 1] + group[at + 2]) + 0.25 * (group[at] + group[at + 3])
                for group in (cells, beside)
            ]
            where = pl.multiple_of((p + 1) * images * width + i * width, width)
            place(both[0], both[1], pooled.at[p], window, where)
        return carry

    lax.fori_loop(0, images, per_image, 0)
    line = images * width
    inner = (height - 2) * line
    rows = slice(2 * line, 2 * line + inner)
    for k in range(depths):
        for u in range(3):
            part = nt_dot(window[0, rows, :], weight[k, u, 0])
            part = part + nt_dot(window[1, rows, :], weight[k, u, 1])
            part = part + nt_dot(window[2, rows, :], weight[k, u, 2])
            if u == 0:
                acc[k, :inner, :] = part
                acc[k, inner:, :] = jnp.zeros((2 * line, channels), F32)
            else:
                acc[k, u * line : u * line + inner, :] += part


def edge_kernel(has_second, flags, *refs):
    sides = 2 if has_second else 1
    rows, (cells, beside, _, acc, weight) = refs[:sides], refs[sides : sides + 5]
    *grads, window, pooled, ends, total = refs[sides + 5 :]
    images, width = cells.shape[0], cells.shape[2]
    depths, count = acc.shape[:2]
    line = images * width
    height = count // line
    row_odd, top, bottom = flags[ROW_ODD] == 1, flags[TOP] == 1, flags[BOTTOM] == 1
    for n in range(sides):
        ends[n] = rows[n][2 * line :, :].astype(F32)
    pooled[...] = jnp.zeros_like(pooled)
    for i in range(images):
        for_rows = []
        for is_end, own in ((False, cells), (True, beside)):
            def came(from_above, n):
                def of(ref_at):
                    if is_end:
                        at = (2 * i + n) * 2
                        return ends[ref_at, at : at + 2, :]
                    at = (2 * i + n) * width
                    return rows[ref_at][at : at + width, :].astype(F32)

                first = of(0)
                second = of(1) if has_second else jnp.zeros_like(first)
                return jnp.where(row_odd, first, second) if from_above else jnp.where(row_odd, second, first)

            edge = [own[i, n] for n in range(6)]
            zero = jnp.zeros_like(edge[0])
            for_rows.append(
                [
                    jnp.where(top, zero, came(True, 0) + 0.25 * edge[0]),
                    0.75 * (edge[0] + edge[1]) + 0.25 * (jnp.where(top, edge[0], came(True, 1)) + edge[2]),
                    0.75 * (edge[4] + edge[5]) + 0.25 * (jnp.where(bottom, edge[5], came(False, 0)) + edge[3]),
                    jnp.where(bottom, zero, came(False, 1) + 0.25 * edge[5]),
                ]
            )
        for n, p in enumerate((0, 1, height, height + 1)):
            place(for_rows[0][n], for_rows[1][n], pooled.at[n], window, p * line + i * width)
    low, high = slice(0, 2 * line), slice(height * line, (height + 2) * line)
    for k in range(depths):
        total[...] = acc[k]
        for v in range(3):
            total[(height - 2) * line :, :] += nt_dot(window[v, high, :], weight[k, 0, v])
            total[: 2 * line, :] += nt_dot(window[v, low, :], weight[k, 2, v])
            middle = jnp.concatenate(
                [window[v, line : 2 * line, :], window[v, height * line : (height + 1) * line, :]], axis=0
            )
            part = nt_dot(middle, weight[k, 1, v])
            total[:line, :] += part[:line]
            total[(height - 1) * line :, :] += part[line:]
        for apart in range(2 * CHIPS):
            at = pl.multiple_of((flags[GRAY] ^ apart) * line, line)
            grads[apart // 2][apart % 2, k] = total[pl.ds(at, line), :].astype(BF16)


def deal(full, split_refs, core, turned):
    if len(split_refs) == 1:
        split_refs[0][...] = full[...]
        return
    kept, *sent = split_refs
    count, rows = kept.shape[:2]
    size = sent[0].shape[0]
    for j in range(count):
        p = (j & ~3 | (j & 1) << 1 | j >> 1 & 1) if turned else j
        kept[p] = full[pl.ds(pl.multiple_of((2 * j + core) * rows, 16), rows), :]
        sent[p // size][p % size] = full[pl.ds(pl.multiple_of((2 * j + 1 - core) * rows, 16), rows), :]


def conv_term_kernel(flags, window, saved, *refs):
    split_refs, top, full, flat = refs[:-3], refs[-3], refs[-2], refs[-1]
    images, depths, height, width, channels = saved.shape
    line = images * width
    count = height * line
    split = top.shape[0]
    for k in range(depths):
        for h in range(height):
            for i in range(images):
                at = (h * images + i) * width
                flat[at : at + width, :] = saved[i, k, h]
        flat_t = flat[...].T
        for n in range(9):
            start = (2 - n // 3) * line
            part = jnp.dot(
                flat_t, window[n % 3, start : start + count, :], preferred_element_type=F32
            ).astype(BF16)
            at = (k * 9 + n) * channels
            if at < split:
                top[at : at + channels, :] = part
            else:
                full[at - split : at - split + channels, :] = part
    deal(full, split_refs, flags[CORE], True)


def pass_on_kernel(*refs):
    for n, piece in enumerate(refs[:-1]):
        refs[-1][n] = piece[1]


def proj_term_kernel(flags, *refs):
    came, (passed, feats, conv_top) = refs[:CHIPS], refs[CHIPS : CHIPS + 3]
    split_refs, tokens, full = refs[CHIPS + 3 : -2], refs[-2], refs[-1]
    images, depths, _, dim = feats.shape
    line = passed.shape[2]
    width = line // images
    for apart in range(2 * CHIPS):
        column = column_of(flags[GRAY] ^ apart)
        for k in range(depths):
            for i in range(images):
                at = pl.multiple_of((i * TILE_COLS + column) * width, width)
                rows = slice(i * width, (i + 1) * width)
                piece = passed[apart // 2, k, rows, :] if apart % 2 else came[apart // 2][0, k, rows, :]
                tokens[k, pl.ds(at, width), :] = piece
    for k in range(depths):
        flat = feats[:, k].reshape(tokens.shape[1], dim)
        part = lax.dot_general(
            flat, tokens[k], (((0,), (0,)), ((), ())), preferred_element_type=F32
        )
        full[k * dim : (k + 1) * dim, :] = part.astype(BF16)
    full[depths * dim :, :] = conv_top[...]
    deal(full, split_refs, flags[CORE], False)


def feat_grad_kernel(tokens, weight, out):
    images, depths, count, dim = out.shape
    for k in range(depths):
        out[:, k] = nt_dot(tokens[k], weight[k]).astype(BF16).reshape(images, count, dim)


def take(part, block, at, columns=None):
    size = part[0].shape[0]
    return part[block // size][block % size + at, :, slice(None) if columns is None else columns].astype(F32)


def round_kernel(jobs, flags, *refs):
    ins, outs, dp = list(refs[: sum(sum(job[0]) for job in jobs)]), refs, flags[DP]
    outs = list(refs[len(ins) :])
    for sizes, at, bits, by_columns, heights in jobs:
        parts = []
        for size in sizes:
            parts.append(ins[:size])
            del ins[:size]
        span = 1 << bits
        mine = 0
        for b in range(bits):
            mine = mine + flags[BITS + at + b] * (1 << b)
        last = span * (2 if by_columns else 1)
        for n in [0] + list(range(last - 1, 0, -1)):
            across, apart = n // span, n % span
            pieces = outs[: len(heights) if n else 1]
            del outs[: len(pieces)]
            count, _, width = pieces[0].shape
            columns = None
            if by_columns:
                columns = pl.ds(pl.multiple_of((dp ^ across) * width, width), width)
            for q in range(count):
                total = take(parts[0], q * span, mine ^ apart, columns)
                for other in parts[1:]:
                    total = total + take(other, q * span, mine ^ apart, columns)
                start = 0
                for piece in pieces:
                    piece[q] = total[start : start + piece.shape[1]].astype(piece.dtype)
                    start += piece.shape[1]


def last_kernel(early_parts, flags, *refs):
    ins, (sent, kept) = list(refs[:-2]), refs[-2:]
    first = flags[DP] == 0
    sums = []
    for sizes in (early_parts, (1,) * (len(ins) - sum(early_parts))):
        total = 0.0
        for size in sizes:
            rows = [piece[0].astype(F32) for piece in ins[:size]]
            total = total + (jnp.concatenate(rows, axis=0) if size > 1 else rows[0])
            del ins[:size]
        sums.append(total)
    sent[...] = jnp.where(first, sums[0], sums[1]).astype(BF16)
    kept[...] = jnp.where(first, sums[1], sums[0])


def join_kernel(scale, flags, kept, came, out):
    width = kept.shape[1]
    at = pl.multiple_of(flags[DP] * width, width)
    out[:, pl.ds(at, width)] = kept[...] * scale
    at = pl.multiple_of((1 - flags[DP]) * width, width)
    out[:, pl.ds(at, width)] = came[...].astype(F32) * scale


def vmem_call(kernel, out_shape, operands, scratch=(), scalars=1, flops=0, limit=16, after=(), aliases=()):
    whole = pl.BlockSpec(memory_space=pltpu.VMEM)
    specs = [pl.BlockSpec(memory_space=pltpu.SMEM)] * scalars + [whole] * (len(operands) - scalars)
    specs += [pl.BlockSpec(memory_space=pl.ANY)] * len(after)
    count = len(operands)

    def run(*refs):
        kernel(*refs[:count], *refs[count + len(after) :])

    moved = sum(a.size * a.dtype.itemsize for a in operands)
    moved += sum(math.prod(s.shape) * s.dtype.itemsize for s in jax.tree.leaves(out_shape))
    return pl.pallas_call(
        run,
        out_shape=out_shape,
        in_specs=specs,
        out_specs=jax.tree.map(lambda _: whole, out_shape),
        scratch_shapes=list(scratch),
        input_output_aliases=dict(aliases),
        compiler_params=pltpu.CompilerParams(vmem_limit_bytes=limit << 20),
        cost_estimate=pl.CostEstimate(flops=flops, bytes_accessed=moved, transcendentals=0),
    )(*operands, *after)


def sds(*shape, dtype=BF16):
    return jax.ShapeDtypeStruct(shape, dtype)


def xor_move(block, apart, across):
    tiles = lax.axis_size("tile")
    if not across:
        return lax.ppermute(block, "tile", [(t, t ^ apart) for t in range(tiles)])
    if not apart:
        return lax.ppermute(block, "dp", [(0, 1), (1, 0)])
    route = [(d * tiles + t, (1 - d) * tiles + (t ^ apart)) for d in range(2) for t in range(tiles)]
    return lax.ppermute(block, ("dp", "tile"), route)


def core_sum(dealt, core, pieces, turned):
    if len(dealt) == 1:
        tiles = lax.axis_size("tile")
        rows, channels = dealt[0].shape[0] // tiles, dealt[0].shape[1]
        pairs = dealt[0].reshape(tiles // 2, 2, rows, channels)
        if turned:
            pairs = pairs.reshape(tiles // 8, 2, 2, 2, rows, channels).swapaxes(1, 2).reshape(pairs.shape)
        kept = lax.dynamic_index_in_dim(pairs, core, 1, keepdims=False)
        sent = lax.dynamic_index_in_dim(pairs, 1 - core, 1, keepdims=False)
        size = sent.shape[0] // pieces
        sent = [sent[n * size : (n + 1) * size] for n in range(pieces)]
    else:
        kept, *sent = dealt
    return [[kept], [xor_move(piece, 1, False) for piece in sent]]


def deal_rounds(jobs, flags, after=()):
    outs, plans, operands = [], [], [flags]
    for parts, at, bits, by_columns, cut in jobs:
        span = 1 << bits
        count, rows, channels = parts[0][0].shape
        channels = channels // 2 if by_columns else channels
        tiles = rows // 16
        heights = [rows]
        if rows % 16 == 0 and cut > 1:
            heights = [16 * (tiles * (n + 1) // cut - tiles * n // cut) for n in range(cut)]
        for n in range(span * (2 if by_columns else 1)):
            if n == 0:
                outs.append(sds(count // span, rows, channels, dtype=F32))
            else:
                outs += [sds(count // span, height, channels) for height in heights]
        plans.append((tuple(len(part) for part in parts), at, bits, by_columns, tuple(heights)))
        operands += [piece for part in parts for piece in part]
    pieces = list(vmem_call(functools.partial(round_kernel, plans), outs, operands, after=after))
    token, sums = pieces[0], []
    for _, at, bits, by_columns, heights in plans:
        span = 1 << bits
        parts = [[pieces.pop(0)]]
        for n in range(span * (2 if by_columns else 1) - 1, 0, -1):
            parts.append([xor_move(pieces.pop(0), (n % span) << at, n >= span) for _ in heights])
        sums.append(parts)
    return sums, token


def per_device(features, proj_weight, conv_weight, saved, cotangent):
    position = lax.axis_index("tile")
    tile_count = lax.axis_size("tile")
    rows = tile_count // TILE_COLS
    gray = position % TILE_COLS
    col, row = column_of(gray), position // TILE_COLS
    images, height2, width2, channels = cotangent.shape
    depths, dim = proj_weight.shape[:2]
    height, width = height2 // 2, width2 // 2
    patches = images * height * width
    line = images * width
    tokens = features.shape[2]
    has_second = rows > 2
    sides = 2 if has_second else 1
    bits = tile_count.bit_length() - 1
    flags = jnp.stack(
        [row % 2, col % 2, row == 0, row == rows - 1, col == 0, col == TILE_COLS - 1]
        + [position % 2, lax.axis_index("dp"), gray]
        + [position >> b & 1 for b in range(bits)]
    ).astype(jnp.int32)

    def swap(block, row_pairs, col_pairs):
        return lax.ppermute(block, "tile", tile_route(row_pairs, col_pairs, rows))

    low, high = cotangent[:, :, :HALO], cotangent[:, :, width2 - HALO :]
    around = paired(TILE_COLS, 1) + [(0, TILE_COLS - 1), (TILE_COLS - 1, 0)]
    col_b = swap(jnp.where(col % 2 == 1, high, low), None, around)
    col_a = swap(jnp.where(col % 2 == 1, low, high), None, paired(TILE_COLS, 0))
    centre = vmem_call(
        centre_kernel,
        sds(images, height2, width + 8, channels, dtype=F32),
        (cotangent,),
        scratch=(pltpu.VMEM((channels // 128, height2, LEFT + width2 + 8, 128), F32),),
        scalars=0,
    )
    *row_out, cells, beside = vmem_call(
        functools.partial(row_pack_kernel, has_second),
        [sds(2 * images * (width + 2), channels)] * sides
        + [sds(images, 6, width, channels, dtype=F32), sds(images, 6, 2, channels, dtype=F32)],
        (flags, centre, col_a, col_b),
        scratch=(pltpu.VMEM((sides, 4 * images, channels), F32),),
    )
    came_rows = [swap(row_out[n], paired(rows, n), None) for n in range(sides)]
    conv_flops = 2 * patches * depths * 9 * channels * channels
    window, acc = vmem_call(
        main_kernel,
        [sds(3, (height + 2) * line, channels), sds(depths, patches, channels, dtype=F32)],
        (flags, centre, col_a, col_b, conv_weight),
        scratch=(pltpu.VMEM((height, LEFT + width + 8, channels), F32),),
        flops=conv_flops,
        after=(row_out[0],),
    )
    *grads, window = vmem_call(
        functools.partial(edge_kernel, has_second),
        [sds(2, depths, line, channels)] * CHIPS + [sds(3, (height + 2) * line, channels)],
        [flags] + came_rows + [cells, beside, window, acc, conv_weight],
        scratch=(
            pltpu.VMEM((4, LEFT + width + 8, channels), F32),
            pltpu.VMEM((sides, 4 * images, channels), F32),
            pltpu.VMEM((patches, channels), F32),
        ),
        flops=conv_flops // 4,
        aliases={sides + 3: CHIPS},
    )
    came = [xor_move(grads[chip], 2 * chip, False) for chip in range(CHIPS - 1, 0, -1)]
    came = [grads[0]] + came[::-1]
    to_pass = vmem_call(pass_on_kernel, sds(CHIPS, depths, line, channels), came, scalars=0)
    passed = xor_move(to_pass, 1, False)

    half_rows = depths * (dim + 9 * channels) // 2
    conv_late = half_rows - depths * dim
    block_rows = half_rows // tile_count
    pieces = 4
    if block_rows % 16:
        dealt = [sds(half_rows, channels)]
    else:
        dealt = [sds(tile_count // 2, block_rows, channels)]
        dealt += [sds(tile_count // 2 // pieces, block_rows, channels)] * pieces
    full = pltpu.VMEM((half_rows, channels), BF16)
    *early, conv_top = vmem_call(
        conv_term_kernel,
        dealt + [sds(conv_late, channels)],
        (flags, window, saved),
        scratch=(full, pltpu.VMEM((patches, channels), BF16)),
        flops=conv_flops,
    )
    (early_parts,), before = deal_rounds([(core_sum(early, position % 2, pieces, True), 2, 1, False, 1)], flags)
    proj_flops = 2 * images * tokens * depths * dim * channels
    *terms, token_grad = vmem_call(
        proj_term_kernel,
        dealt + [sds(depths, images * tokens, channels)],
        [flags] + came + [passed, features, conv_top],
        scratch=(full,),
        flops=proj_flops,
        after=(before,),
    )
    (late_parts,), before = deal_rounds(
        [(core_sum(terms, position % 2, pieces, False), 1, 1, True, 1)], flags, after=(token_grad,)
    )
    at, early_rounds = 2, [(1, 0, True), (1, 1, False)] + [(bit, 1, False) for bit in range(3, bits)]
    while at < bits:
        step = min(2, bits - at)
        (early_parts,), before = deal_rounds([(early_parts, *early_rounds.pop(0), 1)], flags, after=(before,))
        (late_parts, early_parts), before = deal_rounds(
            [(late_parts, at, step, False, 1), (early_parts, *early_rounds.pop(0), 1)], flags, after=(before,)
        )
        at += step
    while early_rounds:
        (early_parts,), before = deal_rounds([(early_parts, *early_rounds.pop(0), 1)], flags, after=(before,))
    feature_grad = vmem_call(
        feat_grad_kernel,
        sds(images, depths, tokens, dim),
        (token_grad, proj_weight),
        scalars=0,
        flops=proj_flops,
        after=(before,),
    )
    sent, kept = vmem_call(
        functools.partial(last_kernel, tuple(len(part) for part in early_parts)),
        [sds(block_rows, channels // 2), sds(block_rows, channels // 2, dtype=F32)],
        [flags] + [piece for part in early_parts + late_parts for piece in part],
    )
    other = xor_move(sent, 0, True)
    scale = 1.0 / math.sqrt(images * lax.axis_size("dp") * tokens * tile_count)
    head_grad = vmem_call(
        functools.partial(join_kernel, scale), sds(block_rows, channels, dtype=F32), (flags, kept, other)
    )
    return feature_grad, head_grad


def solution(mesh):
    in_specs = (
        P("dp", None, "tile", None),
        P(),
        P(),
        P("dp", None, "tile", None, None),
        P("dp", "tile", None, None),
    )
    out_specs = (P("dp", None, "tile", None), P(("dp", "tile"), None))
    return jax.shard_map(
        per_device, mesh=mesh, in_specs=in_specs, out_specs=out_specs, check_vma=False
    )
```

```python
import functools
import math

import jax
import jax.numpy as jnp
from jax import lax
from jax.experimental import pallas as pl
from jax.experimental.pallas import tpu as pltpu
from jax.sharding import PartitionSpec as P

TILE_COLS = 8
HALO = 4
LEFT = 8
BF16 = jnp.bfloat16
F32 = jnp.float32
ROW_ODD, COL_ODD, TOP, BOTTOM, LEFT_END, RIGHT_END, CORE, DP, GRAY, BITS = range(10)
CHIPS = TILE_COLS // 2


def gray_of(column):
    return column ^ column >> 1


def column_of(code):
    return code ^ code >> 1 ^ code >> 2


def paired(count, first):
    pairs = []
    for low in range(first, count - 1, 2):
        pairs += [(low, low + 1), (low + 1, low)]
    return pairs


def tile_route(row_pairs, col_pairs, rows):
    row_moves = row_pairs if row_pairs is not None else [(r, r) for r in range(rows)]
    col_moves = col_pairs if col_pairs is not None else [(c, c) for c in range(TILE_COLS)]
    return [
        (r0 * TILE_COLS + gray_of(c0), r1 * TILE_COLS + gray_of(c1))
        for r0, r1 in row_moves
        for c0, c1 in col_moves
    ]


def nt_dot(left, right):
    return lax.dot_general(left, right, (((1,), (1,)), ((), ())), preferred_element_type=F32)


def centre_kernel(cot, pooled, wide):
    images, height2, width2, channels = cot.shape
    width = width2 // 2
    wide[...] = jnp.zeros_like(wide)

    def per_image(i, carry):
        for r in range(height2):
            value = cot[i, r].astype(F32)
            for h in range(channels // 128):
                wide[h, r, LEFT : LEFT + width2, :] = value[:, h * 128 : (h + 1) * 128]
            pooled[i, r, width : width + 1, :] = value[:1]
            pooled[i, r, width + 1 : width + 2, :] = value[width2 - 1 :]
        for r in range(height2):
            for h in range(channels // 128):
                taps = [wide[h, r, pl.ds(LEFT - 1 + n, width, stride=2), :] for n in range(4)]
                pooled[i, r, :width, h * 128 : (h + 1) * 128] = 0.75 * (taps[1] + taps[2]) + 0.25 * (taps[0] + taps[3])
        return carry

    lax.fori_loop(0, images, per_image, 0)


def pool_columns(flags, centre, col_a, col_b, i, lines):
    width, channels = centre.shape[2] - 8, centre.shape[3]
    col_odd, left, right = flags[COL_ODD] == 1, flags[LEFT_END] == 1, flags[RIGHT_END] == 1
    cell = lax.broadcasted_iota(jnp.int32, (width, channels), 0)
    is_first, is_last = cell == 0, cell == width - 1
    cells, beside = [], []
    for r in lines:
        own_first, own_last = centre[i, r, width : width + 1, :], centre[i, r, width + 1 : width + 2, :]
        one, two = col_a[i, r].astype(F32), col_b[i, r].astype(F32)
        before, after = jnp.where(col_odd, one, two), jnp.where(col_odd, two, one)
        near_before = jnp.where(left, own_first, before[3:4])
        near_after = jnp.where(right, own_last, after[0:1])
        cells.append(
            centre[i, r, :width, :] + 0.25 * (jnp.where(is_first, near_before, 0.0) + jnp.where(is_last, near_after, 0.0))
        )
        first = 0.75 * (before[2:3] + before[3:4]) + 0.25 * (before[1:2] + own_first)
        last = 0.75 * (after[0:1] + after[1:2]) + 0.25 * (own_last + after[2:3])
        beside.append(
            jnp.concatenate([jnp.where(left, 0.0, first), jnp.where(right, 0.0, last)], axis=0)
        )
    return cells, beside


def place(cells, beside, pooled, window, at):
    width = cells.shape[0]
    pooled[LEFT : LEFT + width, :] = cells
    pooled[LEFT - 1 : LEFT, :] = beside[:1]
    pooled[LEFT + width : LEFT + width + 1, :] = beside[1:]
    for v in range(3):
        window[v, pl.ds(at, width), :] = pooled[pl.ds(LEFT + 1 - v, width), :].astype(BF16)


def row_pack_kernel(has_second, flags, centre, col_a, col_b, *refs):
    outs, (cells_out, beside_out, ends) = refs[: 2 if has_second else 1], refs[-3:]
    images, height2, width = centre.shape[0], centre.shape[1], centre.shape[2] - 8
    row_odd = flags[ROW_ODD] == 1
    lines = [0, 1, 2, height2 - 3, height2 - 2, height2 - 1]
    for i in range(images):
        cells, beside = pool_columns(flags, centre, col_a, col_b, i, lines)
        for n in range(6):
            cells_out[i, n] = cells[n]
            beside_out[i, n] = beside[n]
        for group, is_end in ((cells, False), (beside, True)):
            above = [group[0], 0.75 * (group[0] + group[1]) + 0.25 * group[2]]
            below = [0.25 * group[3] + 0.75 * (group[4] + group[5]), group[5]]
            for second in range(len(outs)):
                for n in range(2):
                    odd, even = (below[n], above[n]) if second else (above[n], below[n])
                    value = jnp.where(row_odd, odd, even)
                    if is_end:
                        ends[second, (2 * i + n) * 2 : (2 * i + n) * 2 + 2, :] = value
                    else:
                        at = (2 * i + n) * width
                        outs[second][at : at + width, :] = value.astype(BF16)
    for second in range(len(outs)):
        outs[second][2 * images * width :, :] = ends[second].astype(BF16)


def main_kernel(flags, centre, col_a, col_b, weight, window, acc, pooled):
    images, height2, width, channels = centre.shape[0], centre.shape[1], centre.shape[2] - 8, centre.shape[3]
    height, depths = height2 // 2, weight.shape[0]
    pooled[...] = jnp.zeros_like(pooled)

    def per_image(i, carry):
        cells, beside = pool_columns(flags, centre, col_a, col_b, i, range(1, height2 - 1))
        for p in range(1, height - 1):
            at = 2 * p - 2
            both = [
                0.75 * (group[at + 1] + group[at + 2]) + 0.25 * (group[at] + group[at + 3])
                for group in (cells, beside)
            ]
            where = pl.multiple_of((p + 1) * images * width + i * width, width)
            place(both[0], both[1], pooled.at[p], window, where)
        return carry

    lax.fori_loop(0, images, per_image, 0)
    line = images * width
    inner = (height - 2) * line
    rows = slice(2 * line, 2 * line + inner)
    for k in range(depths):
        for u in range(3):
            part = nt_dot(window[0, rows, :], weight[k, u, 0])
            part = part + nt_dot(window[1, rows, :], weight[k, u, 1])
            part = part + nt_dot(window[2, rows, :], weight[k, u, 2])
            if u == 0:
                acc[k, :inner, :] = part
                acc[k, inner:, :] = jnp.zeros((2 * line, channels), F32)
            else:
                acc[k, u * line : u * line + inner, :] += part


def edge_kernel(has_second, flags, *refs):
    sides = 2 if has_second else 1
    rows, (cells, beside, _, acc, weight) = refs[:sides], refs[sides : sides + 5]
    *grads, window, pooled, ends, total = refs[sides + 5 :]
    images, width = cells.shape[0], cells.shape[2]
    depths, count = acc.shape[:2]
    line = images * width
    height = count // line
    row_odd, top, bottom = flags[ROW_ODD] == 1, flags[TOP] == 1, flags[BOTTOM] == 1
    for n in range(sides):
        ends[n] = rows[n][2 * line :, :].astype(F32)
    pooled[...] = jnp.zeros_like(pooled)
    for i in range(images):
        for_rows = []
        for is_end, own in ((False, cells), (True, beside)):
            def came(from_above, n):
                def of(ref_at):
                    if is_end:
                        at = (2 * i + n) * 2
                        return ends[ref_at, at : at + 2, :]
                    at = (2 * i + n) * width
                    return rows[ref_at][at : at + width, :].astype(F32)

                first = of(0)
                second = of(1) if has_second else jnp.zeros_like(first)
                return jnp.where(row_odd, first, second) if from_above else jnp.where(row_odd, second, first)

            edge = [own[i, n] for n in range(6)]
            zero = jnp.zeros_like(edge[0])
            for_rows.append(
                [
                    jnp.where(top, zero, came(True, 0) + 0.25 * edge[0]),
                    0.75 * (edge[0] + edge[1]) + 0.25 * (jnp.where(top, edge[0], came(True, 1)) + edge[2]),
                    0.75 * (edge[4] + edge[5]) + 0.25 * (jnp.where(bottom, edge[5], came(False, 0)) + edge[3]),
                    jnp.where(bottom, zero, came(False, 1) + 0.25 * edge[5]),
                ]
            )
        for n, p in enumerate((0, 1, height, height + 1)):
            place(for_rows[0][n], for_rows[1][n], pooled.at[n], window, p * line + i * width)
    low, high = slice(0, 2 * line), slice(height * line, (height + 2) * line)
    for k in range(depths):
        total[...] = acc[k]
        for v in range(3):
            total[(height - 2) * line :, :] += nt_dot(window[v, high, :], weight[k, 0, v])
            total[: 2 * line, :] += nt_dot(window[v, low, :], weight[k, 2, v])
            middle = jnp.concatenate(
                [window[v, line : 2 * line, :], window[v, height * line : (height + 1) * line, :]], axis=0
            )
            part = nt_dot(middle, weight[k, 1, v])
            total[:line, :] += part[:line]
            total[(height - 1) * line :, :] += part[line:]
        for apart in range(2 * CHIPS):
            at = pl.multiple_of((flags[GRAY] ^ apart) * line, line)
            grads[apart // 2][apart % 2, k] = total[pl.ds(at, line), :].astype(BF16)


def deal(full, split_refs, core, turned):
    if len(split_refs) == 1:
        split_refs[0][...] = full[...]
        return
    kept, *sent = split_refs
    count, rows = kept.shape[:2]
    size = sent[0].shape[0]
    for j in range(count):
        p = (j & ~3 | (j & 1) << 1 | j >> 1 & 1) if turned else j
        kept[p] = full[pl.ds(pl.multiple_of((2 * j + core) * rows, 16), rows), :]
        sent[p // size][p % size] = full[pl.ds(pl.multiple_of((2 * j + 1 - core) * rows, 16), rows), :]


def conv_term_kernel(flags, window, saved, *refs):
    split_refs, top, full, flat = refs[:-3], refs[-3], refs[-2], refs[-1]
    images, depths, height, width, channels = saved.shape
    line = images * width
    count = height * line
    split = top.shape[0]
    for k in range(depths):
        for h in range(height):
            for i in range(images):
                at = (h * images + i) * width
                flat[at : at + width, :] = saved[i, k, h]
        flat_t = flat[...].T
        for n in range(9):
            start = (2 - n // 3) * line
            part = jnp.dot(
                flat_t, window[n % 3, start : start + count, :], preferred_element_type=F32
            ).astype(BF16)
            at = (k * 9 + n) * channels
            if at < split:
                top[at : at + channels, :] = part
            else:
                full[at - split : at - split + channels, :] = part
    deal(full, split_refs, flags[CORE], True)


def pass_on_kernel(*refs):
    for n, piece in enumerate(refs[:-1]):
        refs[-1][n] = piece[1]


def proj_term_kernel(flags, *refs):
    came, (passed, feats, conv_top) = refs[:CHIPS], refs[CHIPS : CHIPS + 3]
    split_refs, tokens, full = refs[CHIPS + 3 : -2], refs[-2], refs[-1]
    images, depths, _, dim = feats.shape
    line = passed.shape[2]
    width = line // images
    for apart in range(2 * CHIPS):
        column = column_of(flags[GRAY] ^ apart)
        for k in range(depths):
            for i in range(images):
                at = pl.multiple_of((i * TILE_COLS + column) * width, width)
                rows = slice(i * width, (i + 1) * width)
                piece = passed[apart // 2, k, rows, :] if apart % 2 else came[apart // 2][0, k, rows, :]
                tokens[k, pl.ds(at, width), :] = piece
    for k in range(depths):
        flat = feats[:, k].reshape(tokens.shape[1], dim)
        part = lax.dot_general(
            flat, tokens[k], (((0,), (0,)), ((), ())), preferred_element_type=F32
        )
        full[k * dim : (k + 1) * dim, :] = part.astype(BF16)
    full[depths * dim :, :] = conv_top[...]
    deal(full, split_refs, flags[CORE], False)


def feat_grad_kernel(tokens, weight, out):
    images, depths, count, dim = out.shape
    for k in range(depths):
        out[:, k] = nt_dot(tokens[k], weight[k]).astype(BF16).reshape(images, count, dim)


def take(part, block, at, columns=slice(None)):
    pieces, start = part
    size = pieces[0].shape[0]
    if len(pieces) > 1:
        return pieces[block // size][block % size + at, :, columns].astype(F32)
    return pieces[0][start + block + at, :, columns].astype(F32)


def regroup(refs, plan):
    refs, parts = list(refs), []
    for size, start in plan:
        parts.append((refs[:size], start))
        del refs[:size]
    return parts, refs


def round_kernel(jobs, places, flags, *refs):
    dp = flags[DP]
    work = []
    for plan, at, bits, by_columns in jobs:
        parts, refs = regroup(refs, plan)
        work.append((parts, at, bits, by_columns))
    for j, (parts, at, bits, by_columns) in enumerate(work):
        span = 1 << bits
        mine = 0
        for b in range(bits):
            mine = mine + flags[BITS + at + b] * (1 << b)
        for n in range(span * (2 if by_columns else 1)):
            across, apart = n // span, n % span
            index, start, count, cut = places[j, n]
            columns, width = slice(None), refs[index].shape[2]
            if by_columns:
                columns = pl.ds(pl.multiple_of((dp ^ across) * width, width), width)
            for q in range(count * cut):
                out = refs[index + q // count]
                total = take(parts[0], q * span, mine ^ apart, columns)
                for other in parts[1:]:
                    total = total + take(other, q * span, mine ^ apart, columns)
                out[start + q % count] = total.astype(out.dtype)


def last_kernel(early_plan, late_plan, flags, *refs):
    first = flags[DP] == 0
    sums = []
    for plan in (early_plan, late_plan):
        parts, refs = regroup(refs, plan)
        total = take(parts[0], 0, 0)
        for other in parts[1:]:
            total = total + take(other, 0, 0)
        sums.append(total)
    sent, kept = refs
    sent[...] = jnp.where(first, sums[0], sums[1]).astype(BF16)
    kept[...] = jnp.where(first, sums[1], sums[0])


def join_kernel(scale, flags, kept, came, out):
    width = kept.shape[1]
    at = pl.multiple_of(flags[DP] * width, width)
    out[:, pl.ds(at, width)] = kept[...] * scale
    at = pl.multiple_of((1 - flags[DP]) * width, width)
    out[:, pl.ds(at, width)] = came[...].astype(F32) * scale


def vmem_call(kernel, out_shape, operands, scratch=(), scalars=1, flops=0, limit=16, after=(), aliases=()):
    whole = pl.BlockSpec(memory_space=pltpu.VMEM)
    specs = [pl.BlockSpec(memory_space=pltpu.SMEM)] * scalars + [whole] * (len(operands) - scalars)
    specs += [pl.BlockSpec(memory_space=pl.ANY)] * len(after)
    count = len(operands)

    def run(*refs):
        kernel(*refs[:count], *refs[count + len(after) :])

    moved = sum(a.size * a.dtype.itemsize for a in operands)
    moved += sum(math.prod(s.shape) * s.dtype.itemsize for s in jax.tree.leaves(out_shape))
    return pl.pallas_call(
        run,
        out_shape=out_shape,
        in_specs=specs,
        out_specs=jax.tree.map(lambda _: whole, out_shape),
        scratch_shapes=list(scratch),
        input_output_aliases=dict(aliases),
        compiler_params=pltpu.CompilerParams(vmem_limit_bytes=limit << 20),
        cost_estimate=pl.CostEstimate(flops=flops, bytes_accessed=moved, transcendentals=0),
    )(*operands, *after)


def sds(*shape, dtype=BF16):
    return jax.ShapeDtypeStruct(shape, dtype)


def xor_move(block, apart, across):
    tiles = lax.axis_size("tile")
    if not across:
        return lax.ppermute(block, "tile", [(t, t ^ apart) for t in range(tiles)])
    if not apart:
        return lax.ppermute(block, "dp", [(0, 1), (1, 0)])
    route = [(d * tiles + t, (1 - d) * tiles + (t ^ apart)) for d in range(2) for t in range(tiles)]
    return lax.ppermute(block, ("dp", "tile"), route)


def core_sum(dealt, core, pieces, turned):
    if len(dealt) == 1:
        tiles = lax.axis_size("tile")
        rows, channels = dealt[0].shape[0] // tiles, dealt[0].shape[1]
        pairs = dealt[0].reshape(tiles // 2, 2, rows, channels)
        if turned:
            pairs = pairs.reshape(tiles // 8, 2, 2, 2, rows, channels).swapaxes(1, 2).reshape(pairs.shape)
        kept = lax.dynamic_index_in_dim(pairs, core, 1, keepdims=False)
        sent = lax.dynamic_index_in_dim(pairs, 1 - core, 1, keepdims=False)
        size = sent.shape[0] // pieces
        sent = [sent[n * size : (n + 1) * size] for n in range(pieces)]
    else:
        kept, *sent = dealt
    return [([kept], 0), ([xor_move(piece, 1, False) for piece in sent], 0)]


def flat(parts):
    return [piece for pieces, _ in parts for piece in pieces], [(len(pieces), start) for pieces, start in parts]


def deal_rounds(jobs, flags, after=(), cut=1):
    outs, plans, places, moves, operands = [], [], {}, {}, [flags]
    for j, (parts, at, bits, by_columns) in enumerate(jobs):
        span = 1 << bits
        count, rows, channels = parts[0][0][0].shape
        count, channels = count // span, channels // 2 if by_columns else channels
        for n in [0] + list(range(span * (2 if by_columns else 1) - 1, 0, -1)):
            move = (n % span) << at, n >= span
            if n == 0:
                outs.append(sds(count, rows, channels, dtype=F32))
                places[j, n] = len(outs) - 1, 0, count, 1
            elif move in moves:
                index = moves[move]
                places[j, n] = index, outs[index].shape[0], count, 1
                outs[index] = sds(outs[index].shape[0] + count, rows, channels)
            else:
                moves[move] = len(outs)
                places[j, n] = len(outs), 0, count // cut, cut
                outs += [sds(count // cut, rows, channels)] * cut
        pieces, plan = flat(parts)
        plans.append((plan, at, bits, by_columns))
        operands += pieces
    made = list(vmem_call(functools.partial(round_kernel, plans, places), outs, operands, after=after))
    token = made[0]
    for (apart, across), index in moves.items():
        for n in range(index, index + cut):
            made[n] = xor_move(made[n], apart, across)
    sums = []
    for j in range(len(jobs)):
        here = [places[key] for key in places if key[0] == j]
        sums.append([(made[index : index + pieces], start) for index, start, _, pieces in here])
    return sums, token


def per_device(features, proj_weight, conv_weight, saved, cotangent):
    position = lax.axis_index("tile")
    tile_count = lax.axis_size("tile")
    rows = tile_count // TILE_COLS
    gray = position % TILE_COLS
    col, row = column_of(gray), position // TILE_COLS
    images, height2, width2, channels = cotangent.shape
    depths, dim = proj_weight.shape[:2]
    height, width = height2 // 2, width2 // 2
    patches = images * height * width
    line = images * width
    tokens = features.shape[2]
    has_second = rows > 2
    sides = 2 if has_second else 1
    bits = tile_count.bit_length() - 1
    flags = jnp.stack(
        [row % 2, col % 2, row == 0, row == rows - 1, col == 0, col == TILE_COLS - 1]
        + [position % 2, lax.axis_index("dp"), gray]
        + [position >> b & 1 for b in range(bits)]
    ).astype(jnp.int32)

    def swap(block, row_pairs, col_pairs):
        return lax.ppermute(block, "tile", tile_route(row_pairs, col_pairs, rows))

    low, high = cotangent[:, :, :HALO], cotangent[:, :, width2 - HALO :]
    around = paired(TILE_COLS, 1) + [(0, TILE_COLS - 1), (TILE_COLS - 1, 0)]
    col_b = swap(jnp.where(col % 2 == 1, high, low), None, around)
    col_a = swap(jnp.where(col % 2 == 1, low, high), None, paired(TILE_COLS, 0))
    centre = vmem_call(
        centre_kernel,
        sds(images, height2, width + 8, channels, dtype=F32),
        (cotangent,),
        scratch=(pltpu.VMEM((channels // 128, height2, LEFT + width2 + 8, 128), F32),),
        scalars=0,
    )
    *row_out, cells, beside = vmem_call(
        functools.partial(row_pack_kernel, has_second),
        [sds(2 * images * (width + 2), channels)] * sides
        + [sds(images, 6, width, channels, dtype=F32), sds(images, 6, 2, channels, dtype=F32)],
        (flags, centre, col_a, col_b),
        scratch=(pltpu.VMEM((sides, 4 * images, channels), F32),),
    )
    came_rows = [swap(row_out[n], paired(rows, n), None) for n in range(sides)]
    conv_flops = 2 * patches * depths * 9 * channels * channels
    window, acc = vmem_call(
        main_kernel,
        [sds(3, (height + 2) * line, channels), sds(depths, patches, channels, dtype=F32)],
        (flags, centre, col_a, col_b, conv_weight),
        scratch=(pltpu.VMEM((height, LEFT + width + 8, channels), F32),),
        flops=conv_flops,
        after=(row_out[0],),
    )
    *grads, window = vmem_call(
        functools.partial(edge_kernel, has_second),
        [sds(2, depths, line, channels)] * CHIPS + [sds(3, (height + 2) * line, channels)],
        [flags] + came_rows + [cells, beside, window, acc, conv_weight],
        scratch=(
            pltpu.VMEM((4, LEFT + width + 8, channels), F32),
            pltpu.VMEM((sides, 4 * images, channels), F32),
            pltpu.VMEM((patches, channels), F32),
        ),
        flops=conv_flops // 4,
        aliases={sides + 3: CHIPS},
    )
    came = [xor_move(grads[chip], 2 * chip, False) for chip in range(CHIPS - 1, 0, -1)]
    came = [grads[0]] + came[::-1]
    to_pass = vmem_call(pass_on_kernel, sds(CHIPS, depths, line, channels), came, scalars=0)
    passed = xor_move(to_pass, 1, False)

    half_rows = depths * (dim + 9 * channels) // 2
    conv_late = half_rows - depths * dim
    block_rows = half_rows // tile_count
    pieces = 4
    if block_rows % 16:
        dealt = [sds(half_rows, channels)]
    else:
        dealt = [sds(tile_count // 2, block_rows, channels)]
        dealt += [sds(tile_count // 2 // pieces, block_rows, channels)] * pieces
    full = pltpu.VMEM((half_rows, channels), BF16)
    *early, conv_top = vmem_call(
        conv_term_kernel,
        dealt + [sds(conv_late, channels)],
        (flags, window, saved),
        scratch=(full, pltpu.VMEM((patches, channels), BF16)),
        flops=conv_flops,
    )
    (early_parts,), before = deal_rounds([(core_sum(early, position % 2, pieces, True), 1, 0, True)], flags)
    proj_flops = 2 * images * tokens * depths * dim * channels
    *terms, token_grad = vmem_call(
        proj_term_kernel,
        dealt + [sds(depths, images * tokens, channels)],
        [flags] + came + [passed, features, conv_top],
        scratch=(full,),
        flops=proj_flops,
        after=(before,),
    )
    (late_parts,), before = deal_rounds(
        [(core_sum(terms, position % 2, pieces, False), 1, 1, False)], flags, after=(token_grad,), cut=2
    )
    (early_parts,), before = deal_rounds([(early_parts, 2, 1, False)], flags, after=(before,))
    (late_parts,), before = deal_rounds([(late_parts, 1, 0, True)], flags, after=(before,))
    (early_parts,), before = deal_rounds([(early_parts, 1, 1, False)], flags, after=(before,))
    at = 2
    while at < bits:
        step = min(2, bits - at)
        if at > 2 and step == 2:
            (early_parts,), before = deal_rounds([(early_parts, at, 1, False)], flags, after=(before,))
        (late_parts, early_parts), before = deal_rounds(
            [(late_parts, at, step, False), (early_parts, at + step - 1, 1, False)], flags, after=(before,)
        )
        at += step
    feature_grad = vmem_call(
        feat_grad_kernel,
        sds(images, depths, tokens, dim),
        (token_grad, proj_weight),
        scalars=0,
        flops=proj_flops,
        after=(before,),
    )
    early_pieces, early_plan = flat(early_parts)
    late_pieces, late_plan = flat(late_parts)
    sent, kept = vmem_call(
        functools.partial(last_kernel, early_plan, late_plan),
        [sds(block_rows, channels // 2), sds(block_rows, channels // 2, dtype=F32)],
        [flags] + early_pieces + late_pieces,
    )
    other = xor_move(sent, 0, True)
    scale = 1.0 / math.sqrt(images * lax.axis_size("dp") * tokens * tile_count)
    head_grad = vmem_call(
        functools.partial(join_kernel, scale), sds(block_rows, channels, dtype=F32), (flags, kept, other)
    )
    return feature_grad, head_grad


def solution(mesh):
    in_specs = (
        P("dp", None, "tile", None),
        P(),
        P(),
        P("dp", None, "tile", None, None),
        P("dp", "tile", None, None),
    )
    out_specs = (P("dp", None, "tile", None), P(("dp", "tile"), None))
    return jax.shard_map(
        per_device, mesh=mesh, in_specs=in_specs, out_specs=out_specs, check_vma=False
    )
```

```python
import functools
import math

import jax
import jax.numpy as jnp
from jax import lax
from jax.experimental import pallas as pl
from jax.experimental.pallas import tpu as pltpu
from jax.sharding import PartitionSpec as P

TILE_COLS = 8
HALO = 4
LEFT = 8
BF16 = jnp.bfloat16
F32 = jnp.float32
ROW_ODD, COL_ODD, TOP, BOTTOM, LEFT_END, RIGHT_END, CORE, DP, GRAY, BITS = range(10)
CHIPS = TILE_COLS // 2


def gray_of(column):
    return column ^ column >> 1


def column_of(code):
    return code ^ code >> 1 ^ code >> 2


def paired(count, first):
    pairs = []
    for low in range(first, count - 1, 2):
        pairs += [(low, low + 1), (low + 1, low)]
    return pairs


def tile_route(row_pairs, col_pairs, rows):
    row_moves = row_pairs if row_pairs is not None else [(r, r) for r in range(rows)]
    col_moves = col_pairs if col_pairs is not None else [(c, c) for c in range(TILE_COLS)]
    return [
        (r0 * TILE_COLS + gray_of(c0), r1 * TILE_COLS + gray_of(c1))
        for r0, r1 in row_moves
        for c0, c1 in col_moves
    ]


def nt_dot(left, right):
    return lax.dot_general(left, right, (((1,), (1,)), ((), ())), preferred_element_type=F32)


def centre_kernel(cot, pooled, wide):
    images, height2, width2, channels = cot.shape
    width = width2 // 2
    wide[...] = jnp.zeros_like(wide)

    def per_image(i, carry):
        for r in range(height2):
            value = cot[i, r].astype(F32)
            for h in range(channels // 128):
                wide[h, r, LEFT : LEFT + width2, :] = value[:, h * 128 : (h + 1) * 128]
            pooled[i, r, width : width + 1, :] = value[:1]
            pooled[i, r, width + 1 : width + 2, :] = value[width2 - 1 :]
        for r in range(height2):
            for h in range(channels // 128):
                taps = [wide[h, r, pl.ds(LEFT - 1 + n, width, stride=2), :] for n in range(4)]
                pooled[i, r, :width, h * 128 : (h + 1) * 128] = 0.75 * (taps[1] + taps[2]) + 0.25 * (taps[0] + taps[3])
        return carry

    lax.fori_loop(0, images, per_image, 0)


def pool_columns(flags, centre, col_a, col_b, i, lines):
    width, channels = centre.shape[2] - 8, centre.shape[3]
    col_odd, left, right = flags[COL_ODD] == 1, flags[LEFT_END] == 1, flags[RIGHT_END] == 1
    cell = lax.broadcasted_iota(jnp.int32, (width, channels), 0)
    is_first, is_last = cell == 0, cell == width - 1
    cells, beside = [], []
    for r in lines:
        own_first, own_last = centre[i, r, width : width + 1, :], centre[i, r, width + 1 : width + 2, :]
        one, two = col_a[i, r].astype(F32), col_b[i, r].astype(F32)
        before, after = jnp.where(col_odd, one, two), jnp.where(col_odd, two, one)
        near_before = jnp.where(left, own_first, before[3:4])
        near_after = jnp.where(right, own_last, after[0:1])
        cells.append(
            centre[i, r, :width, :] + 0.25 * (jnp.where(is_first, near_before, 0.0) + jnp.where(is_last, near_after, 0.0))
        )
        first = 0.75 * (before[2:3] + before[3:4]) + 0.25 * (before[1:2] + own_first)
        last = 0.75 * (after[0:1] + after[1:2]) + 0.25 * (own_last + after[2:3])
        beside.append(
            jnp.concatenate([jnp.where(left, 0.0, first), jnp.where(right, 0.0, last)], axis=0)
        )
    return cells, beside


def place(cells, beside, pooled, window, at):
    width = cells.shape[0]
    pooled[LEFT : LEFT + width, :] = cells
    pooled[LEFT - 1 : LEFT, :] = beside[:1]
    pooled[LEFT + width : LEFT + width + 1, :] = beside[1:]
    for v in range(3):
        window[v, pl.ds(at, width), :] = pooled[pl.ds(LEFT + 1 - v, width), :].astype(BF16)


def row_pack_kernel(has_second, flags, centre, col_a, col_b, *refs):
    outs, (cells_out, beside_out, ends) = refs[: 2 if has_second else 1], refs[-3:]
    images, height2, width = centre.shape[0], centre.shape[1], centre.shape[2] - 8
    row_odd = flags[ROW_ODD] == 1
    lines = [0, 1, 2, height2 - 3, height2 - 2, height2 - 1]
    for i in range(images):
        cells, beside = pool_columns(flags, centre, col_a, col_b, i, lines)
        for n in range(6):
            cells_out[i, n] = cells[n]
            beside_out[i, n] = beside[n]
        for group, is_end in ((cells, False), (beside, True)):
            above = [group[0], 0.75 * (group[0] + group[1]) + 0.25 * group[2]]
            below = [0.25 * group[3] + 0.75 * (group[4] + group[5]), group[5]]
            for second in range(len(outs)):
                for n in range(2):
                    odd, even = (below[n], above[n]) if second else (above[n], below[n])
                    value = jnp.where(row_odd, odd, even)
                    if is_end:
                        ends[second, (2 * i + n) * 2 : (2 * i + n) * 2 + 2, :] = value
                    else:
                        at = (2 * i + n) * width
                        outs[second][at : at + width, :] = value.astype(BF16)
    for second in range(len(outs)):
        outs[second][2 * images * width :, :] = ends[second].astype(BF16)


def main_kernel(flags, centre, col_a, col_b, weight, window, acc, pooled):
    images, height2, width, channels = centre.shape[0], centre.shape[1], centre.shape[2] - 8, centre.shape[3]
    height, depths = height2 // 2, weight.shape[0]
    pooled[...] = jnp.zeros_like(pooled)

    def per_image(i, carry):
        cells, beside = pool_columns(flags, centre, col_a, col_b, i, range(1, height2 - 1))
        for p in range(1, height - 1):
            at = 2 * p - 2
            both = [
                0.75 * (group[at + 1] + group[at + 2]) + 0.25 * (group[at] + group[at + 3])
                for group in (cells, beside)
            ]
            where = pl.multiple_of((p + 1) * images * width + i * width, width)
            place(both[0], both[1], pooled.at[p], window, where)
        return carry

    lax.fori_loop(0, images, per_image, 0)
    line = images * width
    inner = (height - 2) * line
    rows = slice(2 * line, 2 * line + inner)
    for k in range(depths):
        for u in range(3):
            part = nt_dot(window[0, rows, :], weight[k, u, 0])
            part = part + nt_dot(window[1, rows, :], weight[k, u, 1])
            part = part + nt_dot(window[2, rows, :], weight[k, u, 2])
            if u == 0:
                acc[k, :inner, :] = part
                acc[k, inner:, :] = jnp.zeros((2 * line, channels), F32)
            else:
                acc[k, u * line : u * line + inner, :] += part


def edge_kernel(has_second, flags, *refs):
    sides = 2 if has_second else 1
    rows, (cells, beside, _, acc, weight) = refs[:sides], refs[sides : sides + 5]
    *grads, window, pooled, ends, total = refs[sides + 5 :]
    images, width = cells.shape[0], cells.shape[2]
    depths, count = acc.shape[:2]
    line = images * width
    height = count // line
    row_odd, top, bottom = flags[ROW_ODD] == 1, flags[TOP] == 1, flags[BOTTOM] == 1
    for n in range(sides):
        ends[n] = rows[n][2 * line :, :].astype(F32)
    pooled[...] = jnp.zeros_like(pooled)
    for i in range(images):
        for_rows = []
        for is_end, own in ((False, cells), (True, beside)):
            def came(from_above, n):
                def of(ref_at):
                    if is_end:
                        at = (2 * i + n) * 2
                        return ends[ref_at, at : at + 2, :]
                    at = (2 * i + n) * width
                    return rows[ref_at][at : at + width, :].astype(F32)

                first = of(0)
                second = of(1) if has_second else jnp.zeros_like(first)
                return jnp.where(row_odd, first, second) if from_above else jnp.where(row_odd, second, first)

            edge = [own[i, n] for n in range(6)]
            zero = jnp.zeros_like(edge[0])
            for_rows.append(
                [
                    jnp.where(top, zero, came(True, 0) + 0.25 * edge[0]),
                    0.75 * (edge[0] + edge[1]) + 0.25 * (jnp.where(top, edge[0], came(True, 1)) + edge[2]),
                    0.75 * (edge[4] + edge[5]) + 0.25 * (jnp.where(bottom, edge[5], came(False, 0)) + edge[3]),
                    jnp.where(bottom, zero, came(False, 1) + 0.25 * edge[5]),
                ]
            )
        for n, p in enumerate((0, 1, height, height + 1)):
            place(for_rows[0][n], for_rows[1][n], pooled.at[n], window, p * line + i * width)
    low, high = slice(0, 2 * line), slice(height * line, (height + 2) * line)
    for k in range(depths):
        total[...] = acc[k]
        for v in range(3):
            total[(height - 2) * line :, :] += nt_dot(window[v, high, :], weight[k, 0, v])
            total[: 2 * line, :] += nt_dot(window[v, low, :], weight[k, 2, v])
            middle = jnp.concatenate(
                [window[v, line : 2 * line, :], window[v, height * line : (height + 1) * line, :]], axis=0
            )
            part = nt_dot(middle, weight[k, 1, v])
            total[:line, :] += part[:line]
            total[(height - 1) * line :, :] += part[line:]
        for apart in range(2 * CHIPS):
            at = pl.multiple_of((flags[GRAY] ^ apart) * line, line)
            grads[apart // 2][apart % 2, k] = total[pl.ds(at, line), :].astype(BF16)


def deal(full, split_refs, core, turned):
    if len(split_refs) == 1:
        split_refs[0][...] = full[...]
        return
    kept, *sent = split_refs
    count, rows = kept.shape[:2]
    size = sent[0].shape[0]
    for j in range(count):
        p = (j & ~3 | (j & 1) << 1 | j >> 1 & 1) if turned else j
        kept[p] = full[pl.ds(pl.multiple_of((2 * j + core) * rows, 16), rows), :]
        sent[p // size][p % size] = full[pl.ds(pl.multiple_of((2 * j + 1 - core) * rows, 16), rows), :]


def conv_term_kernel(flags, window, saved, *refs):
    split_refs, top, full, flat = refs[:-3], refs[-3], refs[-2], refs[-1]
    images, depths, height, width, channels = saved.shape
    line = images * width
    count = height * line
    split = top.shape[0]
    for k in range(depths):
        for h in range(height):
            for i in range(images):
                at = (h * images + i) * width
                flat[at : at + width, :] = saved[i, k, h]
        flat_t = flat[...].T
        for n in range(9):
            start = (2 - n // 3) * line
            part = jnp.dot(
                flat_t, window[n % 3, start : start + count, :], preferred_element_type=F32
            ).astype(BF16)
            at = (k * 9 + n) * channels
            if at < split:
                top[at : at + channels, :] = part
            else:
                full[at - split : at - split + channels, :] = part
    deal(full, split_refs, flags[CORE], True)


def pass_on_kernel(*refs):
    for n, piece in enumerate(refs[:-1]):
        refs[-1][n] = piece[1]


def proj_term_kernel(flags, *refs):
    came, (passed, feats, conv_top) = refs[:CHIPS], refs[CHIPS : CHIPS + 3]
    split_refs, tokens, full = refs[CHIPS + 3 : -2], refs[-2], refs[-1]
    images, depths, _, dim = feats.shape
    line = passed.shape[2]
    width = line // images
    for apart in range(2 * CHIPS):
        column = column_of(flags[GRAY] ^ apart)
        for k in range(depths):
            for i in range(images):
                at = pl.multiple_of((i * TILE_COLS + column) * width, width)
                rows = slice(i * width, (i + 1) * width)
                piece = passed[apart // 2, k, rows, :] if apart % 2 else came[apart // 2][0, k, rows, :]
                tokens[k, pl.ds(at, width), :] = piece
    for k in range(depths):
        flat = feats[:, k].reshape(tokens.shape[1], dim)
        part = lax.dot_general(
            flat, tokens[k], (((0,), (0,)), ((), ())), preferred_element_type=F32
        )
        full[k * dim : (k + 1) * dim, :] = part.astype(BF16)
    full[depths * dim :, :] = conv_top[...]
    deal(full, split_refs, flags[CORE], False)


def feat_grad_kernel(tokens, weight, out):
    images, depths, count, dim = out.shape
    for k in range(depths):
        out[:, k] = nt_dot(tokens[k], weight[k]).astype(BF16).reshape(images, count, dim)


def take(part, block, at, columns=slice(None), span=1):
    pieces, start = part
    size = pieces[0].shape[0]
    if len(pieces) == 1:
        return pieces[0][start + block + at, :, columns].astype(F32)
    if span <= size:
        return pieces[block // size][block % size + at, :, columns].astype(F32)
    first = block // size
    inside = at & size - 1
    value = pieces[first][inside, :, columns].astype(F32)
    for n in range(1, span // size):
        value = jnp.where(at >= n * size, pieces[first + n][inside, :, columns].astype(F32), value)
    return value


def regroup(refs, plan):
    refs, parts = list(refs), []
    for size, start in plan:
        parts.append((refs[:size], start))
        del refs[:size]
    return parts, refs


def round_kernel(jobs, places, flags, *refs):
    dp = flags[DP]
    work = []
    for plan, at, bits, by_columns in jobs:
        parts, refs = regroup(refs, plan)
        work.append((parts, at, bits, by_columns))
    for j, (parts, at, bits, by_columns) in enumerate(work):
        span = 1 << bits
        mine = 0
        for b in range(bits):
            mine = mine + flags[BITS + at + b] * (1 << b)
        for n in range(span * (2 if by_columns else 1)):
            across, apart = n // span, n % span
            index, start, count, cut = places[j, n]
            columns, width = slice(None), refs[index].shape[2]
            if by_columns:
                columns = pl.ds(pl.multiple_of((dp ^ across) * width, width), width)
            for q in range(count * cut):
                out = refs[index + q // count]
                total = take(parts[0], q * span, mine ^ apart, columns, span)
                for other in parts[1:]:
                    total = total + take(other, q * span, mine ^ apart, columns, span)
                out[start + q % count] = total.astype(out.dtype)


def last_kernel(early_plan, late_plan, flags, *refs):
    first = flags[DP] == 0
    sums = []
    for plan in (early_plan, late_plan):
        parts, refs = regroup(refs, plan)
        total = take(parts[0], 0, 0)
        for other in parts[1:]:
            total = total + take(other, 0, 0)
        sums.append(total)
    sent, kept = refs
    sent[...] = jnp.where(first, sums[0], sums[1]).astype(BF16)
    kept[...] = jnp.where(first, sums[1], sums[0])


def join_kernel(scale, flags, kept, came, out):
    width = kept.shape[1]
    at = pl.multiple_of(flags[DP] * width, width)
    out[:, pl.ds(at, width)] = kept[...] * scale
    at = pl.multiple_of((1 - flags[DP]) * width, width)
    out[:, pl.ds(at, width)] = came[...].astype(F32) * scale


def vmem_call(kernel, out_shape, operands, scratch=(), scalars=1, flops=0, limit=16, after=(), aliases=()):
    whole = pl.BlockSpec(memory_space=pltpu.VMEM)
    specs = [pl.BlockSpec(memory_space=pltpu.SMEM)] * scalars + [whole] * (len(operands) - scalars)
    specs += [pl.BlockSpec(memory_space=pl.ANY)] * len(after)
    count = len(operands)

    def run(*refs):
        kernel(*refs[:count], *refs[count + len(after) :])

    moved = sum(a.size * a.dtype.itemsize for a in operands)
    moved += sum(math.prod(s.shape) * s.dtype.itemsize for s in jax.tree.leaves(out_shape))
    return pl.pallas_call(
        run,
        out_shape=out_shape,
        in_specs=specs,
        out_specs=jax.tree.map(lambda _: whole, out_shape),
        scratch_shapes=list(scratch),
        input_output_aliases=dict(aliases),
        compiler_params=pltpu.CompilerParams(vmem_limit_bytes=limit << 20),
        cost_estimate=pl.CostEstimate(flops=flops, bytes_accessed=moved, transcendentals=0),
    )(*operands, *after)


def sds(*shape, dtype=BF16):
    return jax.ShapeDtypeStruct(shape, dtype)


def xor_move(block, apart, across):
    tiles = lax.axis_size("tile")
    if not across:
        return lax.ppermute(block, "tile", [(t, t ^ apart) for t in range(tiles)])
    if not apart:
        return lax.ppermute(block, "dp", [(0, 1), (1, 0)])
    route = [(d * tiles + t, (1 - d) * tiles + (t ^ apart)) for d in range(2) for t in range(tiles)]
    return lax.ppermute(block, ("dp", "tile"), route)


def core_sum(dealt, core, pieces, turned):
    if len(dealt) == 1:
        tiles = lax.axis_size("tile")
        rows, channels = dealt[0].shape[0] // tiles, dealt[0].shape[1]
        pairs = dealt[0].reshape(tiles // 2, 2, rows, channels)
        if turned:
            pairs = pairs.reshape(tiles // 8, 2, 2, 2, rows, channels).swapaxes(1, 2).reshape(pairs.shape)
        kept = lax.dynamic_index_in_dim(pairs, core, 1, keepdims=False)
        sent = lax.dynamic_index_in_dim(pairs, 1 - core, 1, keepdims=False)
        size = sent.shape[0] // pieces
        sent = [sent[n * size : (n + 1) * size] for n in range(pieces)]
    else:
        kept, *sent = dealt
    return [([kept], 0), ([xor_move(piece, 1, False) for piece in sent], 0)]


def flat(parts):
    return [piece for pieces, _ in parts for piece in pieces], [(len(pieces), start) for pieces, start in parts]


def deal_rounds(jobs, flags, after=(), cut=1):
    outs, plans, places, moves, operands = [], [], {}, {}, [flags]
    for j, (parts, at, bits, by_columns) in enumerate(jobs):
        span = 1 << bits
        rows, channels = parts[0][0][0].shape[1:]
        count = min(sum(piece.shape[0] for piece in pieces) for pieces, _ in parts)
        count, channels = count // span, channels // 2 if by_columns else channels
        for n in [0] + list(range(span * (2 if by_columns else 1) - 1, 0, -1)):
            move = (n % span) << at, n >= span
            if n == 0:
                outs.append(sds(count, rows, channels, dtype=F32))
                places[j, n] = len(outs) - 1, 0, count, 1
            elif move in moves:
                index = moves[move]
                places[j, n] = index, outs[index].shape[0], count, 1
                outs[index] = sds(outs[index].shape[0] + count, rows, channels)
            else:
                moves[move] = len(outs)
                places[j, n] = len(outs), 0, count // cut, cut
                outs += [sds(count // cut, rows, channels)] * cut
        pieces, plan = flat(parts)
        plans.append((plan, at, bits, by_columns))
        operands += pieces
    made = list(vmem_call(functools.partial(round_kernel, plans, places), outs, operands, after=after))
    token = made[0]
    for (apart, across), index in moves.items():
        for n in range(index, index + cut):
            made[n] = xor_move(made[n], apart, across)
    sums = []
    for j in range(len(jobs)):
        here = [places[key] for key in places if key[0] == j]
        sums.append([(made[index : index + pieces], start) for index, start, _, pieces in here])
    return sums, token


def per_device(features, proj_weight, conv_weight, saved, cotangent):
    position = lax.axis_index("tile")
    tile_count = lax.axis_size("tile")
    rows = tile_count // TILE_COLS
    gray = position % TILE_COLS
    col, row = column_of(gray), position // TILE_COLS
    images, height2, width2, channels = cotangent.shape
    depths, dim = proj_weight.shape[:2]
    height, width = height2 // 2, width2 // 2
    patches = images * height * width
    line = images * width
    tokens = features.shape[2]
    has_second = rows > 2
    sides = 2 if has_second else 1
    bits = tile_count.bit_length() - 1
    flags = jnp.stack(
        [row % 2, col % 2, row == 0, row == rows - 1, col == 0, col == TILE_COLS - 1]
        + [position % 2, lax.axis_index("dp"), gray]
        + [position >> b & 1 for b in range(bits)]
    ).astype(jnp.int32)

    def swap(block, row_pairs, col_pairs):
        return lax.ppermute(block, "tile", tile_route(row_pairs, col_pairs, rows))

    low, high = cotangent[:, :, :HALO], cotangent[:, :, width2 - HALO :]
    around = paired(TILE_COLS, 1) + [(0, TILE_COLS - 1), (TILE_COLS - 1, 0)]
    col_b = swap(jnp.where(col % 2 == 1, high, low), None, around)
    col_a = swap(jnp.where(col % 2 == 1, low, high), None, paired(TILE_COLS, 0))
    centre = vmem_call(
        centre_kernel,
        sds(images, height2, width + 8, channels, dtype=F32),
        (cotangent,),
        scratch=(pltpu.VMEM((channels // 128, height2, LEFT + width2 + 8, 128), F32),),
        scalars=0,
    )
    *row_out, cells, beside = vmem_call(
        functools.partial(row_pack_kernel, has_second),
        [sds(2 * images * (width + 2), channels)] * sides
        + [sds(images, 6, width, channels, dtype=F32), sds(images, 6, 2, channels, dtype=F32)],
        (flags, centre, col_a, col_b),
        scratch=(pltpu.VMEM((sides, 4 * images, channels), F32),),
    )
    came_rows = [swap(row_out[n], paired(rows, n), None) for n in range(sides)]
    conv_flops = 2 * patches * depths * 9 * channels * channels
    window, acc = vmem_call(
        main_kernel,
        [sds(3, (height + 2) * line, channels), sds(depths, patches, channels, dtype=F32)],
        (flags, centre, col_a, col_b, conv_weight),
        scratch=(pltpu.VMEM((height, LEFT + width + 8, channels), F32),),
        flops=conv_flops,
        after=(row_out[0],),
    )
    *grads, window = vmem_call(
        functools.partial(edge_kernel, has_second),
        [sds(2, depths, line, channels)] * CHIPS + [sds(3, (height + 2) * line, channels)],
        [flags] + came_rows + [cells, beside, window, acc, conv_weight],
        scratch=(
            pltpu.VMEM((4, LEFT + width + 8, channels), F32),
            pltpu.VMEM((sides, 4 * images, channels), F32),
            pltpu.VMEM((patches, channels), F32),
        ),
        flops=conv_flops // 4,
        aliases={sides + 3: CHIPS},
    )
    came = [xor_move(grads[chip], 2 * chip, False) for chip in range(CHIPS - 1, 0, -1)]
    came = [grads[0]] + came[::-1]
    to_pass = vmem_call(pass_on_kernel, sds(CHIPS, depths, line, channels), came, scalars=0)
    passed = xor_move(to_pass, 1, False)

    half_rows = depths * (dim + 9 * channels) // 2
    conv_late = half_rows - depths * dim
    block_rows = half_rows // tile_count
    pieces = 4
    if block_rows % 16:
        dealt = [sds(half_rows, channels)]
    else:
        dealt = [sds(tile_count // 2, block_rows, channels)]
        dealt += [sds(tile_count // 2 // pieces, block_rows, channels)] * pieces
    full = pltpu.VMEM((half_rows, channels), BF16)
    *early, conv_top = vmem_call(
        conv_term_kernel,
        dealt + [sds(conv_late, channels)],
        (flags, window, saved),
        scratch=(full, pltpu.VMEM((patches, channels), BF16)),
        flops=conv_flops,
    )
    (early_parts,), before = deal_rounds([(core_sum(early, position % 2, pieces, True), 1, 0, True)], flags)
    proj_flops = 2 * images * tokens * depths * dim * channels
    *terms, token_grad = vmem_call(
        proj_term_kernel,
        dealt + [sds(depths, images * tokens, channels)],
        [flags] + came + [passed, features, conv_top],
        scratch=(full,),
        flops=proj_flops,
        after=(before,),
    )
    (late_parts,), before = deal_rounds(
        [(core_sum(terms, position % 2, pieces, False), 1, 1, False)], flags, after=(token_grad,), cut=2
    )
    own, came_late = late_parts[0][0][0], late_parts[1][0]
    (early_parts,), before = deal_rounds([(early_parts, 2, 1, False)], flags, after=(before,))
    halves = []
    for n in range(2):
        half = [([came_late[n]], 0), ([own], n * (own.shape[0] // 2))]
        waits = (before,) + tuple(halves[0][1][0] if halves else ())
        (dealt_half,), before = deal_rounds([(half, 1, 0, True)], flags, after=waits)
        halves.append(dealt_half)
    (early_parts,), before = deal_rounds([(early_parts, 1, 1, False)], flags, after=(before,))
    late_parts = [([half[n][0][0] for half in halves], 0) for n in range(2)]
    at = 2
    while at < bits:
        step = min(2, bits - at)
        (late_parts,), before = deal_rounds([(late_parts, at, step, False)], flags, after=(before,))
        for bit in range(max(at, 3), at + step):
            (early_parts,), before = deal_rounds([(early_parts, bit, 1, False)], flags, after=(before,))
        at += step
    feature_grad = vmem_call(
        feat_grad_kernel,
        sds(images, depths, tokens, dim),
        (token_grad, proj_weight),
        scalars=0,
        flops=proj_flops,
        after=(before,),
    )
    early_pieces, early_plan = flat(early_parts)
    late_pieces, late_plan = flat(late_parts)
    sent, kept = vmem_call(
        functools.partial(last_kernel, early_plan, late_plan),
        [sds(block_rows, channels // 2), sds(block_rows, channels // 2, dtype=F32)],
        [flags] + early_pieces + late_pieces,
    )
    other = xor_move(sent, 0, True)
    scale = 1.0 / math.sqrt(images * lax.axis_size("dp") * tokens * tile_count)
    head_grad = vmem_call(
        functools.partial(join_kernel, scale), sds(block_rows, channels, dtype=F32), (flags, kept, other)
    )
    return feature_grad, head_grad


def solution(mesh):
    in_specs = (
        P("dp", None, "tile", None),
        P(),
        P(),
        P("dp", None, "tile", None, None),
        P("dp", "tile", None, None),
    )
    out_specs = (P("dp", None, "tile", None), P(("dp", "tile"), None))
    return jax.shard_map(
        per_device, mesh=mesh, in_specs=in_specs, out_specs=out_specs, check_vma=False
    )
```

```python
import functools
import math

import jax
import jax.numpy as jnp
from jax import lax
from jax.experimental import pallas as pl
from jax.experimental.pallas import tpu as pltpu
from jax.sharding import PartitionSpec as P

TILE_COLS = 8
HALO = 4
LEFT = 8
BF16 = jnp.bfloat16
F32 = jnp.float32
ROW_ODD, COL_ODD, TOP, BOTTOM, LEFT_END, RIGHT_END, CORE, DP, GRAY, BITS = range(10)
CHIPS = TILE_COLS // 2


def gray_of(column):
    return column ^ column >> 1


def column_of(code):
    return code ^ code >> 1 ^ code >> 2


def paired(count, first):
    pairs = []
    for low in range(first, count - 1, 2):
        pairs += [(low, low + 1), (low + 1, low)]
    return pairs


def tile_route(row_pairs, col_pairs, rows):
    row_moves = row_pairs if row_pairs is not None else [(r, r) for r in range(rows)]
    col_moves = col_pairs if col_pairs is not None else [(c, c) for c in range(TILE_COLS)]
    return [
        (r0 * TILE_COLS + gray_of(c0), r1 * TILE_COLS + gray_of(c1))
        for r0, r1 in row_moves
        for c0, c1 in col_moves
    ]


def nt_dot(left, right):
    return lax.dot_general(left, right, (((1,), (1,)), ((), ())), preferred_element_type=F32)


def centre_kernel(cot, pooled, wide):
    images, height2, width2, channels = cot.shape
    width = width2 // 2
    wide[...] = jnp.zeros_like(wide)

    def per_image(i, carry):
        for r in range(height2):
            value = cot[i, r].astype(F32)
            for h in range(channels // 128):
                wide[h, r, LEFT : LEFT + width2, :] = value[:, h * 128 : (h + 1) * 128]
            pooled[i, r, width : width + 1, :] = value[:1]
            pooled[i, r, width + 1 : width + 2, :] = value[width2 - 1 :]
        for r in range(height2):
            for h in range(channels // 128):
                taps = [wide[h, r, pl.ds(LEFT - 1 + n, width, stride=2), :] for n in range(4)]
                pooled[i, r, :width, h * 128 : (h + 1) * 128] = 0.75 * (taps[1] + taps[2]) + 0.25 * (taps[0] + taps[3])
        return carry

    lax.fori_loop(0, images, per_image, 0)


def pool_columns(flags, centre, col_a, col_b, i, lines):
    width, channels = centre.shape[2] - 8, centre.shape[3]
    col_odd, left, right = flags[COL_ODD] == 1, flags[LEFT_END] == 1, flags[RIGHT_END] == 1
    cell = lax.broadcasted_iota(jnp.int32, (width, channels), 0)
    is_first, is_last = cell == 0, cell == width - 1
    cells, beside = [], []
    for r in lines:
        own_first, own_last = centre[i, r, width : width + 1, :], centre[i, r, width + 1 : width + 2, :]
        one, two = col_a[i, r].astype(F32), col_b[i, r].astype(F32)
        before, after = jnp.where(col_odd, one, two), jnp.where(col_odd, two, one)
        near_before = jnp.where(left, own_first, before[3:4])
        near_after = jnp.where(right, own_last, after[0:1])
        cells.append(
            centre[i, r, :width, :] + 0.25 * (jnp.where(is_first, near_before, 0.0) + jnp.where(is_last, near_after, 0.0))
        )
        first = 0.75 * (before[2:3] + before[3:4]) + 0.25 * (before[1:2] + own_first)
        last = 0.75 * (after[0:1] + after[1:2]) + 0.25 * (own_last + after[2:3])
        beside.append(
            jnp.concatenate([jnp.where(left, 0.0, first), jnp.where(right, 0.0, last)], axis=0)
        )
    return cells, beside


def place(cells, beside, pooled, window, at):
    width = cells.shape[0]
    pooled[LEFT : LEFT + width, :] = cells
    pooled[LEFT - 1 : LEFT, :] = beside[:1]
    pooled[LEFT + width : LEFT + width + 1, :] = beside[1:]
    for v in range(3):
        window[v, pl.ds(at, width), :] = pooled[pl.ds(LEFT + 1 - v, width), :].astype(BF16)


def facing(group):
    above = [group[0], 0.75 * (group[0] + group[1]) + 0.25 * group[2]]
    below = [0.25 * group[3] + 0.75 * (group[4] + group[5]), group[5]]
    return above, below


def row_pack_kernel(flags, centre, *outs):
    images, height2, width = centre.shape[0], centre.shape[1], centre.shape[2] - 8
    row_odd = flags[ROW_ODD] == 1
    for i in range(images):
        above, below = facing([centre[i, r, :width, :] for r in (0, 1, 2, height2 - 3, height2 - 2, height2 - 1)])
        for second, out in enumerate(outs):
            for n in range(2):
                odd, even = (below[n], above[n]) if second else (above[n], below[n])
                at = (2 * i + n) * width
                out[at : at + width, :] = jnp.where(row_odd, odd, even).astype(BF16)


def corner_pack_kernel(has_second, flags, centre, col_a, col_b, *refs):
    outs, (cells_out, beside_out, ends) = refs[: 2 if has_second else 1], refs[-3:]
    images, height2, width = centre.shape[0], centre.shape[1], centre.shape[2] - 8
    row_odd = flags[ROW_ODD] == 1
    lines = [0, 1, 2, height2 - 3, height2 - 2, height2 - 1]
    for i in range(images):
        cells, beside = pool_columns(flags, centre, col_a, col_b, i, lines)
        added = []
        for n in range(6):
            cells_out[i, n] = cells[n]
            beside_out[i, n] = beside[n]
            more = cells[n] - centre[i, lines[n], :width, :]
            added.append(jnp.concatenate([more[:1], more[width - 1 :], beside[n]], axis=0))
        above, below = facing(added)
        for second in range(len(outs)):
            for n in range(2):
                odd, even = (below[n], above[n]) if second else (above[n], below[n])
                at = (2 * i + n) * 4
                ends[second, at : at + 4, :] = jnp.where(row_odd, odd, even)
    for second in range(len(outs)):
        outs[second][...] = ends[second].astype(BF16)


def main_kernel(flags, centre, col_a, col_b, weight, window, acc, pooled):
    images, height2, width, channels = centre.shape[0], centre.shape[1], centre.shape[2] - 8, centre.shape[3]
    height, depths = height2 // 2, weight.shape[0]
    pooled[...] = jnp.zeros_like(pooled)

    def per_image(i, carry):
        cells, beside = pool_columns(flags, centre, col_a, col_b, i, range(1, height2 - 1))
        for p in range(1, height - 1):
            at = 2 * p - 2
            both = [
                0.75 * (group[at + 1] + group[at + 2]) + 0.25 * (group[at] + group[at + 3])
                for group in (cells, beside)
            ]
            where = pl.multiple_of((p + 1) * images * width + i * width, width)
            place(both[0], both[1], pooled.at[p], window, where)
        return carry

    lax.fori_loop(0, images, per_image, 0)
    line = images * width
    inner = (height - 2) * line
    rows = slice(2 * line, 2 * line + inner)
    for k in range(depths):
        for u in range(3):
            part = nt_dot(window[0, rows, :], weight[k, u, 0])
            part = part + nt_dot(window[1, rows, :], weight[k, u, 1])
            part = part + nt_dot(window[2, rows, :], weight[k, u, 2])
            if u == 0:
                acc[k, :inner, :] = part
                acc[k, inner:, :] = jnp.zeros((2 * line, channels), F32)
            else:
                acc[k, u * line : u * line + inner, :] += part


def edge_kernel(has_second, flags, *refs):
    sides = 2 if has_second else 1
    rows, corners, (cells, beside, _, acc, weight) = refs[:sides], refs[sides : 2 * sides], refs[2 * sides : 2 * sides + 5]
    *grads, window, pooled, ends, total = refs[2 * sides + 5 :]
    images, width = cells.shape[0], cells.shape[2]
    depths, count = acc.shape[:2]
    line = images * width
    height = count // line
    row_odd, top, bottom = flags[ROW_ODD] == 1, flags[TOP] == 1, flags[BOTTOM] == 1
    for n in range(sides):
        ends[n] = corners[n][...].astype(F32)
    pooled[...] = jnp.zeros_like(pooled)
    cell = lax.broadcasted_iota(jnp.int32, (width, cells.shape[3]), 0)
    for i in range(images):
        for_rows = []
        for is_end, own in ((False, cells), (True, beside)):
            def came(from_above, n):
                def of(ref_at):
                    end, at = (2 * i + n) * 4, (2 * i + n) * width
                    if is_end:
                        return ends[ref_at, end + 2 : end + 4, :]
                    more = jnp.where(cell == 0, ends[ref_at, end : end + 1, :], 0.0)
                    more = jnp.where(cell == width - 1, ends[ref_at, end + 1 : end + 2, :], more)
                    return rows[ref_at][at : at + width, :].astype(F32) + more

                first = of(0)
                second = of(1) if has_second else jnp.zeros_like(first)
                return jnp.where(row_odd, first, second) if from_above else jnp.where(row_odd, second, first)

            edge = [own[i, n] for n in range(6)]
            zero = jnp.zeros_like(edge[0])
            for_rows.append(
                [
                    jnp.where(top, zero, came(True, 0) + 0.25 * edge[0]),
                    0.75 * (edge[0] + edge[1]) + 0.25 * (jnp.where(top, edge[0], came(True, 1)) + edge[2]),
                    0.75 * (edge[4] + edge[5]) + 0.25 * (jnp.where(bottom, edge[5], came(False, 0)) + edge[3]),
                    jnp.where(bottom, zero, came(False, 1) + 0.25 * edge[5]),
                ]
            )
        for n, p in enumerate((0, 1, height, height + 1)):
            place(for_rows[0][n], for_rows[1][n], pooled.at[n], window, p * line + i * width)
    low, high = slice(0, 2 * line), slice(height * line, (height + 2) * line)
    for k in range(depths):
        total[...] = acc[k]
        for v in range(3):
            total[(height - 2) * line :, :] += nt_dot(window[v, high, :], weight[k, 0, v])
            total[: 2 * line, :] += nt_dot(window[v, low, :], weight[k, 2, v])
            middle = jnp.concatenate(
                [window[v, line : 2 * line, :], window[v, height * line : (height + 1) * line, :]], axis=0
            )
            part = nt_dot(middle, weight[k, 1, v])
            total[:line, :] += part[:line]
            total[(height - 1) * line :, :] += part[line:]
        for apart in range(2 * CHIPS):
            at = pl.multiple_of((flags[GRAY] ^ apart) * line, line)
            grads[apart // 2][apart % 2, k] = total[pl.ds(at, line), :].astype(BF16)


def deal(full, split_refs, core, turned):
    if len(split_refs) == 1:
        split_refs[0][...] = full[...]
        return
    kept, *sent = split_refs
    count, rows = kept.shape[:2]
    size = sent[0].shape[0]
    for j in range(count):
        p = (j & ~3 | (j & 1) << 1 | j >> 1 & 1) if turned else j
        kept[p] = full[pl.ds(pl.multiple_of((2 * j + core) * rows, 16), rows), :]
        sent[p // size][p % size] = full[pl.ds(pl.multiple_of((2 * j + 1 - core) * rows, 16), rows), :]


def conv_term_kernel(flags, window, saved, *refs):
    split_refs, top, full, flat = refs[:-3], refs[-3], refs[-2], refs[-1]
    images, depths, height, width, channels = saved.shape
    line = images * width
    count = height * line
    split = top.shape[0]
    for k in range(depths):
        for h in range(height):
            for i in range(images):
                at = (h * images + i) * width
                flat[at : at + width, :] = saved[i, k, h]
        flat_t = flat[...].T
        for n in range(9):
            start = (2 - n // 3) * line
            part = jnp.dot(
                flat_t, window[n % 3, start : start + count, :], preferred_element_type=F32
            ).astype(BF16)
            at = (k * 9 + n) * channels
            if at < split:
                top[at : at + channels, :] = part
            else:
                full[at - split : at - split + channels, :] = part
    deal(full, split_refs, flags[CORE], True)


def pass_on_kernel(*refs):
    for n, piece in enumerate(refs[:-1]):
        refs[-1][n] = piece[1]


def proj_term_kernel(flags, *refs):
    came, (passed, feats, conv_top) = refs[:CHIPS], refs[CHIPS : CHIPS + 3]
    split_refs, tokens, full = refs[CHIPS + 3 : -2], refs[-2], refs[-1]
    images, depths, _, dim = feats.shape
    line = passed.shape[2]
    width = line // images
    for apart in range(2 * CHIPS):
        column = column_of(flags[GRAY] ^ apart)
        for k in range(depths):
            for i in range(images):
                at = pl.multiple_of((i * TILE_COLS + column) * width, width)
                rows = slice(i * width, (i + 1) * width)
                piece = passed[apart // 2, k, rows, :] if apart % 2 else came[apart // 2][0, k, rows, :]
                tokens[k, pl.ds(at, width), :] = piece
    for k in range(depths):
        flat = feats[:, k].reshape(tokens.shape[1], dim)
        part = lax.dot_general(
            flat, tokens[k], (((0,), (0,)), ((), ())), preferred_element_type=F32
        )
        full[k * dim : (k + 1) * dim, :] = part.astype(BF16)
    full[depths * dim :, :] = conv_top[...]
    deal(full, split_refs, flags[CORE], False)


def feat_grad_kernel(tokens, weight, out):
    images, depths, count, dim = out.shape
    for k in range(depths):
        out[:, k] = nt_dot(tokens[k], weight[k]).astype(BF16).reshape(images, count, dim)


def take(part, block, at, columns=None):
    size = part[0].shape[0]
    return part[block // size][block % size + at, :, slice(None) if columns is None else columns].astype(F32)


def round_kernel(jobs, flags, *refs):
    ins, outs, dp = list(refs[: sum(sum(job[0]) for job in jobs)]), refs, flags[DP]
    outs = list(refs[len(ins) :])
    for sizes, at, bits, by_columns, heights in jobs:
        parts = []
        for size in sizes:
            parts.append(ins[:size])
            del ins[:size]
        span = 1 << bits
        mine = 0
        for b in range(bits):
            mine = mine + flags[BITS + at + b] * (1 << b)
        last = span * (2 if by_columns else 1)
        for n in [0] + list(range(last - 1, 0, -1)):
            across, apart = n // span, n % span
            pieces = outs[: len(heights) if n else 1]
            del outs[: len(pieces)]
            count, _, width = pieces[0].shape
            columns = None
            if by_columns:
                columns = pl.ds(pl.multiple_of((dp ^ across) * width, width), width)
            for q in range(count):
                total = take(parts[0], q * span, mine ^ apart, columns)
                for other in parts[1:]:
                    total = total + take(other, q * span, mine ^ apart, columns)
                start = 0
                for piece in pieces:
                    piece[q] = total[start : start + piece.shape[1]].astype(piece.dtype)
                    start += piece.shape[1]


def last_kernel(early_parts, flags, *refs):
    ins, (sent, kept) = list(refs[:-2]), refs[-2:]
    first = flags[DP] == 0
    sums = []
    for sizes in (early_parts, (1,) * (len(ins) - sum(early_parts))):
        total = 0.0
        for size in sizes:
            rows = [piece[0].astype(F32) for piece in ins[:size]]
            total = total + (jnp.concatenate(rows, axis=0) if size > 1 else rows[0])
            del ins[:size]
        sums.append(total)
    sent[...] = jnp.where(first, sums[0], sums[1]).astype(BF16)
    kept[...] = jnp.where(first, sums[1], sums[0])


def join_kernel(scale, flags, kept, came, out):
    width = kept.shape[1]
    at = pl.multiple_of(flags[DP] * width, width)
    out[:, pl.ds(at, width)] = kept[...] * scale
    at = pl.multiple_of((1 - flags[DP]) * width, width)
    out[:, pl.ds(at, width)] = came[...].astype(F32) * scale


def vmem_call(kernel, out_shape, operands, scratch=(), scalars=1, flops=0, limit=16, after=(), aliases=()):
    whole = pl.BlockSpec(memory_space=pltpu.VMEM)
    specs = [pl.BlockSpec(memory_space=pltpu.SMEM)] * scalars + [whole] * (len(operands) - scalars)
    specs += [pl.BlockSpec(memory_space=pl.ANY)] * len(after)
    count = len(operands)

    def run(*refs):
        kernel(*refs[:count], *refs[count + len(after) :])

    moved = sum(a.size * a.dtype.itemsize for a in operands)
    moved += sum(math.prod(s.shape) * s.dtype.itemsize for s in jax.tree.leaves(out_shape))
    return pl.pallas_call(
        run,
        out_shape=out_shape,
        in_specs=specs,
        out_specs=jax.tree.map(lambda _: whole, out_shape),
        scratch_shapes=list(scratch),
        input_output_aliases=dict(aliases),
        compiler_params=pltpu.CompilerParams(vmem_limit_bytes=limit << 20),
        cost_estimate=pl.CostEstimate(flops=flops, bytes_accessed=moved, transcendentals=0),
    )(*operands, *after)


def sds(*shape, dtype=BF16):
    return jax.ShapeDtypeStruct(shape, dtype)


def xor_move(block, apart, across):
    tiles = lax.axis_size("tile")
    if not across:
        return lax.ppermute(block, "tile", [(t, t ^ apart) for t in range(tiles)])
    if not apart:
        return lax.ppermute(block, "dp", [(0, 1), (1, 0)])
    route = [(d * tiles + t, (1 - d) * tiles + (t ^ apart)) for d in range(2) for t in range(tiles)]
    return lax.ppermute(block, ("dp", "tile"), route)


def core_sum(dealt, core, pieces, turned):
    if len(dealt) == 1:
        tiles = lax.axis_size("tile")
        rows, channels = dealt[0].shape[0] // tiles, dealt[0].shape[1]
        pairs = dealt[0].reshape(tiles // 2, 2, rows, channels)
        if turned:
            pairs = pairs.reshape(tiles // 8, 2, 2, 2, rows, channels).swapaxes(1, 2).reshape(pairs.shape)
        kept = lax.dynamic_index_in_dim(pairs, core, 1, keepdims=False)
        sent = lax.dynamic_index_in_dim(pairs, 1 - core, 1, keepdims=False)
        size = sent.shape[0] // pieces
        sent = [sent[n * size : (n + 1) * size] for n in range(pieces)]
    else:
        kept, *sent = dealt
    return [[kept], [xor_move(piece, 1, False) for piece in sent]]


def deal_rounds(jobs, flags, after=()):
    outs, plans, operands = [], [], [flags]
    for parts, at, bits, by_columns, cut in jobs:
        span = 1 << bits
        count, rows, channels = parts[0][0].shape
        channels = channels // 2 if by_columns else channels
        tiles = rows // 16
        heights = [rows]
        if rows % 16 == 0 and cut > 1:
            heights = [16 * (tiles * (n + 1) // cut - tiles * n // cut) for n in range(cut)]
        for n in range(span * (2 if by_columns else 1)):
            if n == 0:
                outs.append(sds(count // span, rows, channels, dtype=F32))
            else:
                outs += [sds(count // span, height, channels) for height in heights]
        plans.append((tuple(len(part) for part in parts), at, bits, by_columns, tuple(heights)))
        operands += [piece for part in parts for piece in part]
    pieces = list(vmem_call(functools.partial(round_kernel, plans), outs, operands, after=after))
    token, sums = pieces[0], []
    for _, at, bits, by_columns, heights in plans:
        span = 1 << bits
        parts = [[pieces.pop(0)]]
        for n in range(span * (2 if by_columns else 1) - 1, 0, -1):
            parts.append([xor_move(pieces.pop(0), (n % span) << at, n >= span) for _ in heights])
        sums.append(parts)
    return sums, token


def per_device(features, proj_weight, conv_weight, saved, cotangent):
    position = lax.axis_index("tile")
    tile_count = lax.axis_size("tile")
    rows = tile_count // TILE_COLS
    gray = position % TILE_COLS
    col, row = column_of(gray), position // TILE_COLS
    images, height2, width2, channels = cotangent.shape
    depths, dim = proj_weight.shape[:2]
    height, width = height2 // 2, width2 // 2
    patches = images * height * width
    line = images * width
    tokens = features.shape[2]
    has_second = rows > 2
    sides = 2 if has_second else 1
    bits = tile_count.bit_length() - 1
    flags = jnp.stack(
        [row % 2, col % 2, row == 0, row == rows - 1, col == 0, col == TILE_COLS - 1]
        + [position % 2, lax.axis_index("dp"), gray]
        + [position >> b & 1 for b in range(bits)]
    ).astype(jnp.int32)

    def swap(block, row_pairs, col_pairs):
        return lax.ppermute(block, "tile", tile_route(row_pairs, col_pairs, rows))

    low, high = cotangent[:, :, :HALO], cotangent[:, :, width2 - HALO :]
    around = paired(TILE_COLS, 1) + [(0, TILE_COLS - 1), (TILE_COLS - 1, 0)]
    col_b = swap(jnp.where(col % 2 == 1, high, low), None, around)
    col_a = swap(jnp.where(col % 2 == 1, low, high), None, paired(TILE_COLS, 0))
    centre = vmem_call(
        centre_kernel,
        sds(images, height2, width + 8, channels, dtype=F32),
        (cotangent,),
        scratch=(pltpu.VMEM((channels // 128, height2, LEFT + width2 + 8, 128), F32),),
        scalars=0,
    )
    row_out = vmem_call(row_pack_kernel, [sds(2 * line, channels)] * sides, (flags, centre))
    came_rows = [swap(row_out[n], paired(rows, n), None) for n in range(sides)]
    *corner_out, cells, beside = vmem_call(
        functools.partial(corner_pack_kernel, has_second),
        [sds(8 * images, channels)] * sides
        + [sds(images, 6, width, channels, dtype=F32), sds(images, 6, 2, channels, dtype=F32)],
        (flags, centre, col_a, col_b),
        scratch=(pltpu.VMEM((sides, 8 * images, channels), F32),),
    )
    came_rows += [swap(corner_out[n], paired(rows, n), None) for n in range(sides)]
    conv_flops = 2 * patches * depths * 9 * channels * channels
    window, acc = vmem_call(
        main_kernel,
        [sds(3, (height + 2) * line, channels), sds(depths, patches, channels, dtype=F32)],
        (flags, centre, col_a, col_b, conv_weight),
        scratch=(pltpu.VMEM((height, LEFT + width + 8, channels), F32),),
        flops=conv_flops,
        after=(corner_out[0],),
    )
    *grads, window = vmem_call(
        functools.partial(edge_kernel, has_second),
        [sds(2, depths, line, channels)] * CHIPS + [sds(3, (height + 2) * line, channels)],
        [flags] + came_rows + [cells, beside, window, acc, conv_weight],
        scratch=(
            pltpu.VMEM((4, LEFT + width + 8, channels), F32),
            pltpu.VMEM((sides, 8 * images, channels), F32),
            pltpu.VMEM((patches, channels), F32),
        ),
        flops=conv_flops // 4,
        aliases={2 * sides + 3: CHIPS},
    )
    came = [xor_move(grads[chip], 2 * chip, False) for chip in range(CHIPS - 1, 0, -1)]
    came = [grads[0]] + came[::-1]
    to_pass = vmem_call(pass_on_kernel, sds(CHIPS, depths, line, channels), came, scalars=0)
    passed = xor_move(to_pass, 1, False)

    half_rows = depths * (dim + 9 * channels) // 2
    conv_late = half_rows - depths * dim
    block_rows = half_rows // tile_count
    pieces = 4
    if block_rows % 16:
        dealt = [sds(half_rows, channels)]
    else:
        dealt = [sds(tile_count // 2, block_rows, channels)]
        dealt += [sds(tile_count // 2 // pieces, block_rows, channels)] * pieces
    full = pltpu.VMEM((half_rows, channels), BF16)
    *early, conv_top = vmem_call(
        conv_term_kernel,
        dealt + [sds(conv_late, channels)],
        (flags, window, saved),
        scratch=(full, pltpu.VMEM((patches, channels), BF16)),
        flops=conv_flops,
    )
    (early_parts,), before = deal_rounds([(core_sum(early, position % 2, pieces, True), 1, 0, True, 1)], flags)
    proj_flops = 2 * images * tokens * depths * dim * channels
    *terms, token_grad = vmem_call(
        proj_term_kernel,
        dealt + [sds(depths, images * tokens, channels)],
        [flags] + came + [passed, features, conv_top],
        scratch=(full,),
        flops=proj_flops,
        after=(before,),
    )
    (late_parts,), before = deal_rounds(
        [(core_sum(terms, position % 2, pieces, False), 1, 1, True, 1)], flags, after=(token_grad,)
    )
    at, early_bits = 2, [2, 1] + list(range(3, bits))
    while at < bits:
        step = min(2, bits - at)
        (early_parts,), before = deal_rounds([(early_parts, early_bits.pop(0), 1, False, 1)], flags, after=(before,))
        (late_parts, early_parts), before = deal_rounds(
            [(late_parts, at, step, False, 1), (early_parts, early_bits.pop(0), 1, False, 1)], flags, after=(before,)
        )
        at += step
    while early_bits:
        (early_parts,), before = deal_rounds([(early_parts, early_bits.pop(0), 1, False, 1)], flags, after=(before,))
    feature_grad = vmem_call(
        feat_grad_kernel,
        sds(images, depths, tokens, dim),
        (token_grad, proj_weight),
        scalars=0,
        flops=proj_flops,
        after=(before,),
    )
    sent, kept = vmem_call(
        functools.partial(last_kernel, tuple(len(part) for part in early_parts)),
        [sds(block_rows, channels // 2), sds(block_rows, channels // 2, dtype=F32)],
        [flags] + [piece for part in early_parts + late_parts for piece in part],
    )
    other = xor_move(sent, 0, True)
    scale = 1.0 / math.sqrt(images * lax.axis_size("dp") * tokens * tile_count)
    head_grad = vmem_call(
        functools.partial(join_kernel, scale), sds(block_rows, channels, dtype=F32), (flags, kept, other)
    )
    return feature_grad, head_grad


def solution(mesh):
    in_specs = (
        P("dp", None, "tile", None),
        P(),
        P(),
        P("dp", None, "tile", None, None),
        P("dp", "tile", None, None),
    )
    out_specs = (P("dp", None, "tile", None), P(("dp", "tile"), None))
    return jax.shard_map(
        per_device, mesh=mesh, in_specs=in_specs, out_specs=out_specs, check_vma=False
    )
```

```python
import functools
import math

import jax
import jax.numpy as jnp
from jax import lax
from jax.experimental import pallas as pl
from jax.experimental.pallas import tpu as pltpu
from jax.sharding import PartitionSpec as P

TILE_COLS = 8
HALO = 4
LEFT = 8
BF16 = jnp.bfloat16
F32 = jnp.float32
ROW_ODD, COL_ODD, TOP, BOTTOM, LEFT_END, RIGHT_END, CORE, DP, GRAY, BITS = range(10)
CHIPS = TILE_COLS // 2


def gray_of(column):
    return column ^ column >> 1


def column_of(code):
    return code ^ code >> 1 ^ code >> 2


def paired(count, first):
    pairs = []
    for low in range(first, count - 1, 2):
        pairs += [(low, low + 1), (low + 1, low)]
    return pairs


def tile_route(row_pairs, col_pairs, rows):
    row_moves = row_pairs if row_pairs is not None else [(r, r) for r in range(rows)]
    col_moves = col_pairs if col_pairs is not None else [(c, c) for c in range(TILE_COLS)]
    return [
        (r0 * TILE_COLS + gray_of(c0), r1 * TILE_COLS + gray_of(c1))
        for r0, r1 in row_moves
        for c0, c1 in col_moves
    ]


def nt_dot(left, right):
    return lax.dot_general(left, right, (((1,), (1,)), ((), ())), preferred_element_type=F32)


def facing(group):
    above = [group[0], 0.75 * (group[0] + group[1]) + 0.25 * group[2]]
    below = [0.25 * group[3] + 0.75 * (group[4] + group[5]), group[5]]
    return above, below


def centre_kernel(flags, cot, pooled, *refs):
    outs, wide = refs[:-1], refs[-1]
    row_odd = flags[ROW_ODD] == 1
    images, height2, width2, channels = cot.shape
    width = width2 // 2
    wide[...] = jnp.zeros_like(wide)

    def per_image(i, carry):
        for r in range(height2):
            value = cot[i, r].astype(F32)
            for h in range(channels // 128):
                wide[h, r, LEFT : LEFT + width2, :] = value[:, h * 128 : (h + 1) * 128]
            pooled[i, r, width : width + 1, :] = value[:1]
            pooled[i, r, width + 1 : width + 2, :] = value[width2 - 1 :]
        for r in range(height2):
            for h in range(channels // 128):
                taps = [wide[h, r, pl.ds(LEFT - 1 + n, width, stride=2), :] for n in range(4)]
                pooled[i, r, :width, h * 128 : (h + 1) * 128] = 0.75 * (taps[1] + taps[2]) + 0.25 * (taps[0] + taps[3])
        above, below = facing([pooled[i, r, :width, :] for r in (0, 1, 2, height2 - 3, height2 - 2, height2 - 1)])
        for second, out in enumerate(outs):
            for n in range(2):
                odd, even = (below[n], above[n]) if second else (above[n], below[n])
                at = pl.multiple_of((2 * i + n) * width, width)
                out[pl.ds(at, width), :] = jnp.where(row_odd, odd, even).astype(BF16)
        return carry

    lax.fori_loop(0, images, per_image, 0)


def pool_columns(flags, centre, col_a, col_b, i, lines):
    width, channels = centre.shape[2] - 8, centre.shape[3]
    col_odd, left, right = flags[COL_ODD] == 1, flags[LEFT_END] == 1, flags[RIGHT_END] == 1
    cell = lax.broadcasted_iota(jnp.int32, (width, channels), 0)
    is_first, is_last = cell == 0, cell == width - 1
    cells, beside = [], []
    for r in lines:
        own_first, own_last = centre[i, r, width : width + 1, :], centre[i, r, width + 1 : width + 2, :]
        one, two = col_a[i, r].astype(F32), col_b[i, r].astype(F32)
        before, after = jnp.where(col_odd, one, two), jnp.where(col_odd, two, one)
        near_before = jnp.where(left, own_first, before[3:4])
        near_after = jnp.where(right, own_last, after[0:1])
        cells.append(
            centre[i, r, :width, :] + 0.25 * (jnp.where(is_first, near_before, 0.0) + jnp.where(is_last, near_after, 0.0))
        )
        first = 0.75 * (before[2:3] + before[3:4]) + 0.25 * (before[1:2] + own_first)
        last = 0.75 * (after[0:1] + after[1:2]) + 0.25 * (own_last + after[2:3])
        beside.append(
            jnp.concatenate([jnp.where(left, 0.0, first), jnp.where(right, 0.0, last)], axis=0)
        )
    return cells, beside


def place(cells, beside, pooled, window, at):
    width = cells.shape[0]
    pooled[LEFT : LEFT + width, :] = cells
    pooled[LEFT - 1 : LEFT, :] = beside[:1]
    pooled[LEFT + width : LEFT + width + 1, :] = beside[1:]
    for v in range(3):
        window[v, pl.ds(at, width), :] = pooled[pl.ds(LEFT + 1 - v, width), :].astype(BF16)


def corner_pack_kernel(has_second, flags, centre, col_a, col_b, *refs):
    outs, (cells_out, beside_out, ends) = refs[: 2 if has_second else 1], refs[-3:]
    images, height2, width = centre.shape[0], centre.shape[1], centre.shape[2] - 8
    row_odd = flags[ROW_ODD] == 1
    lines = [0, 1, 2, height2 - 3, height2 - 2, height2 - 1]
    for i in range(images):
        cells, beside = pool_columns(flags, centre, col_a, col_b, i, lines)
        added = []
        for n in range(6):
            cells_out[i, n] = cells[n]
            beside_out[i, n] = beside[n]
            more = cells[n] - centre[i, lines[n], :width, :]
            added.append(jnp.concatenate([more[:1], more[width - 1 :], beside[n]], axis=0))
        above, below = facing(added)
        for second in range(len(outs)):
            for n in range(2):
                odd, even = (below[n], above[n]) if second else (above[n], below[n])
                at = (2 * i + n) * 4
                ends[second, at : at + 4, :] = jnp.where(row_odd, odd, even)
    for second in range(len(outs)):
        outs[second][...] = ends[second].astype(BF16)


def main_kernel(flags, centre, col_a, col_b, weight, window, acc, pooled):
    images, height2, width, channels = centre.shape[0], centre.shape[1], centre.shape[2] - 8, centre.shape[3]
    height, depths = height2 // 2, weight.shape[0]
    pooled[...] = jnp.zeros_like(pooled)

    def per_image(i, carry):
        cells, beside = pool_columns(flags, centre, col_a, col_b, i, range(1, height2 - 1))
        for p in range(1, height - 1):
            at = 2 * p - 2
            both = [
                0.75 * (group[at + 1] + group[at + 2]) + 0.25 * (group[at] + group[at + 3])
                for group in (cells, beside)
            ]
            where = pl.multiple_of((p + 1) * images * width + i * width, width)
            place(both[0], both[1], pooled.at[p], window, where)
        return carry

    lax.fori_loop(0, images, per_image, 0)
    line = images * width
    inner = (height - 2) * line
    rows = slice(2 * line, 2 * line + inner)
    for k in range(depths):
        for u in range(3):
            part = nt_dot(window[0, rows, :], weight[k, u, 0])
            part = part + nt_dot(window[1, rows, :], weight[k, u, 1])
            part = part + nt_dot(window[2, rows, :], weight[k, u, 2])
            if u == 0:
                acc[k, :inner, :] = part
                acc[k, inner:, :] = jnp.zeros((2 * line, channels), F32)
            else:
                acc[k, u * line : u * line + inner, :] += part


def edge_kernel(has_second, flags, *refs):
    sides = 2 if has_second else 1
    rows, corners, (cells, beside, _, acc, weight) = refs[:sides], refs[sides : 2 * sides], refs[2 * sides : 2 * sides + 5]
    *grads, window, pooled, ends, total = refs[2 * sides + 5 :]
    images, width = cells.shape[0], cells.shape[2]
    depths, count = acc.shape[:2]
    line = images * width
    height = count // line
    row_odd, top, bottom = flags[ROW_ODD] == 1, flags[TOP] == 1, flags[BOTTOM] == 1
    for n in range(sides):
        ends[n] = corners[n][...].astype(F32)
    pooled[...] = jnp.zeros_like(pooled)
    cell = lax.broadcasted_iota(jnp.int32, (width, cells.shape[3]), 0)
    for i in range(images):
        for_rows = []
        for is_end, own in ((False, cells), (True, beside)):
            def came(from_above, n):
                def of(ref_at):
                    end, at = (2 * i + n) * 4, (2 * i + n) * width
                    if is_end:
                        return ends[ref_at, end + 2 : end + 4, :]
                    more = jnp.where(cell == 0, ends[ref_at, end : end + 1, :], 0.0)
                    more = jnp.where(cell == width - 1, ends[ref_at, end + 1 : end + 2, :], more)
                    return rows[ref_at][at : at + width, :].astype(F32) + more

                first = of(0)
                second = of(1) if has_second else jnp.zeros_like(first)
                return jnp.where(row_odd, first, second) if from_above else jnp.where(row_odd, second, first)

            edge = [own[i, n] for n in range(6)]
            zero = jnp.zeros_like(edge[0])
            for_rows.append(
                [
                    jnp.where(top, zero, came(True, 0) + 0.25 * edge[0]),
                    0.75 * (edge[0] + edge[1]) + 0.25 * (jnp.where(top, edge[0], came(True, 1)) + edge[2]),
                    0.75 * (edge[4] + edge[5]) + 0.25 * (jnp.where(bottom, edge[5], came(False, 0)) + edge[3]),
                    jnp.where(bottom, zero, came(False, 1) + 0.25 * edge[5]),
                ]
            )
        for n, p in enumerate((0, 1, height, height + 1)):
            place(for_rows[0][n], for_rows[1][n], pooled.at[n], window, p * line + i * width)
    low, high = slice(0, 2 * line), slice(height * line, (height + 2) * line)
    for k in range(depths):
        total[...] = acc[k]
        for v in range(3):
            total[(height - 2) * line :, :] += nt_dot(window[v, high, :], weight[k, 0, v])
            total[: 2 * line, :] += nt_dot(window[v, low, :], weight[k, 2, v])
            middle = jnp.concatenate(
                [window[v, line : 2 * line, :], window[v, height * line : (height + 1) * line, :]], axis=0
            )
            part = nt_dot(middle, weight[k, 1, v])
            total[:line, :] += part[:line]
            total[(height - 1) * line :, :] += part[line:]
        for apart in range(2 * CHIPS):
            at = pl.multiple_of((flags[GRAY] ^ apart) * line, line)
            grads[apart // 2][apart % 2, k] = total[pl.ds(at, line), :].astype(BF16)


def deal(full, split_refs, core, turned):
    if len(split_refs) == 1:
        split_refs[0][...] = full[...]
        return
    kept, *sent = split_refs
    count, rows = kept.shape[:2]
    size = sent[0].shape[0]
    for j in range(count):
        p = (j & ~3 | (j & 1) << 1 | j >> 1 & 1) if turned else j
        kept[p] = full[pl.ds(pl.multiple_of((2 * j + core) * rows, 16), rows), :]
        sent[p // size][p % size] = full[pl.ds(pl.multiple_of((2 * j + 1 - core) * rows, 16), rows), :]


def conv_term_kernel(flags, window, saved, *refs):
    split_refs, top, full, flat = refs[:-3], refs[-3], refs[-2], refs[-1]
    images, depths, height, width, channels = saved.shape
    line = images * width
    count = height * line
    split = top.shape[0]
    for k in range(depths):
        for h in range(height):
            for i in range(images):
                at = (h * images + i) * width
                flat[at : at + width, :] = saved[i, k, h]
        flat_t = flat[...].T
        for n in range(9):
            start = (2 - n // 3) * line
            part = jnp.dot(
                flat_t, window[n % 3, start : start + count, :], preferred_element_type=F32
            ).astype(BF16)
            at = (k * 9 + n) * channels
            if at < split:
                top[at : at + channels, :] = part
            else:
                full[at - split : at - split + channels, :] = part
    deal(full, split_refs, flags[CORE], True)


def pass_on_kernel(*refs):
    for n, piece in enumerate(refs[:-1]):
        refs[-1][n] = piece[1]


def proj_term_kernel(flags, *refs):
    came, (passed, feats, conv_top) = refs[:CHIPS], refs[CHIPS : CHIPS + 3]
    split_refs, tokens, full = refs[CHIPS + 3 : -2], refs[-2], refs[-1]
    images, depths, _, dim = feats.shape
    line = passed.shape[2]
    width = line // images
    for apart in range(2 * CHIPS):
        column = column_of(flags[GRAY] ^ apart)
        for k in range(depths):
            for i in range(images):
                at = pl.multiple_of((i * TILE_COLS + column) * width, width)
                rows = slice(i * width, (i + 1) * width)
                piece = passed[apart // 2, k, rows, :] if apart % 2 else came[apart // 2][0, k, rows, :]
                tokens[k, pl.ds(at, width), :] = piece
    for k in range(depths):
        flat = feats[:, k].reshape(tokens.shape[1], dim)
        part = lax.dot_general(
            flat, tokens[k], (((0,), (0,)), ((), ())), preferred_element_type=F32
        )
        full[k * dim : (k + 1) * dim, :] = part.astype(BF16)
    full[depths * dim :, :] = conv_top[...]
    deal(full, split_refs, flags[CORE], False)


def feat_grad_kernel(tokens, weight, out):
    images, depths, count, dim = out.shape
    for k in range(depths):
        out[:, k] = nt_dot(tokens[k], weight[k]).astype(BF16).reshape(images, count, dim)


def take(part, block, at, columns=None):
    size = part[0].shape[0]
    return part[block // size][block % size + at, :, slice(None) if columns is None else columns].astype(F32)


def round_kernel(jobs, flags, *refs):
    ins, outs, dp = list(refs[: sum(sum(job[0]) for job in jobs)]), refs, flags[DP]
    outs = list(refs[len(ins) :])
    for sizes, at, bits, by_columns, heights in jobs:
        parts = []
        for size in sizes:
            parts.append(ins[:size])
            del ins[:size]
        span = 1 << bits
        mine = 0
        for b in range(bits):
            mine = mine + flags[BITS + at + b] * (1 << b)
        last = span * (2 if by_columns else 1)
        for n in [0] + list(range(last - 1, 0, -1)):
            across, apart = n // span, n % span
            pieces = outs[: len(heights) if n else 1]
            del outs[: len(pieces)]
            count, _, width = pieces[0].shape
            columns = None
            if by_columns:
                columns = pl.ds(pl.multiple_of((dp ^ across) * width, width), width)
            for q in range(count):
                total = take(parts[0], q * span, mine ^ apart, columns)
                for other in parts[1:]:
                    total = total + take(other, q * span, mine ^ apart, columns)
                start = 0
                for piece in pieces:
                    piece[q] = total[start : start + piece.shape[1]].astype(piece.dtype)
                    start += piece.shape[1]


def last_kernel(early_parts, flags, *refs):
    ins, (sent, kept) = list(refs[:-2]), refs[-2:]
    first = flags[DP] == 0
    sums = []
    for sizes in (early_parts, (1,) * (len(ins) - sum(early_parts))):
        total = 0.0
        for size in sizes:
            rows = [piece[0].astype(F32) for piece in ins[:size]]
            total = total + (jnp.concatenate(rows, axis=0) if size > 1 else rows[0])
            del ins[:size]
        sums.append(total)
    sent[...] = jnp.where(first, sums[0], sums[1]).astype(BF16)
    kept[...] = jnp.where(first, sums[1], sums[0])


def join_kernel(scale, flags, kept, came, out):
    width = kept.shape[1]
    at = pl.multiple_of(flags[DP] * width, width)
    out[:, pl.ds(at, width)] = kept[...] * scale
    at = pl.multiple_of((1 - flags[DP]) * width, width)
    out[:, pl.ds(at, width)] = came[...].astype(F32) * scale


def vmem_call(kernel, out_shape, operands, scratch=(), scalars=1, flops=0, limit=16, after=(), aliases=()):
    whole = pl.BlockSpec(memory_space=pltpu.VMEM)
    specs = [pl.BlockSpec(memory_space=pltpu.SMEM)] * scalars + [whole] * (len(operands) - scalars)
    specs += [pl.BlockSpec(memory_space=pl.ANY)] * len(after)
    count = len(operands)

    def run(*refs):
        kernel(*refs[:count], *refs[count + len(after) :])

    moved = sum(a.size * a.dtype.itemsize for a in operands)
    moved += sum(math.prod(s.shape) * s.dtype.itemsize for s in jax.tree.leaves(out_shape))
    return pl.pallas_call(
        run,
        out_shape=out_shape,
        in_specs=specs,
        out_specs=jax.tree.map(lambda _: whole, out_shape),
        scratch_shapes=list(scratch),
        input_output_aliases=dict(aliases),
        compiler_params=pltpu.CompilerParams(vmem_limit_bytes=limit << 20),
        cost_estimate=pl.CostEstimate(flops=flops, bytes_accessed=moved, transcendentals=0),
    )(*operands, *after)


def sds(*shape, dtype=BF16):
    return jax.ShapeDtypeStruct(shape, dtype)


def xor_move(block, apart, across):
    tiles = lax.axis_size("tile")
    if not across:
        return lax.ppermute(block, "tile", [(t, t ^ apart) for t in range(tiles)])
    if not apart:
        return lax.ppermute(block, "dp", [(0, 1), (1, 0)])
    route = [(d * tiles + t, (1 - d) * tiles + (t ^ apart)) for d in range(2) for t in range(tiles)]
    return lax.ppermute(block, ("dp", "tile"), route)


def core_sum(dealt, core, pieces, turned):
    if len(dealt) == 1:
        tiles = lax.axis_size("tile")
        rows, channels = dealt[0].shape[0] // tiles, dealt[0].shape[1]
        pairs = dealt[0].reshape(tiles // 2, 2, rows, channels)
        if turned:
            pairs = pairs.reshape(tiles // 8, 2, 2, 2, rows, channels).swapaxes(1, 2).reshape(pairs.shape)
        kept = lax.dynamic_index_in_dim(pairs, core, 1, keepdims=False)
        sent = lax.dynamic_index_in_dim(pairs, 1 - core, 1, keepdims=False)
        size = sent.shape[0] // pieces
        sent = [sent[n * size : (n + 1) * size] for n in range(pieces)]
    else:
        kept, *sent = dealt
    return [[kept], [xor_move(piece, 1, False) for piece in sent]]


def deal_rounds(jobs, flags, after=()):
    outs, plans, operands = [], [], [flags]
    for parts, at, bits, by_columns, cut in jobs:
        span = 1 << bits
        count, rows, channels = parts[0][0].shape
        channels = channels // 2 if by_columns else channels
        tiles = rows // 16
        heights = [rows]
        if rows % 16 == 0 and cut > 1:
            heights = [16 * (tiles * (n + 1) // cut - tiles * n // cut) for n in range(cut)]
        for n in range(span * (2 if by_columns else 1)):
            if n == 0:
                outs.append(sds(count // span, rows, channels, dtype=F32))
            else:
                outs += [sds(count // span, height, channels) for height in heights]
        plans.append((tuple(len(part) for part in parts), at, bits, by_columns, tuple(heights)))
        operands += [piece for part in parts for piece in part]
    pieces = list(vmem_call(functools.partial(round_kernel, plans), outs, operands, after=after))
    token, sums = pieces[0], []
    for _, at, bits, by_columns, heights in plans:
        span = 1 << bits
        parts = [[pieces.pop(0)]]
        for n in range(span * (2 if by_columns else 1) - 1, 0, -1):
            parts.append([xor_move(pieces.pop(0), (n % span) << at, n >= span) for _ in heights])
        sums.append(parts)
    return sums, token


def per_device(features, proj_weight, conv_weight, saved, cotangent):
    position = lax.axis_index("tile")
    tile_count = lax.axis_size("tile")
    rows = tile_count // TILE_COLS
    gray = position % TILE_COLS
    col, row = column_of(gray), position // TILE_COLS
    images, height2, width2, channels = cotangent.shape
    depths, dim = proj_weight.shape[:2]
    height, width = height2 // 2, width2 // 2
    patches = images * height * width
    line = images * width
    tokens = features.shape[2]
    has_second = rows > 2
    sides = 2 if has_second else 1
    bits = tile_count.bit_length() - 1
    flags = jnp.stack(
        [row % 2, col % 2, row == 0, row == rows - 1, col == 0, col == TILE_COLS - 1]
        + [position % 2, lax.axis_index("dp"), gray]
        + [position >> b & 1 for b in range(bits)]
    ).astype(jnp.int32)

    def swap(block, row_pairs, col_pairs):
        return lax.ppermute(block, "tile", tile_route(row_pairs, col_pairs, rows))

    low, high = cotangent[:, :, :HALO], cotangent[:, :, width2 - HALO :]
    around = paired(TILE_COLS, 1) + [(0, TILE_COLS - 1), (TILE_COLS - 1, 0)]
    col_b = swap(jnp.where(col % 2 == 1, high, low), None, around)
    col_a = swap(jnp.where(col % 2 == 1, low, high), None, paired(TILE_COLS, 0))
    centre, *row_out = vmem_call(
        centre_kernel,
        [sds(images, height2, width + 8, channels, dtype=F32)] + [sds(2 * line, channels)] * sides,
        (flags, cotangent),
        scratch=(pltpu.VMEM((channels // 128, height2, LEFT + width2 + 8, 128), F32),),
    )
    came_rows = [swap(row_out[n], paired(rows, n), None) for n in range(sides)]
    *corner_out, cells, beside = vmem_call(
        functools.partial(corner_pack_kernel, has_second),
        [sds(8 * images, channels)] * sides
        + [sds(images, 6, width, channels, dtype=F32), sds(images, 6, 2, channels, dtype=F32)],
        (flags, centre, col_a, col_b),
        scratch=(pltpu.VMEM((sides, 8 * images, channels), F32),),
    )
    came_rows += [swap(corner_out[n], paired(rows, n), None) for n in range(sides)]
    conv_flops = 2 * patches * depths * 9 * channels * channels
    window, acc = vmem_call(
        main_kernel,
        [sds(3, (height + 2) * line, channels), sds(depths, patches, channels, dtype=F32)],
        (flags, centre, col_a, col_b, conv_weight),
        scratch=(pltpu.VMEM((height, LEFT + width + 8, channels), F32),),
        flops=conv_flops,
        after=(corner_out[0],),
    )
    *grads, window = vmem_call(
        functools.partial(edge_kernel, has_second),
        [sds(2, depths, line, channels)] * CHIPS + [sds(3, (height + 2) * line, channels)],
        [flags] + came_rows + [cells, beside, window, acc, conv_weight],
        scratch=(
            pltpu.VMEM((4, LEFT + width + 8, channels), F32),
            pltpu.VMEM((sides, 8 * images, channels), F32),
            pltpu.VMEM((patches, channels), F32),
        ),
        flops=conv_flops // 4,
        aliases={2 * sides + 3: CHIPS},
    )
    came = [xor_move(grads[chip], 2 * chip, False) for chip in range(CHIPS - 1, 0, -1)]
    came = [grads[0]] + came[::-1]
    to_pass = vmem_call(pass_on_kernel, sds(CHIPS, depths, line, channels), came, scalars=0)
    passed = xor_move(to_pass, 1, False)

    half_rows = depths * (dim + 9 * channels) // 2
    conv_late = half_rows - depths * dim
    block_rows = half_rows // tile_count
    pieces = 4
    if block_rows % 16:
        dealt = [sds(half_rows, channels)]
    else:
        dealt = [sds(tile_count // 2, block_rows, channels)]
        dealt += [sds(tile_count // 2 // pieces, block_rows, channels)] * pieces
    full = pltpu.VMEM((half_rows, channels), BF16)
    *early, conv_top = vmem_call(
        conv_term_kernel,
        dealt + [sds(conv_late, channels)],
        (flags, window, saved),
        scratch=(full, pltpu.VMEM((patches, channels), BF16)),
        flops=conv_flops,
    )
    (early_parts,), before = deal_rounds([(core_sum(early, position % 2, pieces, True), 1, 0, True, 1)], flags)
    proj_flops = 2 * images * tokens * depths * dim * channels
    *terms, token_grad = vmem_call(
        proj_term_kernel,
        dealt + [sds(depths, images * tokens, channels)],
        [flags] + came + [passed, features, conv_top],
        scratch=(full,),
        flops=proj_flops,
        after=(before,),
    )
    (late_parts,), before = deal_rounds(
        [(core_sum(terms, position % 2, pieces, False), 1, 1, True, 1)], flags, after=(token_grad,)
    )
    at, early_bits = 2, [2, 1] + list(range(3, bits))
    while at < bits:
        step = min(2, bits - at)
        (early_parts,), before = deal_rounds([(early_parts, early_bits.pop(0), 1, False, 1)], flags, after=(before,))
        (late_parts, early_parts), before = deal_rounds(
            [(late_parts, at, step, False, 1), (early_parts, early_bits.pop(0), 1, False, 1)], flags, after=(before,)
        )
        at += step
    while early_bits:
        (early_parts,), before = deal_rounds([(early_parts, early_bits.pop(0), 1, False, 1)], flags, after=(before,))
    feature_grad = vmem_call(
        feat_grad_kernel,
        sds(images, depths, tokens, dim),
        (token_grad, proj_weight),
        scalars=0,
        flops=proj_flops,
        after=(before,),
    )
    sent, kept = vmem_call(
        functools.partial(last_kernel, tuple(len(part) for part in early_parts)),
        [sds(block_rows, channels // 2), sds(block_rows, channels // 2, dtype=F32)],
        [flags] + [piece for part in early_parts + late_parts for piece in part],
    )
    other = xor_move(sent, 0, True)
    scale = 1.0 / math.sqrt(images * lax.axis_size("dp") * tokens * tile_count)
    head_grad = vmem_call(
        functools.partial(join_kernel, scale), sds(block_rows, channels, dtype=F32), (flags, kept, other)
    )
    return feature_grad, head_grad


def solution(mesh):
    in_specs = (
        P("dp", None, "tile", None),
        P(),
        P(),
        P("dp", None, "tile", None, None),
        P("dp", "tile", None, None),
    )
    out_specs = (P("dp", None, "tile", None), P(("dp", "tile"), None))
    return jax.shard_map(
        per_device, mesh=mesh, in_specs=in_specs, out_specs=out_specs, check_vma=False
    )
```

```python
import functools
import math

import jax
import jax.numpy as jnp
from jax import lax
from jax.experimental import pallas as pl
from jax.experimental.pallas import tpu as pltpu
from jax.sharding import PartitionSpec as P

TILE_COLS = 8
HALO = 4
LEFT = 8
BF16 = jnp.bfloat16
F32 = jnp.float32
ROW_ODD, COL_ODD, TOP, BOTTOM, LEFT_END, RIGHT_END, CORE, DP, GRAY, BITS = range(10)
CHIPS = TILE_COLS // 2


def gray_of(column):
    return column ^ column >> 1


def column_of(code):
    return code ^ code >> 1 ^ code >> 2


def paired(count, first):
    pairs = []
    for low in range(first, count - 1, 2):
        pairs += [(low, low + 1), (low + 1, low)]
    return pairs


def tile_route(row_pairs, col_pairs, rows):
    row_moves = row_pairs if row_pairs is not None else [(r, r) for r in range(rows)]
    col_moves = col_pairs if col_pairs is not None else [(c, c) for c in range(TILE_COLS)]
    return [
        (r0 * TILE_COLS + gray_of(c0), r1 * TILE_COLS + gray_of(c1))
        for r0, r1 in row_moves
        for c0, c1 in col_moves
    ]


def nt_dot(left, right):
    return lax.dot_general(left, right, (((1,), (1,)), ((), ())), preferred_element_type=F32)


def centre_kernel(cot, pooled, wide):
    images, height2, width2, channels = cot.shape
    width = width2 // 2
    wide[...] = jnp.zeros_like(wide)

    def per_image(i, carry):
        for r in range(height2):
            value = cot[i, r].astype(F32)
            for h in range(channels // 128):
                wide[h, r, LEFT : LEFT + width2, :] = value[:, h * 128 : (h + 1) * 128]
            pooled[i, r, width : width + 1, :] = value[:1]
            pooled[i, r, width + 1 : width + 2, :] = value[width2 - 1 :]
        for r in range(height2):
            for h in range(channels // 128):
                taps = [wide[h, r, pl.ds(LEFT - 1 + n, width, stride=2), :] for n in range(4)]
                pooled[i, r, :width, h * 128 : (h + 1) * 128] = 0.75 * (taps[1] + taps[2]) + 0.25 * (taps[0] + taps[3])
        return carry

    lax.fori_loop(0, images, per_image, 0)


def column_ends(flags, centre, col_a, col_b, i, r):
    width = centre.shape[2] - 8
    col_odd, left, right = flags[COL_ODD] == 1, flags[LEFT_END] == 1, flags[RIGHT_END] == 1
    own_first, own_last = centre[i, r, width : width + 1, :], centre[i, r, width + 1 : width + 2, :]
    one, two = col_a[i, r].astype(F32), col_b[i, r].astype(F32)
    before, after = jnp.where(col_odd, one, two), jnp.where(col_odd, two, one)
    first = 0.75 * (before[2:3] + before[3:4]) + 0.25 * (before[1:2] + own_first)
    last = 0.75 * (after[0:1] + after[1:2]) + 0.25 * (own_last + after[2:3])
    return (
        0.25 * jnp.where(left, own_first, before[3:4]),
        0.25 * jnp.where(right, own_last, after[0:1]),
        jnp.where(left, 0.0, first),
        jnp.where(right, 0.0, last),
    )


def pool_columns(flags, centre, col_a, col_b, i, lines):
    width, channels = centre.shape[2] - 8, centre.shape[3]
    cell = lax.broadcasted_iota(jnp.int32, (width, channels), 0)
    is_first, is_last = cell == 0, cell == width - 1
    cells, beside = [], []
    for r in lines:
        to_first, to_last, first, last = column_ends(flags, centre, col_a, col_b, i, r)
        cells.append(centre[i, r, :width, :] + (jnp.where(is_first, to_first, 0.0) + jnp.where(is_last, to_last, 0.0)))
        beside.append(jnp.concatenate([first, last], axis=0))
    return cells, beside


def place(cells, beside, pooled, window, at):
    width = cells.shape[0]
    pooled[LEFT : LEFT + width, :] = cells
    pooled[LEFT - 1 : LEFT, :] = beside[:1]
    pooled[LEFT + width : LEFT + width + 1, :] = beside[1:]
    for v in range(3):
        window[v, pl.ds(at, width), :] = pooled[pl.ds(LEFT + 1 - v, width), :].astype(BF16)


def facing(group):
    above = [group[0], 0.75 * (group[0] + group[1]) + 0.25 * group[2]]
    below = [0.25 * group[3] + 0.75 * (group[4] + group[5]), group[5]]
    return above, below


def row_pack_kernel(flags, centre, *outs):
    images, height2, width = centre.shape[0], centre.shape[1], centre.shape[2] - 8
    row_odd = flags[ROW_ODD] == 1
    for i in range(images):
        above, below = facing([centre[i, r, :width, :] for r in (0, 1, 2, height2 - 3, height2 - 2, height2 - 1)])
        for second, out in enumerate(outs):
            for n in range(2):
                odd, even = (below[n], above[n]) if second else (above[n], below[n])
                at = (2 * i + n) * width
                out[at : at + width, :] = jnp.where(row_odd, odd, even).astype(BF16)


def corner_pack_kernel(flags, centre, col_a, col_b, *refs):
    outs, ends = refs[:-1], refs[-1]
    images, height2 = centre.shape[:2]
    row_odd = flags[ROW_ODD] == 1
    for i in range(images):
        lines = (0, 1, 2, height2 - 3, height2 - 2, height2 - 1)
        above, below = facing(
            [jnp.concatenate(column_ends(flags, centre, col_a, col_b, i, r), axis=0) for r in lines]
        )
        for second in range(len(outs)):
            for n in range(2):
                odd, even = (below[n], above[n]) if second else (above[n], below[n])
                at = (2 * i + n) * 4
                ends[second, at : at + 4, :] = jnp.where(row_odd, odd, even)
    for second in range(len(outs)):
        outs[second][...] = ends[second].astype(BF16)


def main_kernel(flags, centre, col_a, col_b, weight, window, acc, cells_out, beside_out, pooled):
    images, height2, width, channels = centre.shape[0], centre.shape[1], centre.shape[2] - 8, centre.shape[3]
    height, depths = height2 // 2, weight.shape[0]
    pooled[...] = jnp.zeros_like(pooled)

    def per_image(i, carry):
        cells, beside = pool_columns(flags, centre, col_a, col_b, i, range(height2))
        for n, r in enumerate((0, 1, 2, height2 - 3, height2 - 2, height2 - 1)):
            cells_out[i, n] = cells[r]
            beside_out[i, n] = beside[r]
        for p in range(1, height - 1):
            at = 2 * p - 1
            both = [
                0.75 * (group[at + 1] + group[at + 2]) + 0.25 * (group[at] + group[at + 3])
                for group in (cells, beside)
            ]
            where = pl.multiple_of((p + 1) * images * width + i * width, width)
            place(both[0], both[1], pooled.at[p], window, where)
        return carry

    lax.fori_loop(0, images, per_image, 0)
    line = images * width
    inner = (height - 2) * line
    rows = slice(2 * line, 2 * line + inner)
    for k in range(depths):
        for u in range(3):
            part = nt_dot(window[0, rows, :], weight[k, u, 0])
            part = part + nt_dot(window[1, rows, :], weight[k, u, 1])
            part = part + nt_dot(window[2, rows, :], weight[k, u, 2])
            if u == 0:
                acc[k, :inner, :] = part
                acc[k, inner:, :] = jnp.zeros((2 * line, channels), F32)
            else:
                acc[k, u * line : u * line + inner, :] += part


def edge_kernel(has_second, flags, *refs):
    sides = 2 if has_second else 1
    rows, corners, (cells, beside, _, acc, weight) = refs[:sides], refs[sides : 2 * sides], refs[2 * sides : 2 * sides + 5]
    *grads, window, pooled, ends, total = refs[2 * sides + 5 :]
    images, width = cells.shape[0], cells.shape[2]
    depths, count = acc.shape[:2]
    line = images * width
    height = count // line
    row_odd, top, bottom = flags[ROW_ODD] == 1, flags[TOP] == 1, flags[BOTTOM] == 1
    for n in range(sides):
        ends[n] = corners[n][...].astype(F32)
    pooled[...] = jnp.zeros_like(pooled)
    cell = lax.broadcasted_iota(jnp.int32, (width, cells.shape[3]), 0)
    for i in range(images):
        for_rows = []
        for is_end, own in ((False, cells), (True, beside)):
            def came(from_above, n):
                def of(ref_at):
                    end, at = (2 * i + n) * 4, (2 * i + n) * width
                    if is_end:
                        return ends[ref_at, end + 2 : end + 4, :]
                    more = jnp.where(cell == 0, ends[ref_at, end : end + 1, :], 0.0)
                    more = jnp.where(cell == width - 1, ends[ref_at, end + 1 : end + 2, :], more)
                    return rows[ref_at][at : at + width, :].astype(F32) + more

                first = of(0)
                second = of(1) if has_second else jnp.zeros_like(first)
                return jnp.where(row_odd, first, second) if from_above else jnp.where(row_odd, second, first)

            edge = [own[i, n] for n in range(6)]
            zero = jnp.zeros_like(edge[0])
            for_rows.append(
                [
                    jnp.where(top, zero, came(True, 0) + 0.25 * edge[0]),
                    0.75 * (edge[0] + edge[1]) + 0.25 * (jnp.where(top, edge[0], came(True, 1)) + edge[2]),
                    0.75 * (edge[4] + edge[5]) + 0.25 * (jnp.where(bottom, edge[5], came(False, 0)) + edge[3]),
                    jnp.where(bottom, zero, came(False, 1) + 0.25 * edge[5]),
                ]
            )
        for n, p in enumerate((0, 1, height, height + 1)):
            place(for_rows[0][n], for_rows[1][n], pooled.at[n], window, p * line + i * width)
    low, high = slice(0, 2 * line), slice(height * line, (height + 2) * line)
    for k in range(depths):
        total[...] = acc[k]
        for v in range(3):
            total[(height - 2) * line :, :] += nt_dot(window[v, high, :], weight[k, 0, v])
            total[: 2 * line, :] += nt_dot(window[v, low, :], weight[k, 2, v])
            middle = jnp.concatenate(
                [window[v, line : 2 * line, :], window[v, height * line : (height + 1) * line, :]], axis=0
            )
            part = nt_dot(middle, weight[k, 1, v])
            total[:line, :] += part[:line]
            total[(height - 1) * line :, :] += part[line:]
        for apart in range(2 * CHIPS):
            at = pl.multiple_of((flags[GRAY] ^ apart) * line, line)
            grads[apart // 2][apart % 2, k] = total[pl.ds(at, line), :].astype(BF16)


def deal(full, split_refs, core, turned):
    if len(split_refs) == 1:
        split_refs[0][...] = full[...]
        return
    kept, *sent = split_refs
    count, rows = kept.shape[:2]
    size = sent[0].shape[0]
    for j in range(count):
        p = (j & ~3 | (j & 1) << 1 | j >> 1 & 1) if turned else j
        kept[p] = full[pl.ds(pl.multiple_of((2 * j + core) * rows, 16), rows), :]
        sent[p // size][p % size] = full[pl.ds(pl.multiple_of((2 * j + 1 - core) * rows, 16), rows), :]


def conv_term_kernel(flags, window, saved, *refs):
    split_refs, top, full, flat = refs[:-3], refs[-3], refs[-2], refs[-1]
    images, depths, height, width, channels = saved.shape
    line = images * width
    count = height * line
    split = top.shape[0]
    for k in range(depths):
        for h in range(height):
            for i in range(images):
                at = (h * images + i) * width
                flat[at : at + width, :] = saved[i, k, h]
        flat_t = flat[...].T
        for n in range(9):
            start = (2 - n // 3) * line
            part = jnp.dot(
                flat_t, window[n % 3, start : start + count, :], preferred_element_type=F32
            ).astype(BF16)
            at = (k * 9 + n) * channels
            if at < split:
                top[at : at + channels, :] = part
            else:
                full[at - split : at - split + channels, :] = part
    deal(full, split_refs, flags[CORE], True)


def pass_on_kernel(*refs):
    for n, piece in enumerate(refs[:-1]):
        refs[-1][n] = piece[1]


def proj_term_kernel(flags, *refs):
    came, (passed, feats, conv_top) = refs[:CHIPS], refs[CHIPS : CHIPS + 3]
    split_refs, tokens, full = refs[CHIPS + 3 : -2], refs[-2], refs[-1]
    images, depths, _, dim = feats.shape
    line = passed.shape[2]
    width = line // images
    for apart in range(2 * CHIPS):
        column = column_of(flags[GRAY] ^ apart)
        for k in range(depths):
            for i in range(images):
                at = pl.multiple_of((i * TILE_COLS + column) * width, width)
                rows = slice(i * width, (i + 1) * width)
                piece = passed[apart // 2, k, rows, :] if apart % 2 else came[apart // 2][0, k, rows, :]
                tokens[k, pl.ds(at, width), :] = piece
    for k in range(depths):
        flat = feats[:, k].reshape(tokens.shape[1], dim)
        part = lax.dot_general(
            flat, tokens[k], (((0,), (0,)), ((), ())), preferred_element_type=F32
        )
        full[k * dim : (k + 1) * dim, :] = part.astype(BF16)
    full[depths * dim :, :] = conv_top[...]
    deal(full, split_refs, flags[CORE], False)


def feat_grad_kernel(tokens, weight, out):
    images, depths, count, dim = out.shape
    for k in range(depths):
        out[:, k] = nt_dot(tokens[k], weight[k]).astype(BF16).reshape(images, count, dim)


def take(part, block, at, columns=None):
    size = part[0].shape[0]
    return part[block // size][block % size + at, :, slice(None) if columns is None else columns].astype(F32)


def round_kernel(jobs, flags, *refs):
    ins, outs, dp = list(refs[: sum(sum(job[0]) for job in jobs)]), refs, flags[DP]
    outs = list(refs[len(ins) :])
    for sizes, at, bits, by_columns, heights in jobs:
        parts = []
        for size in sizes:
            parts.append(ins[:size])
            del ins[:size]
        span = 1 << bits
        mine = 0
        for b in range(bits):
            mine = mine + flags[BITS + at + b] * (1 << b)
        last = span * (2 if by_columns else 1)
        for n in [0] + list(range(last - 1, 0, -1)):
            across, apart = n // span, n % span
            pieces = outs[: len(heights) if n else 1]
            del outs[: len(pieces)]
            count, _, width = pieces[0].shape
            columns = None
            if by_columns:
                columns = pl.ds(pl.multiple_of((dp ^ across) * width, width), width)
            for q in range(count):
                total = take(parts[0], q * span, mine ^ apart, columns)
                for other in parts[1:]:
                    total = total + take(other, q * span, mine ^ apart, columns)
                start = 0
                for piece in pieces:
                    piece[q] = total[start : start + piece.shape[1]].astype(piece.dtype)
                    start += piece.shape[1]


def last_kernel(early_parts, flags, *refs):
    ins, (sent, kept) = list(refs[:-2]), refs[-2:]
    first = flags[DP] == 0
    sums = []
    for sizes in (early_parts, (1,) * (len(ins) - sum(early_parts))):
        total = 0.0
        for size in sizes:
            rows = [piece[0].astype(F32) for piece in ins[:size]]
            total = total + (jnp.concatenate(rows, axis=0) if size > 1 else rows[0])
            del ins[:size]
        sums.append(total)
    sent[...] = jnp.where(first, sums[0], sums[1]).astype(BF16)
    kept[...] = jnp.where(first, sums[1], sums[0])


def join_kernel(scale, flags, kept, came, out):
    width = kept.shape[1]
    at = pl.multiple_of(flags[DP] * width, width)
    out[:, pl.ds(at, width)] = kept[...] * scale
    at = pl.multiple_of((1 - flags[DP]) * width, width)
    out[:, pl.ds(at, width)] = came[...].astype(F32) * scale


def vmem_call(kernel, out_shape, operands, scratch=(), scalars=1, flops=0, limit=16, after=(), aliases=()):
    whole = pl.BlockSpec(memory_space=pltpu.VMEM)
    specs = [pl.BlockSpec(memory_space=pltpu.SMEM)] * scalars + [whole] * (len(operands) - scalars)
    specs += [pl.BlockSpec(memory_space=pl.ANY)] * len(after)
    count = len(operands)

    def run(*refs):
        kernel(*refs[:count], *refs[count + len(after) :])

    moved = sum(a.size * a.dtype.itemsize for a in operands)
    moved += sum(math.prod(s.shape) * s.dtype.itemsize for s in jax.tree.leaves(out_shape))
    return pl.pallas_call(
        run,
        out_shape=out_shape,
        in_specs=specs,
        out_specs=jax.tree.map(lambda _: whole, out_shape),
        scratch_shapes=list(scratch),
        input_output_aliases=dict(aliases),
        compiler_params=pltpu.CompilerParams(vmem_limit_bytes=limit << 20),
        cost_estimate=pl.CostEstimate(flops=flops, bytes_accessed=moved, transcendentals=0),
    )(*operands, *after)


def sds(*shape, dtype=BF16):
    return jax.ShapeDtypeStruct(shape, dtype)


def xor_move(block, apart, across):
    tiles = lax.axis_size("tile")
    if not across:
        return lax.ppermute(block, "tile", [(t, t ^ apart) for t in range(tiles)])
    if not apart:
        return lax.ppermute(block, "dp", [(0, 1), (1, 0)])
    route = [(d * tiles + t, (1 - d) * tiles + (t ^ apart)) for d in range(2) for t in range(tiles)]
    return lax.ppermute(block, ("dp", "tile"), route)


def core_sum(dealt, core, pieces, turned):
    if len(dealt) == 1:
        tiles = lax.axis_size("tile")
        rows, channels = dealt[0].shape[0] // tiles, dealt[0].shape[1]
        pairs = dealt[0].reshape(tiles // 2, 2, rows, channels)
        if turned:
            pairs = pairs.reshape(tiles // 8, 2, 2, 2, rows, channels).swapaxes(1, 2).reshape(pairs.shape)
        kept = lax.dynamic_index_in_dim(pairs, core, 1, keepdims=False)
        sent = lax.dynamic_index_in_dim(pairs, 1 - core, 1, keepdims=False)
        size = sent.shape[0] // pieces
        sent = [sent[n * size : (n + 1) * size] for n in range(pieces)]
    else:
        kept, *sent = dealt
    return [[kept], [xor_move(piece, 1, False) for piece in sent]]


def deal_rounds(jobs, flags, after=()):
    outs, plans, operands = [], [], [flags]
    for parts, at, bits, by_columns, cut in jobs:
        span = 1 << bits
        count, rows, channels = parts[0][0].shape
        channels = channels // 2 if by_columns else channels
        tiles = rows // 16
        heights = [rows]
        if rows % 16 == 0 and cut > 1:
            heights = [16 * (tiles * (n + 1) // cut - tiles * n // cut) for n in range(cut)]
        for n in range(span * (2 if by_columns else 1)):
            if n == 0:
                outs.append(sds(count // span, rows, channels, dtype=F32))
            else:
                outs += [sds(count // span, height, channels) for height in heights]
        plans.append((tuple(len(part) for part in parts), at, bits, by_columns, tuple(heights)))
        operands += [piece for part in parts for piece in part]
    pieces = list(vmem_call(functools.partial(round_kernel, plans), outs, operands, after=after))
    token, sums = pieces[0], []
    for _, at, bits, by_columns, heights in plans:
        span = 1 << bits
        parts = [[pieces.pop(0)]]
        for n in range(span * (2 if by_columns else 1) - 1, 0, -1):
            parts.append([xor_move(pieces.pop(0), (n % span) << at, n >= span) for _ in heights])
        sums.append(parts)
    return sums, token


def per_device(features, proj_weight, conv_weight, saved, cotangent):
    position = lax.axis_index("tile")
    tile_count = lax.axis_size("tile")
    rows = tile_count // TILE_COLS
    gray = position % TILE_COLS
    col, row = column_of(gray), position // TILE_COLS
    images, height2, width2, channels = cotangent.shape
    depths, dim = proj_weight.shape[:2]
    height, width = height2 // 2, width2 // 2
    patches = images * height * width
    line = images * width
    tokens = features.shape[2]
    has_second = rows > 2
    sides = 2 if has_second else 1
    bits = tile_count.bit_length() - 1
    flags = jnp.stack(
        [row % 2, col % 2, row == 0, row == rows - 1, col == 0, col == TILE_COLS - 1]
        + [position % 2, lax.axis_index("dp"), gray]
        + [position >> b & 1 for b in range(bits)]
    ).astype(jnp.int32)

    def swap(block, row_pairs, col_pairs):
        return lax.ppermute(block, "tile", tile_route(row_pairs, col_pairs, rows))

    low, high = cotangent[:, :, :HALO], cotangent[:, :, width2 - HALO :]
    around = paired(TILE_COLS, 1) + [(0, TILE_COLS - 1), (TILE_COLS - 1, 0)]
    col_b = swap(jnp.where(col % 2 == 1, high, low), None, around)
    col_a = swap(jnp.where(col % 2 == 1, low, high), None, paired(TILE_COLS, 0))
    centre = vmem_call(
        centre_kernel,
        sds(images, height2, width + 8, channels, dtype=F32),
        (cotangent,),
        scratch=(pltpu.VMEM((channels // 128, height2, LEFT + width2 + 8, 128), F32),),
        scalars=0,
    )
    row_out = vmem_call(row_pack_kernel, [sds(2 * line, channels)] * sides, (flags, centre))
    came_rows = [swap(row_out[n], paired(rows, n), None) for n in range(sides)]
    corner_out = vmem_call(
        corner_pack_kernel,
        [sds(8 * images, channels)] * sides,
        (flags, centre, col_a, col_b),
        scratch=(pltpu.VMEM((sides, 8 * images, channels), F32),),
    )
    came_rows += [swap(corner_out[n], paired(rows, n), None) for n in range(sides)]
    conv_flops = 2 * patches * depths * 9 * channels * channels
    window, acc, cells, beside = vmem_call(
        main_kernel,
        [
            sds(3, (height + 2) * line, channels),
            sds(depths, patches, channels, dtype=F32),
            sds(images, 6, width, channels, dtype=F32),
            sds(images, 6, 2, channels, dtype=F32),
        ],
        (flags, centre, col_a, col_b, conv_weight),
        scratch=(pltpu.VMEM((height, LEFT + width + 8, channels), F32),),
        flops=conv_flops,
        after=(corner_out[0],),
    )
    *grads, window = vmem_call(
        functools.partial(edge_kernel, has_second),
        [sds(2, depths, line, channels)] * CHIPS + [sds(3, (height + 2) * line, channels)],
        [flags] + came_rows + [cells, beside, window, acc, conv_weight],
        scratch=(
            pltpu.VMEM((4, LEFT + width + 8, channels), F32),
            pltpu.VMEM((sides, 8 * images, channels), F32),
            pltpu.VMEM((patches, channels), F32),
        ),
        flops=conv_flops // 4,
        aliases={2 * sides + 3: CHIPS},
    )
    came = [xor_move(grads[chip], 2 * chip, False) for chip in range(CHIPS - 1, 0, -1)]
    came = [grads[0]] + came[::-1]
    to_pass = vmem_call(pass_on_kernel, sds(CHIPS, depths, line, channels), came, scalars=0)
    passed = xor_move(to_pass, 1, False)

    half_rows = depths * (dim + 9 * channels) // 2
    conv_late = half_rows - depths * dim
    block_rows = half_rows // tile_count
    pieces = 4
    if block_rows % 16:
        dealt = [sds(half_rows, channels)]
    else:
        dealt = [sds(tile_count // 2, block_rows, channels)]
        dealt += [sds(tile_count // 2 // pieces, block_rows, channels)] * pieces
    full = pltpu.VMEM((half_rows, channels), BF16)
    *early, conv_top = vmem_call(
        conv_term_kernel,
        dealt + [sds(conv_late, channels)],
        (flags, window, saved),
        scratch=(full, pltpu.VMEM((patches, channels), BF16)),
        flops=conv_flops,
    )
    (early_parts,), before = deal_rounds([(core_sum(early, position % 2, pieces, True), 1, 0, True, 1)], flags)
    proj_flops = 2 * images * tokens * depths * dim * channels
    *terms, token_grad = vmem_call(
        proj_term_kernel,
        dealt + [sds(depths, images * tokens, channels)],
        [flags] + came + [passed, features, conv_top],
        scratch=(full,),
        flops=proj_flops,
        after=(before,),
    )
    (late_parts,), before = deal_rounds(
        [(core_sum(terms, position % 2, pieces, False), 1, 1, True, 1)], flags, after=(token_grad,)
    )
    at, early_bits = 2, [2, 1] + list(range(3, bits))
    while at < bits:
        step = min(2, bits - at)
        (early_parts,), before = deal_rounds([(early_parts, early_bits.pop(0), 1, False, 1)], flags, after=(before,))
        (late_parts, early_parts), before = deal_rounds(
            [(late_parts, at, step, False, 1), (early_parts, early_bits.pop(0), 1, False, 1)], flags, after=(before,)
        )
        at += step
    while early_bits:
        (early_parts,), before = deal_rounds([(early_parts, early_bits.pop(0), 1, False, 1)], flags, after=(before,))
    feature_grad = vmem_call(
        feat_grad_kernel,
        sds(images, depths, tokens, dim),
        (token_grad, proj_weight),
        scalars=0,
        flops=proj_flops,
        after=(before,),
    )
    sent, kept = vmem_call(
        functools.partial(last_kernel, tuple(len(part) for part in early_parts)),
        [sds(block_rows, channels // 2), sds(block_rows, channels // 2, dtype=F32)],
        [flags] + [piece for part in early_parts + late_parts for piece in part],
    )
    other = xor_move(sent, 0, True)
    scale = 1.0 / math.sqrt(images * lax.axis_size("dp") * tokens * tile_count)
    head_grad = vmem_call(
        functools.partial(join_kernel, scale), sds(block_rows, channels, dtype=F32), (flags, kept, other)
    )
    return feature_grad, head_grad


def solution(mesh):
    in_specs = (
        P("dp", None, "tile", None),
        P(),
        P(),
        P("dp", None, "tile", None, None),
        P("dp", "tile", None, None),
    )
    out_specs = (P("dp", None, "tile", None), P(("dp", "tile"), None))
    return jax.shard_map(
        per_device, mesh=mesh, in_specs=in_specs, out_specs=out_specs, check_vma=False
    )
```

```python
import functools
import math

import jax
import jax.numpy as jnp
from jax import lax
from jax.experimental import pallas as pl
from jax.experimental.pallas import tpu as pltpu
from jax.sharding import PartitionSpec as P

TILE_COLS = 8
HALO = 4
LEFT = 8
BF16 = jnp.bfloat16
F32 = jnp.float32
ROW_ODD, COL_ODD, TOP, BOTTOM, LEFT_END, RIGHT_END, CORE, DP, GRAY, BITS = range(10)
CHIPS = TILE_COLS // 2


def gray_of(column):
    return column ^ column >> 1


def column_of(code):
    return code ^ code >> 1 ^ code >> 2


def paired(count, first):
    pairs = []
    for low in range(first, count - 1, 2):
        pairs += [(low, low + 1), (low + 1, low)]
    return pairs


def tile_route(row_pairs, col_pairs, rows):
    row_moves = row_pairs if row_pairs is not None else [(r, r) for r in range(rows)]
    col_moves = col_pairs if col_pairs is not None else [(c, c) for c in range(TILE_COLS)]
    return [
        (r0 * TILE_COLS + gray_of(c0), r1 * TILE_COLS + gray_of(c1))
        for r0, r1 in row_moves
        for c0, c1 in col_moves
    ]


def nt_dot(left, right):
    return lax.dot_general(left, right, (((1,), (1,)), ((), ())), preferred_element_type=F32)


def centre_kernel(cot, pooled, wide):
    images, height2, width2, channels = cot.shape
    width = width2 // 2
    wide[...] = jnp.zeros_like(wide)

    def per_image(i, carry):
        for r in range(height2):
            value = cot[i, r].astype(F32)
            for h in range(channels // 128):
                wide[h, r, LEFT : LEFT + width2, :] = value[:, h * 128 : (h + 1) * 128]
            pooled[i, r, width : width + 1, :] = value[:1]
            pooled[i, r, width + 1 : width + 2, :] = value[width2 - 1 :]
        for r in range(height2):
            for h in range(channels // 128):
                taps = [wide[h, r, pl.ds(LEFT - 1 + n, width, stride=2), :] for n in range(4)]
                pooled[i, r, :width, h * 128 : (h + 1) * 128] = 0.75 * (taps[1] + taps[2]) + 0.25 * (taps[0] + taps[3])
        return carry

    lax.fori_loop(0, images, per_image, 0)


def column_ends(flags, centre, col_a, col_b, i, r):
    width = centre.shape[2] - 8
    col_odd, left, right = flags[COL_ODD] == 1, flags[LEFT_END] == 1, flags[RIGHT_END] == 1
    own_first, own_last = centre[i, r, width : width + 1, :], centre[i, r, width + 1 : width + 2, :]
    one, two = col_a[i, r].astype(F32), col_b[i, r].astype(F32)
    before, after = jnp.where(col_odd, one, two), jnp.where(col_odd, two, one)
    first = 0.75 * (before[2:3] + before[3:4]) + 0.25 * (before[1:2] + own_first)
    last = 0.75 * (after[0:1] + after[1:2]) + 0.25 * (own_last + after[2:3])
    return (
        0.25 * jnp.where(left, own_first, before[3:4]),
        0.25 * jnp.where(right, own_last, after[0:1]),
        jnp.where(left, 0.0, first),
        jnp.where(right, 0.0, last),
    )


def pool_columns(flags, centre, col_a, col_b, i, lines):
    width, channels = centre.shape[2] - 8, centre.shape[3]
    cell = lax.broadcasted_iota(jnp.int32, (width, channels), 0)
    is_first, is_last = cell == 0, cell == width - 1
    cells, beside = [], []
    for r in lines:
        to_first, to_last, first, last = column_ends(flags, centre, col_a, col_b, i, r)
        cells.append(centre[i, r, :width, :] + (jnp.where(is_first, to_first, 0.0) + jnp.where(is_last, to_last, 0.0)))
        beside.append(jnp.concatenate([first, last], axis=0))
    return cells, beside


def place(cells, beside, pooled, window, at):
    width = cells.shape[0]
    pooled[LEFT : LEFT + width, :] = cells
    pooled[LEFT - 1 : LEFT, :] = beside[:1]
    pooled[LEFT + width : LEFT + width + 1, :] = beside[1:]
    for v in range(3):
        window[v, pl.ds(at, width), :] = pooled[pl.ds(LEFT + 1 - v, width), :].astype(BF16)


def facing(group):
    above = [group[0], 0.75 * (group[0] + group[1]) + 0.25 * group[2]]
    below = [0.25 * group[3] + 0.75 * (group[4] + group[5]), group[5]]
    return above, below


def row_pack_kernel(flags, centre, *outs):
    images, height2, width = centre.shape[0], centre.shape[1], centre.shape[2] - 8
    row_odd = flags[ROW_ODD] == 1
    for i in range(images):
        above, below = facing([centre[i, r, :width, :] for r in (0, 1, 2, height2 - 3, height2 - 2, height2 - 1)])
        for second, out in enumerate(outs):
            for n in range(2):
                odd, even = (below[n], above[n]) if second else (above[n], below[n])
                at = (2 * i + n) * width
                out[at : at + width, :] = jnp.where(row_odd, odd, even).astype(BF16)


def corner_pack_kernel(flags, centre, col_a, col_b, *refs):
    outs, ends = refs[:-1], refs[-1]
    images, height2 = centre.shape[:2]
    row_odd = flags[ROW_ODD] == 1
    for i in range(images):
        lines = (0, 1, 2, height2 - 3, height2 - 2, height2 - 1)
        above, below = facing(
            [jnp.concatenate(column_ends(flags, centre, col_a, col_b, i, r), axis=0) for r in lines]
        )
        for second in range(len(outs)):
            for n in range(2):
                odd, even = (below[n], above[n]) if second else (above[n], below[n])
                at = (2 * i + n) * 4
                ends[second, at : at + 4, :] = jnp.where(row_odd, odd, even)
    for second in range(len(outs)):
        outs[second][...] = ends[second].astype(BF16)


def main_kernel(flags, centre, col_a, col_b, weight, window, acc, cells_out, beside_out, pooled):
    images, height2, width, channels = centre.shape[0], centre.shape[1], centre.shape[2] - 8, centre.shape[3]
    height, depths = height2 // 2, weight.shape[0]
    pooled[...] = jnp.zeros_like(pooled)

    def per_image(i, carry):
        cells, beside = pool_columns(flags, centre, col_a, col_b, i, range(height2))
        for n, r in enumerate((0, 1, 2, height2 - 3, height2 - 2, height2 - 1)):
            cells_out[i, n] = cells[r]
            beside_out[i, n] = beside[r]
        for p in range(1, height - 1):
            at = 2 * p - 1
            both = [
                0.75 * (group[at + 1] + group[at + 2]) + 0.25 * (group[at] + group[at + 3])
                for group in (cells, beside)
            ]
            where = pl.multiple_of((p + 1) * images * width + i * width, width)
            place(both[0], both[1], pooled.at[p], window, where)
        return carry

    lax.fori_loop(0, images, per_image, 0)
    line = images * width
    inner = (height - 2) * line
    rows = slice(2 * line, 2 * line + inner)
    for k in range(depths):
        for u in range(3):
            part = nt_dot(window[0, rows, :], weight[k, u, 0])
            part = part + nt_dot(window[1, rows, :], weight[k, u, 1])
            part = part + nt_dot(window[2, rows, :], weight[k, u, 2])
            if u == 0:
                acc[k, :inner, :] = part
                acc[k, inner:, :] = jnp.zeros((2 * line, channels), F32)
            else:
                acc[k, u * line : u * line + inner, :] += part


def edge_kernel(has_second, flags, *refs):
    sides = 2 if has_second else 1
    rows, corners, (cells, beside, _, acc, weight) = refs[:sides], refs[sides : 2 * sides], refs[2 * sides : 2 * sides + 5]
    *grads, window, pooled, ends, total = refs[2 * sides + 5 :]
    images, width = cells.shape[0], cells.shape[2]
    depths, count = acc.shape[:2]
    line = images * width
    height = count // line
    row_odd, top, bottom = flags[ROW_ODD] == 1, flags[TOP] == 1, flags[BOTTOM] == 1
    for n in range(sides):
        ends[n] = corners[n][...].astype(F32)
    pooled[...] = jnp.zeros_like(pooled)
    cell = lax.broadcasted_iota(jnp.int32, (width, cells.shape[3]), 0)
    for i in range(images):
        for_rows = []
        for is_end, own in ((False, cells), (True, beside)):
            def came(from_above, n):
                def of(ref_at):
                    end, at = (2 * i + n) * 4, (2 * i + n) * width
                    if is_end:
                        return ends[ref_at, end + 2 : end + 4, :]
                    more = jnp.where(cell == 0, ends[ref_at, end : end + 1, :], 0.0)
                    more = jnp.where(cell == width - 1, ends[ref_at, end + 1 : end + 2, :], more)
                    return rows[ref_at][at : at + width, :].astype(F32) + more

                first = of(0)
                second = of(1) if has_second else jnp.zeros_like(first)
                return jnp.where(row_odd, first, second) if from_above else jnp.where(row_odd, second, first)

            edge = [own[i, n] for n in range(6)]
            zero = jnp.zeros_like(edge[0])
            for_rows.append(
                [
                    jnp.where(top, zero, came(True, 0) + 0.25 * edge[0]),
                    0.75 * (edge[0] + edge[1]) + 0.25 * (jnp.where(top, edge[0], came(True, 1)) + edge[2]),
                    0.75 * (edge[4] + edge[5]) + 0.25 * (jnp.where(bottom, edge[5], came(False, 0)) + edge[3]),
                    jnp.where(bottom, zero, came(False, 1) + 0.25 * edge[5]),
                ]
            )
        for n, p in enumerate((0, 1, height, height + 1)):
            place(for_rows[0][n], for_rows[1][n], pooled.at[n], window, p * line + i * width)
    low, high = slice(0, 2 * line), slice(height * line, (height + 2) * line)
    for k in range(depths):
        total[...] = acc[k]
        for v in range(3):
            total[(height - 2) * line :, :] += nt_dot(window[v, high, :], weight[k, 0, v])
            total[: 2 * line, :] += nt_dot(window[v, low, :], weight[k, 2, v])
            middle = jnp.concatenate(
                [window[v, line : 2 * line, :], window[v, height * line : (height + 1) * line, :]], axis=0
            )
            part = nt_dot(middle, weight[k, 1, v])
            total[:line, :] += part[:line]
            total[(height - 1) * line :, :] += part[line:]
        for apart in range(2 * CHIPS):
            at = pl.multiple_of((flags[GRAY] ^ apart) * line, line)
            grads[apart // 2][apart % 2, k] = total[pl.ds(at, line), :].astype(BF16)


def deal(full, split_refs, core, turned):
    if len(split_refs) == 1:
        split_refs[0][...] = full[...]
        return
    kept, *sent = split_refs
    count, rows = kept.shape[:2]
    size = sent[0].shape[0]
    for j in range(count):
        p = (j & ~3 | (j & 1) << 1 | j >> 1 & 1) if turned else j
        kept[p] = full[pl.ds(pl.multiple_of((2 * j + core) * rows, 16), rows), :]
        sent[p // size][p % size] = full[pl.ds(pl.multiple_of((2 * j + 1 - core) * rows, 16), rows), :]


def conv_term_kernel(flags, window, saved, *refs):
    split_refs, top, full, flat = refs[:-3], refs[-3], refs[-2], refs[-1]
    images, depths, height, width, channels = saved.shape
    line = images * width
    count = height * line
    split = top.shape[0]
    for k in range(depths):
        for h in range(height):
            for i in range(images):
                at = (h * images + i) * width
                flat[at : at + width, :] = saved[i, k, h]
        flat_t = flat[...].T
        for n in range(9):
            start = (2 - n // 3) * line
            part = jnp.dot(
                flat_t, window[n % 3, start : start + count, :], preferred_element_type=F32
            ).astype(BF16)
            at = (k * 9 + n) * channels
            if at < split:
                top[at : at + channels, :] = part
            else:
                full[at - split : at - split + channels, :] = part
    deal(full, split_refs, flags[CORE], True)


def pass_on_kernel(*refs):
    for n, piece in enumerate(refs[:-1]):
        refs[-1][n] = piece[1]


def proj_term_kernel(flags, *refs):
    came, (passed, feats, conv_top) = refs[:CHIPS], refs[CHIPS : CHIPS + 3]
    split_refs, tokens, full = refs[CHIPS + 3 : -2], refs[-2], refs[-1]
    images, depths, _, dim = feats.shape
    line = passed.shape[2]
    width = line // images
    for apart in range(2 * CHIPS):
        column = column_of(flags[GRAY] ^ apart)
        for k in range(depths):
            for i in range(images):
                at = pl.multiple_of((i * TILE_COLS + column) * width, width)
                rows = slice(i * width, (i + 1) * width)
                piece = passed[apart // 2, k, rows, :] if apart % 2 else came[apart // 2][0, k, rows, :]
                tokens[k, pl.ds(at, width), :] = piece
    for k in range(depths):
        flat = feats[:, k].reshape(tokens.shape[1], dim)
        part = lax.dot_general(
            flat, tokens[k], (((0,), (0,)), ((), ())), preferred_element_type=F32
        )
        full[k * dim : (k + 1) * dim, :] = part.astype(BF16)
    full[depths * dim :, :] = conv_top[...]
    deal(full, split_refs, flags[CORE], False)


def feat_grad_kernel(tokens, weight, out):
    images, depths, count, dim = out.shape
    for k in range(depths):
        out[:, k] = nt_dot(tokens[k], weight[k]).astype(BF16).reshape(images, count, dim)


def take(part, block, at, columns=None):
    size = part[0].shape[0]
    return part[block // size][block % size + at, :, slice(None) if columns is None else columns].astype(F32)


def round_kernel(jobs, flags, *refs):
    ins, outs, dp = list(refs[: sum(sum(job[0]) for job in jobs)]), refs, flags[DP]
    outs = list(refs[len(ins) :])
    for sizes, at, bits, by_columns, heights in jobs:
        parts = []
        for size in sizes:
            parts.append(ins[:size])
            del ins[:size]
        span = 1 << bits
        mine = 0
        for b in range(bits):
            mine = mine + flags[BITS + at + b] * (1 << b)
        last = span * (2 if by_columns else 1)
        for n in [0] + (list(range(last - 1, 0, -1)) if by_columns else list(range(1, last))):
            across, apart = n // span, n % span
            pieces = outs[: len(heights) if n else 1]
            del outs[: len(pieces)]
            count, _, width = pieces[0].shape
            columns = None
            if by_columns:
                columns = pl.ds(pl.multiple_of((dp ^ across) * width, width), width)
            for q in range(count):
                total = take(parts[0], q * span, mine ^ apart, columns)
                for other in parts[1:]:
                    total = total + take(other, q * span, mine ^ apart, columns)
                start = 0
                for piece in pieces:
                    piece[q] = total[start : start + piece.shape[1]].astype(piece.dtype)
                    start += piece.shape[1]


def last_kernel(early_parts, flags, *refs):
    ins, (sent, kept) = list(refs[:-2]), refs[-2:]
    first = flags[DP] == 0
    sums = []
    for sizes in (early_parts, (1,) * (len(ins) - sum(early_parts))):
        total = 0.0
        for size in sizes:
            rows = [piece[0].astype(F32) for piece in ins[:size]]
            total = total + (jnp.concatenate(rows, axis=0) if size > 1 else rows[0])
            del ins[:size]
        sums.append(total)
    sent[...] = jnp.where(first, sums[0], sums[1]).astype(BF16)
    kept[...] = jnp.where(first, sums[1], sums[0])


def join_kernel(scale, flags, kept, came, out):
    width = kept.shape[1]
    at = pl.multiple_of(flags[DP] * width, width)
    out[:, pl.ds(at, width)] = kept[...] * scale
    at = pl.multiple_of((1 - flags[DP]) * width, width)
    out[:, pl.ds(at, width)] = came[...].astype(F32) * scale


def vmem_call(kernel, out_shape, operands, scratch=(), scalars=1, flops=0, limit=16, after=(), aliases=()):
    whole = pl.BlockSpec(memory_space=pltpu.VMEM)
    specs = [pl.BlockSpec(memory_space=pltpu.SMEM)] * scalars + [whole] * (len(operands) - scalars)
    specs += [pl.BlockSpec(memory_space=pl.ANY)] * len(after)
    count = len(operands)

    def run(*refs):
        kernel(*refs[:count], *refs[count + len(after) :])

    moved = sum(a.size * a.dtype.itemsize for a in operands)
    moved += sum(math.prod(s.shape) * s.dtype.itemsize for s in jax.tree.leaves(out_shape))
    return pl.pallas_call(
        run,
        out_shape=out_shape,
        in_specs=specs,
        out_specs=jax.tree.map(lambda _: whole, out_shape),
        scratch_shapes=list(scratch),
        input_output_aliases=dict(aliases),
        compiler_params=pltpu.CompilerParams(vmem_limit_bytes=limit << 20),
        cost_estimate=pl.CostEstimate(flops=flops, bytes_accessed=moved, transcendentals=0),
    )(*operands, *after)


def sds(*shape, dtype=BF16):
    return jax.ShapeDtypeStruct(shape, dtype)


def xor_move(block, apart, across):
    tiles = lax.axis_size("tile")
    if not across:
        return lax.ppermute(block, "tile", [(t, t ^ apart) for t in range(tiles)])
    if not apart:
        return lax.ppermute(block, "dp", [(0, 1), (1, 0)])
    route = [(d * tiles + t, (1 - d) * tiles + (t ^ apart)) for d in range(2) for t in range(tiles)]
    return lax.ppermute(block, ("dp", "tile"), route)


def core_sum(dealt, core, pieces, turned):
    if len(dealt) == 1:
        tiles = lax.axis_size("tile")
        rows, channels = dealt[0].shape[0] // tiles, dealt[0].shape[1]
        pairs = dealt[0].reshape(tiles // 2, 2, rows, channels)
        if turned:
            pairs = pairs.reshape(tiles // 8, 2, 2, 2, rows, channels).swapaxes(1, 2).reshape(pairs.shape)
        kept = lax.dynamic_index_in_dim(pairs, core, 1, keepdims=False)
        sent = lax.dynamic_index_in_dim(pairs, 1 - core, 1, keepdims=False)
        size = sent.shape[0] // pieces
        sent = [sent[n * size : (n + 1) * size] for n in range(pieces)]
    else:
        kept, *sent = dealt
    return [[kept], [xor_move(piece, 1, False) for piece in sent]]


def deal_rounds(jobs, flags, after=()):
    outs, plans, operands = [], [], [flags]
    for parts, at, bits, by_columns, cut in jobs:
        span = 1 << bits
        count, rows, channels = parts[0][0].shape
        channels = channels // 2 if by_columns else channels
        tiles = rows // 16
        heights = [rows]
        if rows % 16 == 0 and cut > 1:
            heights = [16 * (tiles * (n + 1) // cut - tiles * n // cut) for n in range(cut)]
        for n in range(span * (2 if by_columns else 1)):
            if n == 0:
                outs.append(sds(count // span, rows, channels, dtype=F32))
            else:
                outs += [sds(count // span, height, channels) for height in heights]
        plans.append((tuple(len(part) for part in parts), at, bits, by_columns, tuple(heights)))
        operands += [piece for part in parts for piece in part]
    pieces = list(vmem_call(functools.partial(round_kernel, plans), outs, operands, after=after))
    token, sums = pieces[0], []
    for _, at, bits, by_columns, heights in plans:
        span = 1 << bits
        parts = [[pieces.pop(0)]]
        order = range(2 * span - 1, 0, -1) if by_columns else range(1, span)
        for n in order:
            parts.append([xor_move(pieces.pop(0), (n % span) << at, n >= span) for _ in heights])
        sums.append(parts)
    return sums, token


def per_device(features, proj_weight, conv_weight, saved, cotangent):
    position = lax.axis_index("tile")
    tile_count = lax.axis_size("tile")
    rows = tile_count // TILE_COLS
    gray = position % TILE_COLS
    col, row = column_of(gray), position // TILE_COLS
    images, height2, width2, channels = cotangent.shape
    depths, dim = proj_weight.shape[:2]
    height, width = height2 // 2, width2 // 2
    patches = images * height * width
    line = images * width
    tokens = features.shape[2]
    has_second = rows > 2
    sides = 2 if has_second else 1
    bits = tile_count.bit_length() - 1
    flags = jnp.stack(
        [row % 2, col % 2, row == 0, row == rows - 1, col == 0, col == TILE_COLS - 1]
        + [position % 2, lax.axis_index("dp"), gray]
        + [position >> b & 1 for b in range(bits)]
    ).astype(jnp.int32)

    def swap(block, row_pairs, col_pairs):
        return lax.ppermute(block, "tile", tile_route(row_pairs, col_pairs, rows))

    low, high = cotangent[:, :, :HALO], cotangent[:, :, width2 - HALO :]
    around = paired(TILE_COLS, 1) + [(0, TILE_COLS - 1), (TILE_COLS - 1, 0)]
    col_b = swap(jnp.where(col % 2 == 1, high, low), None, around)
    col_a = swap(jnp.where(col % 2 == 1, low, high), None, paired(TILE_COLS, 0))
    centre = vmem_call(
        centre_kernel,
        sds(images, height2, width + 8, channels, dtype=F32),
        (cotangent,),
        scratch=(pltpu.VMEM((channels // 128, height2, LEFT + width2 + 8, 128), F32),),
        scalars=0,
    )
    row_out = vmem_call(row_pack_kernel, [sds(2 * line, channels)] * sides, (flags, centre))
    came_rows = [swap(row_out[n], paired(rows, n), None) for n in range(sides)]
    corner_out = vmem_call(
        corner_pack_kernel,
        [sds(8 * images, channels)] * sides,
        (flags, centre, col_a, col_b),
        scratch=(pltpu.VMEM((sides, 8 * images, channels), F32),),
    )
    came_rows += [swap(corner_out[n], paired(rows, n), None) for n in range(sides)]
    conv_flops = 2 * patches * depths * 9 * channels * channels
    window, acc, cells, beside = vmem_call(
        main_kernel,
        [
            sds(3, (height + 2) * line, channels),
            sds(depths, patches, channels, dtype=F32),
            sds(images, 6, width, channels, dtype=F32),
            sds(images, 6, 2, channels, dtype=F32),
        ],
        (flags, centre, col_a, col_b, conv_weight),
        scratch=(pltpu.VMEM((height, LEFT + width + 8, channels), F32),),
        flops=conv_flops,
        after=(corner_out[0],),
    )
    *grads, window = vmem_call(
        functools.partial(edge_kernel, has_second),
        [sds(2, depths, line, channels)] * CHIPS + [sds(3, (height + 2) * line, channels)],
        [flags] + came_rows + [cells, beside, window, acc, conv_weight],
        scratch=(
            pltpu.VMEM((4, LEFT + width + 8, channels), F32),
            pltpu.VMEM((sides, 8 * images, channels), F32),
            pltpu.VMEM((patches, channels), F32),
        ),
        flops=conv_flops // 4,
        aliases={2 * sides + 3: CHIPS},
    )
    came = [xor_move(grads[chip], 2 * chip, False) for chip in range(CHIPS - 1, 0, -1)]
    came = [grads[0]] + came[::-1]
    to_pass = vmem_call(pass_on_kernel, sds(CHIPS, depths, line, channels), came, scalars=0)
    passed = xor_move(to_pass, 1, False)

    half_rows = depths * (dim + 9 * channels) // 2
    conv_late = half_rows - depths * dim
    block_rows = half_rows // tile_count
    pieces = 4
    if block_rows % 16:
        dealt = [sds(half_rows, channels)]
    else:
        dealt = [sds(tile_count // 2, block_rows, channels)]
        dealt += [sds(tile_count // 2 // pieces, block_rows, channels)] * pieces
    full = pltpu.VMEM((half_rows, channels), BF16)
    *early, conv_top = vmem_call(
        conv_term_kernel,
        dealt + [sds(conv_late, channels)],
        (flags, window, saved),
        scratch=(full, pltpu.VMEM((patches, channels), BF16)),
        flops=conv_flops,
    )
    (early_parts,), before = deal_rounds([(core_sum(early, position % 2, pieces, True), 1, 0, True, 1)], flags)
    proj_flops = 2 * images * tokens * depths * dim * channels
    *terms, token_grad = vmem_call(
        proj_term_kernel,
        dealt + [sds(depths, images * tokens, channels)],
        [flags] + came + [passed, features, conv_top],
        scratch=(full,),
        flops=proj_flops,
        after=(before,),
    )
    (late_parts,), before = deal_rounds(
        [(core_sum(terms, position % 2, pieces, False), 1, 1, True, 1)], flags, after=(token_grad,)
    )
    at, early_bits = 2, [2, 1] + list(range(3, bits))
    while at < bits:
        step = min(2, bits - at)
        (early_parts,), before = deal_rounds([(early_parts, early_bits.pop(0), 1, False, 1)], flags, after=(before,))
        (late_parts, early_parts), before = deal_rounds(
            [(late_parts, at, step, False, 1), (early_parts, early_bits.pop(0), 1, False, 1)], flags, after=(before,)
        )
        at += step
    while early_bits:
        (early_parts,), before = deal_rounds([(early_parts, early_bits.pop(0), 1, False, 1)], flags, after=(before,))
    feature_grad = vmem_call(
        feat_grad_kernel,
        sds(images, depths, tokens, dim),
        (token_grad, proj_weight),
        scalars=0,
        flops=proj_flops,
        after=(before,),
    )
    sent, kept = vmem_call(
        functools.partial(last_kernel, tuple(len(part) for part in early_parts)),
        [sds(block_rows, channels // 2), sds(block_rows, channels // 2, dtype=F32)],
        [flags] + [piece for part in early_parts + late_parts for piece in part],
    )
    other = xor_move(sent, 0, True)
    scale = 1.0 / math.sqrt(images * lax.axis_size("dp") * tokens * tile_count)
    head_grad = vmem_call(
        functools.partial(join_kernel, scale), sds(block_rows, channels, dtype=F32), (flags, kept, other)
    )
    return feature_grad, head_grad


def solution(mesh):
    in_specs = (
        P("dp", None, "tile", None),
        P(),
        P(),
        P("dp", None, "tile", None, None),
        P("dp", "tile", None, None),
    )
    out_specs = (P("dp", None, "tile", None), P(("dp", "tile"), None))
    return jax.shard_map(
        per_device, mesh=mesh, in_specs=in_specs, out_specs=out_specs, check_vma=False
    )
```
